32 devices in a mesh: segment: 4 (over z), ctx: 8 (over y, x, core).
Axes of the slice: x: 2, y: 2, z: 4, core: 2. Of those that a mesh axis runs over, the one named last changes fastest.
Arguments:
- acts: bfloat16 [4, 1024, 2048], P('segment', 'ctx'), may hold values from -10 to 10
- norm_gains: float32 [4, 3, 2048], P('segment'), may hold values from 0.25 to 1.75
- w_kv: bfloat16 [4, 2048, 1024], P('segment', None, 'ctx'), may hold values from -1 to 36.35534
- dt_in: bfloat16 [4, 2048, 128], P('segment'), may hold values from -0.125 to 0.125
- dt_out: bfloat16 [4, 128, 2048], P('segment'), may hold values from -0.5 to 0.5
- dt_bias: float32 [4, 2048], P('segment'), may hold values from -3 to -1
- decay_rate: float32 [4, 2048], P('segment'), may hold values from 0.002 to 2
- w_bc: bfloat16 [4, 2048, 32], P('segment'), may hold values from -0.03125 to 0.03125
- skip_gain: float32 [4, 2048], P('segment'), may hold values from 0.25 to 1.75
- w_router: bfloat16 [4, 2048, 4], P('segment'), may hold values from -1.109145 to 1.109145
- routes: int32 [4, 1024, 2], P('segment', 'ctx'), may hold values from 0 to 3, all different within a row; in each aligned block of 128 rows (0 to 127, 128 to 255, ..., all dimensions but the last counted through in order) at most 64 rows name the same one
- w_up: bfloat16 [4, 2048, 28672], P('segment', None, 'ctx'), may hold values from -0.125 to 0.125
- w_down: bfloat16 [4, 28672, 2048], P('segment', 'ctx'), may hold values from -0.0625 to 0.0625
Outputs:
- handed: bfloat16 [4, 1024, 2048], P('segment', 'ctx')
The draws below stay inside these ranges and needn't reach their ends.
Inputs may be any that keep to these rules, and one draw needn't show every extreme that they name: `routes`: in each section, the 128 rows of one context shard name every expert exactly 64 times; a token's 2 experts differ.
All inputs are finite; a program needn't handle non-finite values.
Results may differ from the reference program's by a relative error of at most 0.017.
Values may be sent and summed in bfloat16 or wider, within the bound.
No kernel may reach another device: no remote copies, remote signals or barrier semaphores. Data moves between devices by JAX's collectives and lax.ppermute only.
A program may use at most 128 MiB of HBM per device.

```python
import math
import jax
import jax.numpy as jnp
import numpy as np
from jax import lax

D = 2048
HEADS = 16
KVH = 4
HD = 128
NS = 16
RANK = 128
EXPERTS = 4
EFF = 7168
TOP = 2
TOK_DEV = 128
SECTIONS = 4
SEQ = 1024
CAP = 64
N_SEGMENT = 4
N_CTX = 8


def draw_acts(key, part):
    jitter_key = jax.random.fold_in(key, 11)
    jitter = jax.random.normal(jitter_key, (SECTIONS, SEQ, D), jnp.float32)
    values = jnp.clip(jitter, -6.0, 6.0)
    return values.astype(jnp.bfloat16)


def draw_w_kv(key, part):
    weight_key = jax.random.fold_in(key, 17)
    entries = jnp.clip(jax.random.normal(weight_key, (SECTIONS, D, 2 * KVH * HD), jnp.float32), -6.0, 6.0) * D ** (-0.5)
    return entries.astype(jnp.bfloat16)


def draw_w_router(key, part):
    router_key = jax.random.fold_in(key, 23)
    entries = jnp.clip(jax.random.normal(router_key, (SECTIONS, D, EXPERTS), jnp.float32), -6.0, 6.0) * D ** (-0.5)
    return entries.astype(jnp.bfloat16)


def shard_levels(key, dims, cuts, least, high):
    level = 1.0
    for axis_at, shards_of in cuts:
        draws = jax.random.uniform(jax.random.fold_in(jax.random.fold_in(key, 6), axis_at), (shards_of,), jnp.float32, least / len(cuts), high / len(cuts))
        level = level * jnp.repeat(jnp.exp(draws), dims[axis_at] // shards_of).reshape((-1,) + (1,) * (len(dims) - 1 - axis_at))
    return level


def assign_block(key, own, number, rows, count, top, limit, slope):
    order = jax.random.permutation(key, count)
    heavy_load, common = shares(count, rows * top, limit, slope, True), shares(count, rows * top, limit, slope, False)
    places = jnp.arange(count)

    def named(tallies, offset_by):
        used = int((tallies > 0).sum())
        fixed = max(1, used // 4)
        moved = fixed + (places - fixed + offset_by * (used - fixed)) % max(1, count - fixed)
        return jnp.zeros((count,), jnp.int32).at[order[jnp.where(places < fixed, places, moved)]].set(jnp.asarray(tallies, jnp.int32))

    tallies = jnp.where(number % 4 == 0, named(heavy_load, number // 4), named(common, number - number // 4 - 1))
    mixed = jax.random.permutation(jax.random.fold_in(own, 3), count)
    giver, receiver = mixed[0:count // 2 * 2:2], mixed[1:count // 2 * 2:2]
    slack = jnp.minimum(tallies[giver] - 1, limit - tallies[receiver]) // 2
    slack = jnp.where((giver == order[0]) | (receiver == order[0]) | (tallies[receiver] == 0), 0, jnp.maximum(slack, 0))
    moved = jax.random.randint(jax.random.fold_in(own, 4), (count // 2,), 0, 1 << 20) % (slack + 1)
    tallies = tallies.at[giver].add(-moved).at[receiver].add(moved)
    items = jnp.searchsorted(jnp.cumsum(tallies), jnp.arange(rows * top), side="right").astype(jnp.int32)
    grid = items.reshape(top, rows).T
    grid = grid[jax.random.permutation(jax.random.fold_in(own, 1), rows)]
    offset_by = jax.random.randint(jax.random.fold_in(own, 2), (rows, 1), 0, top)
    return jnp.take_along_axis(grid, (jnp.arange(top)[None, :] + offset_by) % top, axis=1)


def shares(number_of, total, most, lean, full):
    weights = [(1 << 20) // math.isqrt(rank ** lean) + 1 for rank in range(1, number_of + 1)]
    largest = most if full else min(most, max(-(-total // number_of), total * weights[0] // sum(weights)))
    least = 1 if total - largest >= number_of - 1 else 0
    counts, spare = [largest] + [least] * (number_of - 1), total - largest - least * (number_of - 1)
    while spare > 0:
        candidates = [i for i in range(1, number_of) if counts[i] < largest] or [i for i in range(1, number_of) if counts[i] < most]
        whole, budget = sum([weights[i] for i in candidates]), spare
        for i in candidates:
            addition = min(most - counts[i], max(1, budget * weights[i] // whole), spare)
            counts[i] = counts[i] + addition
            spare = spare - addition
    return np.array(counts)


def bell_draw(own_key, shape, scale, bound, shards=(), kind=jnp.bfloat16):
    values = jax.random.normal(own_key, shape, jnp.float32) * scale
    if len(shards) > 0:
        values = shard_levels(own_key, shape, shards, -0.22, 0.18) * values
    return jnp.clip(values, min=-bound, max=bound).astype(kind)


def setup_inputs(seed: int = 0) -> dict:
    arg_keys = jax.random.split(jax.random.key(seed), 14)
    acts = draw_acts(jax.random.fold_in(arg_keys[13], 71), 0)
    norm_gains = jnp.clip(1.0 + 0.15 * jax.random.normal(arg_keys[1], (SECTIONS, 3, D), jnp.float32), 0.25, 1.75)
    w_kv = draw_w_kv(jax.random.fold_in(arg_keys[13], 71), 0)
    dt_in = bell_draw(arg_keys[3], (SECTIONS, D, RANK), D ** -0.5, 0.125, ((0, 4),))
    dt_out = bell_draw(arg_keys[4], (SECTIONS, RANK, D), RANK ** -0.5, 0.5, ((0, 4),))
    dt_bias = jnp.clip(-3.0 + 2.0 * jax.random.uniform(arg_keys[5], (SECTIONS, D), jnp.float32) ** shard_levels(arg_keys[5], (SECTIONS, D), ((0, 4),), -0.2, 0.2), -3.0, -1.0)
    decay_rate = jnp.clip(jnp.exp(math.log(2.0) - 6.9077552 * jax.random.uniform(arg_keys[6], (SECTIONS, D), jnp.float32) ** shard_levels(arg_keys[6], (SECTIONS, D), ((0, 4),), -0.2, 0.2)), 0.002, 2.0)
    w_bc = bell_draw(arg_keys[7], (SECTIONS, D, 2 * NS), (16 * D) ** -0.5, 0.03125, ((0, 4),))
    skip_gain = jnp.clip(1.0 + 0.15 * jax.random.normal(arg_keys[8], (SECTIONS, D), jnp.float32), 0.25, 1.75)
    w_router = draw_w_router(jax.random.fold_in(arg_keys[13], 71), 0)
    routes_keys = jax.random.split(jax.random.fold_in(arg_keys[10], 1), SECTIONS * SEQ // TOK_DEV)
    routes_turns = jax.random.permutation(jax.random.fold_in(arg_keys[10], 3), SECTIONS * SEQ // TOK_DEV)
    routes = jax.vmap(lambda own, number: assign_block(jax.random.fold_in(arg_keys[10], 2), own, number, TOK_DEV, EXPERTS, TOP, CAP, 0))(routes_keys, routes_turns).reshape((SECTIONS, SEQ, TOP))
    w_up = bell_draw(arg_keys[11], (SECTIONS, D, EXPERTS * EFF), D ** -0.5, 0.125, ((0, 4), (2, 8)))
    w_down = bell_draw(arg_keys[12], (SECTIONS, EXPERTS * EFF, D), EFF ** -0.5, 0.0625, ((0, 4), (1, 8)))
    return {"acts": acts, "norm_gains": norm_gains, "w_kv": w_kv, "dt_in": dt_in, "dt_out": dt_out, "dt_bias": dt_bias, "decay_rate": decay_rate, "w_bc": w_bc, "skip_gain": skip_gain, "w_router": w_router, "routes": routes, "w_up": w_up, "w_down": w_down}


def rms_norm(values, gain):
    return values * lax.rsqrt(lax.optimization_barrier(jnp.mean(values * values, -1, keepdims=True)) + 1e-06) * gain

def attend(normed, kv_rows):
    seq = normed.shape[0]
    group = HEADS // KVH
    keys = kv_rows[:, :KVH * HD].reshape(seq, KVH, HD).astype(jnp.float32)
    values = kv_rows[:, KVH * HD:].reshape(seq, KVH, HD).astype(jnp.float32)
    width = min(512, seq)
    queries = normed.reshape(seq // width, width, KVH, group, HD)
    starts = jnp.arange(seq // width, dtype=jnp.int32) * width
    key_pos = jnp.arange(seq, dtype=jnp.int32)

    def block(item):
        query_block, start = item
        scores = jnp.einsum('tgrd,sgd->tgrs', query_block.astype(jnp.float32), keys) * HD ** (-0.5)
        query_pos = start + jnp.arange(width, dtype=jnp.int32)
        allowed = (key_pos[None, :] <= query_pos[:, None])[:, None, None, :]
        scores = jnp.where(allowed, scores, -1e+30)
        largest = lax.optimization_barrier(jnp.max(scores, -1, keepdims=True))
        weights = jnp.where(allowed, jnp.exp(scores - largest), 0.0)
        total = lax.optimization_barrier(jnp.sum(weights, -1))
        rounded = lax.optimization_barrier(weights.astype(jnp.bfloat16)).astype(jnp.float32)
        mixed = jnp.einsum('tgrs,sgd->tgrd', rounded, values)
        return (mixed / total[..., None]).reshape(width, KVH * group * HD)
    return lax.map(block, (queries, starts)).reshape(seq, KVH * group * HD)

def reference(acts, norm_gains, w_kv, dt_in, dt_out, dt_bias, decay_rate, w_bc, skip_gain, w_router, routes, w_up, w_down):
    parts = N_CTX // EXPERTS
    part_width = EFF // parts
    per_expert = SEQ * TOP // EXPERTS
    results = []
    for section in range(N_SEGMENT):
        start_x = acts[section].astype(jnp.float32)
        normed = rms_norm(start_x, norm_gains[section, 0]).astype(jnp.bfloat16)
        kv_rows = jnp.dot(normed, w_kv[section], preferred_element_type=jnp.float32).astype(jnp.bfloat16)
        first = start_x + attend(normed, kv_rows)
        mixed_in = rms_norm(first, norm_gains[section, 1]).astype(jnp.bfloat16)
        low_rank = jnp.dot(mixed_in, dt_in[section], preferred_element_type=jnp.float32).astype(jnp.bfloat16)
        step_size = jax.nn.softplus(jnp.dot(low_rank, dt_out[section], preferred_element_type=jnp.float32) + dt_bias[section])
        keep = jnp.exp(-step_size * decay_rate[section])
        both = jnp.dot(mixed_in, w_bc[section], preferred_element_type=jnp.float32)
        b_part = both[:, :NS]
        c_part = both[:, NS:]
        driven = step_size * mixed_in.astype(jnp.float32)

        def advance(state, item):
            keep_row, drive_row, b_row, c_row = item
            state = keep_row[:, None] * state + drive_row[:, None] * b_row[None, :]
            return (state, lax.optimization_barrier(jnp.sum(state * c_row[None, :], -1)))
        state_zero = jnp.zeros((D, NS), jnp.float32)
        _, read_out = lax.scan(advance, state_zero, (keep, driven, b_part, c_part))
        second = first + read_out + skip_gain[section] * mixed_in.astype(jnp.float32)
        expert_in = rms_norm(second, norm_gains[section, 2]).astype(jnp.bfloat16)
        logits = jnp.dot(expert_in, w_router[section], preferred_element_type=jnp.float32)
        chosen = jnp.take_along_axis(logits, routes[section], 1)
        gates = jax.nn.softmax(chosen, -1)
        flat_route = routes[section].reshape(-1)
        flat_gate = gates.reshape(-1)
        moe_sum = jnp.zeros((SEQ, D), jnp.float32)
        for expert in range(EXPERTS):
            picked = jnp.nonzero(flat_route == expert, size=per_expert)[0].astype(jnp.int32)
            token_rows = (picked // TOP).astype(jnp.int32)
            rows = expert_in[token_rows]
            up_cols = w_up[section][:, expert * EFF:(expert + 1) * EFF]
            hidden = jax.nn.silu(jnp.dot(rows, up_cols, preferred_element_type=jnp.float32)).astype(jnp.bfloat16)
            expert_out = jnp.zeros((per_expert, D), jnp.float32)
            for part in range(parts):
                low = expert * EFF + part * part_width
                piece = jnp.dot(hidden[:, part * part_width:(part + 1) * part_width], w_down[section][low:low + part_width], preferred_element_type=jnp.float32)
                expert_out = expert_out + piece.astype(jnp.bfloat16).astype(jnp.float32)
            moe_sum = moe_sum.at[token_rows].add(expert_out * flat_gate[picked][:, None])
        results.append((second + moe_sum).astype(jnp.bfloat16))
    return jnp.roll(jnp.stack(results), 1, 0)
```

```python
import functools

import jax
import jax.numpy as jnp
from jax import lax
from jax.experimental import pallas as pl
from jax.experimental.pallas import tpu as pltpu
from jax.sharding import PartitionSpec as P

HEADS = 16
KVH = 4
HD = 128
GROUP = HEADS // KVH
EXPERTS = 4
EIGHT = 8
STRIP = 16
LANES = 128
PAIR = 2
CHUNKS = 2
F32 = jnp.float32
BF16 = jnp.bfloat16
VMEM = pl.BlockSpec(memory_space=pltpu.VMEM)
SMEM = pl.BlockSpec(memory_space=pltpu.SMEM)


def params(mib):
    return pltpu.CompilerParams(vmem_limit_bytes=mib * 2**20)


def cost(flops, moved, transcendentals=0):
    return pl.CostEstimate(
        flops=int(flops), bytes_accessed=int(moved), transcendentals=int(transcendentals)
    )


def shape(dims, dtype):
    return jax.ShapeDtypeStruct(tuple(dims), dtype)


def in_hbm(array):
    return pltpu.with_memory_space_constraint(array, pltpu.HBM)


def rms_norm(values, gain):
    return values * lax.rsqrt(jnp.mean(values * values, -1, keepdims=True) + 1e-06) * gain


def strips(rows, body):
    def step(index, carry):
        body(pl.ds(pl.multiple_of(index * STRIP, STRIP), STRIP))
        return carry

    lax.fori_loop(0, rows // STRIP, step, 0, unroll=4)


def split(values):
    high = values.astype(BF16)
    return high, (values - high.astype(F32)).astype(BF16)


def dot(a, b, dims=((1,), (0,))):
    return lax.dot_general(a, b, (dims, ((), ())), preferred_element_type=F32)


def dot_split(a, b, dims=((1,), (0,))):
    a_high, a_low = a
    b_high, b_low = b
    return dot(a_high, b_high, dims) + (dot(a_high, b_low, dims) + dot(a_low, b_high, dims))


def iota(dims, axis):
    return lax.broadcasted_iota(jnp.int32, dims, axis)


def norm_kernel(gains, *refs):
    xs, out = refs[:-1], refs[-1]
    rows = xs[0].shape[0]
    for slot, x in enumerate(xs):

        def body(at, slot=slot, x=x):
            out[slot, at, :] = rms_norm(x[at, :].astype(F32), gains[0]).astype(BF16)

        strips(rows, body)


def project_kernel(place, gains, near, w_own, w_other, *refs):
    xs, (q_out, kv_out, far, weights) = refs[:-4], refs[-4:]
    rows, width = xs[0].shape
    head = place[0] % KVH
    key_at = place[1]
    weights[:, pl.ds(pl.multiple_of(key_at * HD, HD), HD)] = w_own[...]
    weights[:, pl.ds(pl.multiple_of((1 - key_at) * HD, HD), HD)] = w_other[...]
    norm_kernel(gains, *xs, far)
    for half, normed in enumerate((near, far)):
        count = normed.shape[0]
        both = dot(normed[...].reshape(count * rows, width), weights[...]).astype(BF16)
        here = pl.ds(half * count * rows, count * rows)
        kv_out[0, here, :] = both[:, :HD]
        kv_out[1, here, :] = both[:, HD:]
        for slot in range(count):
            for part in range(GROUP):
                cols = pl.ds(pl.multiple_of((head * GROUP + part) * HD, HD), HD)
                q_out[half * count + slot, pl.ds(part * rows, rows), :] = normed[slot, :, cols]


def near_kernel(place, q, kv, largest_out, total_out, summed):
    me = place[0]
    rows = q.shape[1] // GROUP
    count = kv.shape[1]
    lane = iota((rows, count), 1)
    key_shard = me ^ (lane // rows)
    later = lane % rows > iota((rows, count), 0)
    for slot in range(KVH):
        shard = me ^ slot
        hidden = (key_shard > shard) | ((key_shard == shard) & later)
        scores = dot(q[slot], kv[0], ((1,), (1,))) * HD ** (-0.5)
        scores = scores.reshape(GROUP, rows, count)
        scores = jnp.where(hidden[None], -1e30, scores).reshape(GROUP * rows, count)
        largest = jnp.max(scores, -1, keepdims=True)
        weights = jnp.exp(scores - largest)
        total = jnp.sum(weights, -1, keepdims=True)
        summed[slot] = dot(weights.astype(BF16), kv[1])
        largest_out[slot] = jnp.broadcast_to(largest, (GROUP * rows, LANES))
        total_out[slot] = jnp.broadcast_to(total, (GROUP * rows, LANES))


def far_kernel(turn, slots, last, place, q, largest, total, summed, past, *outs):
    rows = q.shape[1] // GROUP
    wide = past.shape[1] // LANES
    mine = place[0] // KVH
    seen = (mine ^ turn) < mine

    def keep(at, top, weight, value):
        if last:
            result = (value / weight).astype(BF16)
            for part in range(GROUP):
                cols = slice(part * HD, (part + 1) * HD)
                outs[at][:, cols] = result[part * rows : (part + 1) * rows]
        else:
            outs[0][slots[at]] = top
            outs[1][slots[at]] = weight
            outs[2][slots[at]] = value

    @pl.when(seen)
    def _():
        for at, slot in enumerate(slots):
            scores = dot(q[slot], past[0], ((1,), (1,))) * HD ** (-0.5)
            top = jnp.broadcast_to(jnp.max(scores, -1, keepdims=True), (GROUP * rows, LANES))
            newest = jnp.maximum(largest[slot], top)
            weights = jnp.exp(scores - jnp.concatenate([newest] * wide, 1))
            fade = jnp.exp(largest[slot] - newest)
            weight = jnp.broadcast_to(jnp.sum(weights, -1, keepdims=True), (GROUP * rows, LANES))
            value = summed[slot] * fade + dot(weights.astype(BF16), past[1])
            keep(at, newest, total[slot] * fade + weight, value)

    @pl.when(jnp.logical_not(seen))
    def _():
        for at, slot in enumerate(slots):
            keep(at, largest[slot], total[slot], summed[slot])


def prepare_kernel(
    place, x, gains, skip, dt_in, dt_out, bias, rate, w_bct, *refs
):
    attended = refs[:KVH]
    base, keep_out, drive_out, chunk_state, chunk_keep, bc_out, coef_out, ends = refs[KVH:-4]
    mixed, pre, tail_high, tail_low = refs[-4:]
    rows, width = x.shape
    state = w_bct.shape[0] // 2
    chunks = rows // EIGHT
    head = place[0] % KVH
    span = GROUP * HD
    for slot in range(KVH):
        cols = pl.ds(pl.multiple_of((head ^ slot) * span, span), span)
        base[:, cols] = x[:, cols].astype(F32) + attended[slot][...].astype(F32)

    def normalize(at):
        first = base[at, :]
        mixed_in = rms_norm(first, gains[1]).astype(BF16)
        mixed[at, :] = mixed_in
        base[at, :] = first + skip[...] * mixed_in.astype(F32)

    strips(rows, normalize)
    low_rank = dot(mixed[...], dt_in[...]).astype(BF16)
    pre[...] = dot(low_rank, dt_out[...])
    bc = dot(mixed[...], w_bct[...], ((1,), (1,)))
    bct = dot(w_bct[...], mixed[...], ((1,), (1,)))
    bc_out[...] = bc
    b_rows = bct[:state]
    coupling = dot_split(split(bc[:, state:]), split(b_rows))
    row, lane = iota((rows, rows), 0), iota((rows, rows), 1)
    coef = jnp.zeros((rows, rows), F32)
    for back in range(EIGHT):
        diagonal = jnp.sum(jnp.where(lane == row - back, coupling, 0.0), 1, keepdims=True)
        coef = coef + jnp.where((lane == back) & (row % EIGHT >= back), diagonal, 0.0)
    coef_out[...] = coef

    edge = iota((EIGHT, width), 0)

    def steps(index, carry):
        at = pl.ds(pl.multiple_of(index * STRIP, STRIP), STRIP)
        raw = pre[at, :] + bias[...]
        step_size = jnp.maximum(raw, 0.0) + jnp.log1p(jnp.exp(-jnp.abs(raw)))
        keep = jnp.exp(-step_size * rate[...])
        drive = step_size * mixed[at, :].astype(F32)
        keep_out[at, :] = keep
        drive_out[at, :] = drive
        tails = []
        for part in range(STRIP // EIGHT):
            kept = keep[part * EIGHT : (part + 1) * EIGHT]
            after = jnp.where(edge < EIGHT - 1, pltpu.roll(kept, EIGHT - 1, 0), 1.0)
            for hop in (1, 2, 4):
                after = after * jnp.where(
                    edge < EIGHT - hop, pltpu.roll(after, EIGHT - hop, 0), 1.0
                )
            chunk_keep[pl.ds(index * (STRIP // EIGHT) + part, 1), :] = after[0:1] * kept[0:1]
            tails.append(after * drive[part * EIGHT : (part + 1) * EIGHT])
        high, low = split(jnp.concatenate(tails, 0))
        tail_high[at, :] = high
        tail_low[at, :] = low
        return carry

    lax.fori_loop(0, rows // STRIP, steps, 0, unroll=2)

    spread = jnp.concatenate([b_rows] * chunks, 0)
    own = iota(spread.shape, 0) // state == iota(spread.shape, 1) // EIGHT
    spread = split(jnp.where(own, spread, 0.0))
    chunk_state[...] = dot_split(spread, (tail_high[...], tail_low[...]))
    products = []
    for tile in range(width // LANES):
        cols = pl.ds(tile * LANES, LANES)
        total = jnp.zeros((state, LANES), F32)
        product = jnp.ones((1, LANES), F32)
        for chunk in range(chunks):
            kept = chunk_keep[chunk : chunk + 1, cols]
            total = total * kept + chunk_state[chunk * state : (chunk + 1) * state, cols]
            product = product * kept
        ends[:, cols] = total.astype(BF16)
        products.append(product)
    ends[:, width:] = jnp.concatenate(products, 0).astype(BF16)


def pair_kernel(place, own, other, ends):
    width = own.shape[1] - LANES
    first = lax.rem(place[0], 2) == 0
    mine = own[...].astype(F32)
    its = other[...].astype(F32)
    earlier = jnp.where(first, mine, its)
    later = jnp.where(first, its, mine)
    fade = later[:, width:]
    for tile in range(width // LANES):
        cols = slice(tile * LANES, (tile + 1) * LANES)
        ends[:, cols] = (earlier[:, cols] * fade[tile : tile + 1] + later[:, cols]).astype(BF16)
    ends[:, width:] = (earlier[:, width:] * fade).astype(BF16)


def within_kernel(coef, base, keep, drive, second, faded):
    rows, width = base.shape
    edge = iota((EIGHT, width), 0)

    def chunk(index, carry):
        at = pl.ds(pl.multiple_of(index * EIGHT, EIGHT), EIGHT)
        kept = keep[at, :]
        factors = coef[at, :]
        moved = drive[at, :]
        total = base[at, :] + factors[:, 0:1] * moved
        for back in range(1, EIGHT):
            moved = kept * pltpu.roll(moved, 1, 0)
            total = total + factors[:, back : back + 1] * moved
        second[at, :] = total
        for hop in (1, 2, 4):
            kept = kept * jnp.where(edge >= hop, pltpu.roll(kept, hop, 0), 1.0)
        faded[at, :] = kept
        return carry

    lax.fori_loop(0, rows // EIGHT, chunk, 0, unroll=2)


def route_kernel(
    place, before, faded, chunk_state, chunk_keep, bc, gains, router_t, routes_t, beside, *refs
):
    ends, (second, weighting), packed = refs[:-10], refs[-10:-8], refs[-8:-4]
    state_high, state_low, carried, expert_in = refs[-4:]
    rows, width = before.shape
    chunks = chunk_keep.shape[0]
    state = chunk_state.shape[0] // chunks
    me = place[0]
    own = place[2]
    fades = [end[:, width:].astype(F32) for end in ends]
    last_fade = beside[:, width:].astype(F32)
    second_core = lax.rem(me, 2) == 1
    for tile in range(width // LANES):
        cols = pl.ds(tile * LANES, LANES)
        total = jnp.zeros((state, LANES), F32)
        for end, fade in zip(ends[::-1], fades[::-1]):
            total = total * fade[tile : tile + 1] + end[:, cols].astype(F32)
        joined = total * last_fade[tile : tile + 1] + beside[:, cols].astype(F32)
        total = jnp.where(second_core, joined, total)
        for chunk in range(chunks):
            at = pl.ds(chunk * state, state)
            high, low = split(total)
            state_high[at, cols] = high
            state_low[at, cols] = low
            total = total * chunk_keep[chunk : chunk + 1, cols] + chunk_state[at, cols]
    wide = chunks * state
    repeat = (iota((state, wide), 1) % state == iota((state, wide), 0)).astype(BF16)
    here = iota((rows, wide), 1) // state == iota((rows, wide), 0) // EIGHT
    spread = [
        jnp.where(here, dot(part, repeat), 0.0).astype(BF16) for part in split(bc[:, state:])
    ]
    carried[...] = dot_split(spread, (state_high[...], state_low[...]))

    def normalize(at):
        values = before[at, :] + carried[at, :] * faded[at, :]
        second[at, :] = values
        expert_in[at, :] = rms_norm(values, gains[2]).astype(BF16)

    strips(rows, normalize)

    expert = iota((EXPERTS, rows), 0)
    uses = (routes_t[0:1, :] == expert) | (routes_t[1:2, :] == expert)
    logits = jnp.where(uses, dot(router_t[...], expert_in[...], ((1,), (1,))), -1e30)
    gates = jnp.where(uses, jnp.exp(logits - jnp.max(logits, 0, keepdims=True)), 0.0)
    gates = gates / jnp.sum(gates, 0, keepdims=True)
    sooner = (iota((rows, rows), 0) < iota((rows, rows), 1)).astype(BF16)
    ranks = dot(jnp.where(uses, 1.0, 0.0).astype(BF16), sooner)
    ranks = jnp.where(uses, ranks, -1.0).astype(jnp.int32)
    capacity = packed[0].shape[0]
    place_row = iota((capacity, rows), 0)
    weights = []
    for slot in range(EXPERTS):
        mine = expert == (own ^ slot)
        rank = jnp.sum(jnp.where(mine, ranks, 0), 0, keepdims=True)
        gate = jnp.sum(jnp.where(mine, gates, 0.0), 0, keepdims=True)
        placing = place_row == rank
        weights.append(jnp.where(placing, gate, 0.0))
        packed[slot][...] = dot(placing.astype(BF16), expert_in[...]).astype(BF16)
    weighting[...] = jnp.concatenate(weights, 0).T


def fetch_kernel(pieces, *refs):
    count = len(pieces)
    sources, outs, sems = refs[:count], refs[-count - 1 : -1], refs[-1]
    copies = []
    for source, out, number in zip(sources, outs, pieces):
        rows = source.shape[0] // number
        for piece in range(number):
            at = pl.ds(piece * rows, rows)
            copies.append(
                pltpu.make_async_copy(source.at[at], out.at[at], sems.at[len(copies)])
            )
    for copy in copies:
        copy.start()
    for copy in copies:
        copy.wait()


def fetch(arrays, pieces, after):
    return pl.pallas_call(
        functools.partial(fetch_kernel, pieces),
        out_shape=tuple(shape(array.shape, array.dtype) for array in arrays),
        in_specs=[pl.BlockSpec(memory_space=pl.ANY)] * (len(arrays) + 1),
        out_specs=(VMEM,) * len(arrays),
        scratch_shapes=[pltpu.SemaphoreType.DMA((sum(pieces),))],
        compiler_params=params(4),
        cost_estimate=cost(0, sum(array.size * 4 for array in arrays)),
        name="fetch",
    )(*[in_hbm(array) for array in arrays], after)


def gather_kernel(after, *refs):
    blocks, out = refs[:-1], refs[-1]
    capacity = blocks[0].shape[0]
    for at, block in enumerate(blocks):
        out[at * capacity : (at + 1) * capacity, :] = block[...]


def up_kernel(w_up, tokens, hidden):
    tile = 256 if hidden.shape[1] % 256 == 0 else LANES
    for low in range(0, hidden.shape[1], tile):
        cols = slice(low, low + tile)
        raised = dot(tokens[...], w_up[:, cols])
        hidden[:, cols] = (raised * jax.nn.sigmoid(raised)).astype(BF16)


def down_kernel(start, w_down, *refs):
    hiddens, outs = refs[:-PAIR], refs[-PAIR:]
    hidden = jnp.concatenate([block[...] for block in hiddens], 0)
    rows, width = outs[0].shape
    tile = 256
    for low in range(0, width, tile):
        result = dot(hidden, w_down[:, start + low : start + low + tile]).astype(BF16)
        for at, out in enumerate(outs):
            out[:, low : low + tile] = result[at * rows : (at + 1) * rows]


def join_kernel(*refs):
    parts, outs = refs[:-EXPERTS], refs[-EXPERTS:]
    capacity = outs[0].shape[0]
    for slot, out in enumerate(outs):
        at = slice(slot * capacity, (slot + 1) * capacity)
        total = parts[0][at, :].astype(F32)
        for part in parts[1:]:
            total = total + part[at, :].astype(F32)
        out[...] = total.astype(BF16)


def finish_kernel(start, second, weighting, *refs):
    blocks, out = refs[:-1], refs[-1]
    rows = jnp.concatenate([block[...] for block in blocks], 0)
    high, low = split(weighting[...])
    cols = slice(start, start + out.shape[1])
    out[...] = (second[:, cols] + (dot(high, rows) + dot(low, rows))).astype(BF16)


def exchange(value, axis, mask, later_only=False):
    count = lax.axis_size(axis)
    pairs = [(at, at ^ mask) for at in range(count) if not later_only or at < at ^ mask]
    return lax.ppermute(value, axis, pairs)


def handed_on(value, axis, steps):
    count = lax.axis_size(axis)
    return lax.ppermute(value, axis, [(at, at + steps) for at in range(count - steps)])


def shifted(value, axis, steps):
    count = lax.axis_size(axis)
    return lax.ppermute(value, axis, [(at, (at + steps) % count) for at in range(count)])


def head_weights(w_kv, shard_count, shard_index):
    if w_kv.shape[1] == HD and shard_count == 2 * KVH:
        return w_kv, exchange(w_kv, "ctx", KVH), shard_index // KVH
    whole = lax.all_gather(w_kv, "ctx", axis=1, tiled=True)
    head = shard_index % KVH
    return (
        lax.dynamic_slice_in_dim(whole, head * HD, HD, 1),
        lax.dynamic_slice_in_dim(whole, (KVH + head) * HD, HD, 1),
        jnp.zeros_like(shard_index),
    )


def on_device(
    acts,
    norm_gains,
    w_kv,
    dt_in,
    dt_out,
    dt_bias,
    decay_rate,
    w_bc,
    skip_gain,
    w_router,
    routes,
    w_up,
    w_down,
):
    shard_count = lax.axis_size("ctx")
    me = lax.axis_index("ctx")
    tokens = acts[0]
    rows, width = tokens.shape
    gains = norm_gains.transpose(1, 0, 2)
    parts = shard_count // EXPERTS
    group_rows = KVH * rows
    state = w_bc.shape[2] // 2
    chunks = rows // EIGHT
    capacity = rows * routes.shape[2] // EXPERTS

    near_tokens = exchange(tokens, "ctx", 2)
    w_own, w_other, key_at = head_weights(w_kv[0], shard_count, me)
    beside = exchange(tokens, "ctx", 1)
    far_tokens = exchange(near_tokens, "ctx", 1)
    place = jnp.stack([me, key_at, me // parts]).astype(jnp.int32)
    near_normed = pl.pallas_call(
        norm_kernel,
        out_shape=shape((2, rows, width), BF16),
        in_specs=[VMEM] * 3,
        out_specs=VMEM,
        compiler_params=params(16),
        cost_estimate=cost(16 * rows * width, 8 * rows * width),
        name="norm",
    )(in_hbm(gains), in_hbm(tokens), beside)
    queries, kv = pl.pallas_call(
        project_kernel,
        out_shape=(
            shape((KVH, GROUP * rows, HD), BF16),
            shape((2, group_rows, HD), BF16),
        ),
        in_specs=[SMEM] + [VMEM] * 6,
        out_specs=(VMEM, VMEM),
        scratch_shapes=[
            pltpu.VMEM((2, rows, width), BF16),
            pltpu.VMEM((width, 2 * HD), BF16),
        ],
        compiler_params=params(24),
        cost_estimate=cost(4 * group_rows * width * HD, 8 * group_rows * width),
        name="project",
    )(place, in_hbm(gains), near_normed, in_hbm(w_own), w_other, near_tokens, far_tokens)
    turns = shard_count // KVH
    pasts = [exchange(kv, "ctx", turn * KVH, later_only=True) for turn in range(1, turns)]
    small = [dt_in[0], dt_out[0], w_bc[0].T, tokens, w_router[0].T]
    in_one, in_two, in_bct, in_tokens, in_router = fetch(small, (2, 2, 1, 2, 1), kv)
    scored = GROUP * rows * group_rows * KVH
    tallies = (shape((KVH, GROUP * rows, LANES), F32),) * 2 + (
        shape((KVH, GROUP * rows, HD), F32),
    )
    tally = pl.pallas_call(
        near_kernel,
        out_shape=tallies,
        in_specs=[SMEM, VMEM, VMEM],
        out_specs=(VMEM,) * 3,
        compiler_params=params(16),
        cost_estimate=cost(4 * scored * HD, 4 * group_rows * GROUP * HD * 4, scored),
        name="near",
    )(place, queries, kv)
    attended = [None] * KVH
    for slots in ((2, 3), (0, 1)):
        state_now = tally
        for turn, past in enumerate(pasts, 1):
            last = turn == turns - 1
            state_now = pl.pallas_call(
                functools.partial(far_kernel, turn, slots, last),
                out_shape=(shape((rows, GROUP * HD), BF16),) * len(slots) if last else tallies,
                in_specs=[SMEM] + [VMEM] * 5,
                out_specs=(VMEM,) * (len(slots) if last else 3),
                compiler_params=params(16),
                cost_estimate=cost(2 * scored * HD, 2 * group_rows * GROUP * HD * 4, scored // 2),
                name="far",
            )(place, queries, *state_now, past)
        for slot, block in zip(slots, state_now):
            attended[slot] = exchange(block, "ctx", slot) if slot else block

    base, keep, drive, chunk_state, chunk_keep, bc, coef, ends = pl.pallas_call(
        prepare_kernel,
        out_shape=(
            shape((rows, width), F32),
            shape((rows, width), F32),
            shape((rows, width), F32),
            shape((chunks * state, width), F32),
            shape((chunks, width), F32),
            shape((rows, 2 * state), F32),
            shape((rows, rows), F32),
            shape((state, width + LANES), BF16),
        ),
        in_specs=[SMEM] + [VMEM] * (8 + KVH),
        out_specs=(VMEM,) * 8,
        scratch_shapes=[
            pltpu.VMEM((rows, width), BF16),
            pltpu.VMEM((rows, width), F32),
            pltpu.VMEM((rows, width), BF16),
            pltpu.VMEM((rows, width), BF16),
        ],
        compiler_params=params(32),
        cost_estimate=cost(10 * rows * width * 256, 30 * rows * width, 3 * rows * width),
        name="prepare",
    )(
        place,
        in_tokens,
        in_hbm(gains),
        in_hbm(skip_gain),
        in_one,
        in_two,
        in_hbm(dt_bias),
        in_hbm(decay_rate),
        in_bct,
        *attended,
    )
    beside_ends = exchange(ends, "ctx", 1)
    chip_ends = pl.pallas_call(
        pair_kernel,
        out_shape=shape(ends.shape, BF16),
        in_specs=[SMEM, VMEM, VMEM],
        out_specs=VMEM,
        compiler_params=params(8),
        cost_estimate=cost(4 * ends.size, 8 * ends.size),
        name="pair",
    )(place, ends, beside_ends)
    earlier_ends = [handed_on(chip_ends, "ctx", steps) for steps in range(2, shard_count, 2)]
    before, faded = pl.pallas_call(
        within_kernel,
        out_shape=(shape((rows, width), F32), shape((rows, width), F32)),
        in_specs=[VMEM] * 4,
        out_specs=(VMEM, VMEM),
        compiler_params=params(16),
        cost_estimate=cost(40 * rows * width, 20 * rows * width),
        name="within",
    )(coef, base, keep, drive)
    second, weighting, *packed = pl.pallas_call(
        route_kernel,
        out_shape=(shape((rows, width), F32), shape((rows, EXPERTS * capacity), F32))
        + (shape((capacity, width), BF16),) * EXPERTS,
        in_specs=[SMEM] + [VMEM] * (9 + len(earlier_ends)),
        out_specs=(VMEM,) * (2 + EXPERTS),
        scratch_shapes=[
            pltpu.VMEM((chunks * state, width), BF16),
            pltpu.VMEM((chunks * state, width), BF16),
            pltpu.VMEM((rows, width), F32),
            pltpu.VMEM((rows, width), BF16),
        ],
        compiler_params=params(24),
        cost_estimate=cost(10 * rows * width * 256, 30 * rows * width),
        name="route",
    )(
        place,
        before,
        faded,
        chunk_state,
        chunk_keep,
        bc,
        in_hbm(gains),
        in_router,
        in_hbm(routes[0].T),
        beside_ends,
        *earlier_ends,
    )

    arrived = [packed[0]] + [
        exchange(packed[slot], "ctx", slot * parts) for slot in range(1, EXPERTS)
    ]
    raising, lowering = fetch([w_up[0], w_down[0]], (16, 16), packed[0])
    units = raising.shape[1]
    expert_rows = EXPERTS * capacity
    arrived = pl.pallas_call(
        gather_kernel,
        out_shape=shape((expert_rows, width), BF16),
        in_specs=[pl.BlockSpec(memory_space=pl.ANY)] + [VMEM] * EXPERTS,
        out_specs=VMEM,
        compiler_params=params(8),
        cost_estimate=cost(0, 4 * expert_rows * width),
        name="gather",
    )(raising, *arrived)
    hiddens = []
    for turn in range(parts):
        hiddens.append(
            pl.pallas_call(
                up_kernel,
                out_shape=shape((expert_rows, units), BF16),
                in_specs=[VMEM, VMEM],
                out_specs=VMEM,
                compiler_params=params(14),
                cost_estimate=cost(2 * expert_rows * width * units, 2 * width * units),
                name="up",
            )(raising, exchange(arrived, "ctx", turn) if turn else arrived)
        )
    chunk_width = width // CHUNKS
    results = []
    for chunk in range(CHUNKS):
        start = chunk * chunk_width
        part_out = []
        for turn in range(0, parts, PAIR):
            part_out += pl.pallas_call(
                functools.partial(down_kernel, start),
                out_shape=(shape((expert_rows, chunk_width), BF16),) * PAIR,
                in_specs=[VMEM] * (1 + PAIR),
                out_specs=(VMEM,) * PAIR,
                compiler_params=params(14),
                cost_estimate=cost(
                    2 * PAIR * expert_rows * chunk_width * units, 2 * chunk_width * units
                ),
                name="down",
            )(lowering, *hiddens[turn : turn + PAIR])
        sums = [part_out[0]] + [
            exchange(part_out[turn], "ctx", turn) for turn in range(1, parts)
        ]
        joined = pl.pallas_call(
            join_kernel,
            out_shape=(shape((capacity, chunk_width), BF16),) * EXPERTS,
            in_specs=[VMEM] * parts,
            out_specs=(VMEM,) * EXPERTS,
            compiler_params=params(8),
            cost_estimate=cost(
                4 * EXPERTS * capacity * chunk_width, 8 * EXPERTS * capacity * chunk_width
            ),
            name="join",
        )(*sums)
        returned = [joined[0]] + [
            exchange(joined[slot], "ctx", slot * parts) for slot in range(1, EXPERTS)
        ]
        finished = pl.pallas_call(
            functools.partial(finish_kernel, start),
            out_shape=shape((rows, chunk_width), BF16),
            in_specs=[VMEM] * (2 + EXPERTS),
            out_specs=VMEM,
            compiler_params=params(8),
            cost_estimate=cost(
                4 * rows * EXPERTS * capacity * chunk_width, 10 * rows * chunk_width
            ),
            name="finish",
        )(second, weighting, *returned)
        results.append(shifted(finished, "segment", 1))
    return jnp.concatenate(results, 1)[None]


def solution(mesh):
    in_specs = (
        P("segment", "ctx", None),
        P("segment", None, None),
        P("segment", None, "ctx"),
        P("segment", None, None),
        P("segment", None, None),
        P("segment", None),
        P("segment", None),
        P("segment", None, None),
        P("segment", None),
        P("segment", None, None),
        P("segment", "ctx", None),
        P("segment", None, "ctx"),
        P("segment", "ctx", None),
    )
    out_specs = P("segment", "ctx", None)
    return jax.shard_map(
        on_device, mesh=mesh, in_specs=in_specs, out_specs=out_specs, check_vma=False
    )
```

```python
import functools

import jax
import jax.numpy as jnp
from jax import lax
from jax.experimental import pallas as pl
from jax.experimental.pallas import tpu as pltpu
from jax.sharding import PartitionSpec as P

HEADS = 16
KVH = 4
HD = 128
GROUP = HEADS // KVH
EXPERTS = 4
EIGHT = 8
STRIP = 16
LANES = 128
PAIR = 2
BATCHES = ((0, 3), (1, 2))
CHUNKS = 2
F32 = jnp.float32
BF16 = jnp.bfloat16
VMEM = pl.BlockSpec(memory_space=pltpu.VMEM)
ANY = pl.BlockSpec(memory_space=pl.ANY)
SMEM = pl.BlockSpec(memory_space=pltpu.SMEM)


def params(mib):
    return pltpu.CompilerParams(vmem_limit_bytes=mib * 2**20)


def cost(flops, moved, transcendentals=0):
    return pl.CostEstimate(
        flops=int(flops), bytes_accessed=int(moved), transcendentals=int(transcendentals)
    )


def shape(dims, dtype):
    return jax.ShapeDtypeStruct(tuple(dims), dtype)


def in_hbm(array):
    return pltpu.with_memory_space_constraint(array, pltpu.HBM)


def rms_norm(values, gain):
    return values * lax.rsqrt(jnp.mean(values * values, -1, keepdims=True) + 1e-06) * gain


def strips(rows, body):
    def step(index, carry):
        body(pl.ds(pl.multiple_of(index * STRIP, STRIP), STRIP))
        return carry

    lax.fori_loop(0, rows // STRIP, step, 0, unroll=4)


def split(values):
    high = values.astype(BF16)
    return high, (values - high.astype(F32)).astype(BF16)


def dot(a, b, dims=((1,), (0,))):
    return lax.dot_general(a, b, (dims, ((), ())), preferred_element_type=F32)


def dot_split(a, b, dims=((1,), (0,))):
    a_high, a_low = a
    b_high, b_low = b
    count = a_high.shape[0]
    both = dot(jnp.concatenate([a_high, a_low], 0), b_high, dims)
    return both[:count] + (both[count:] + dot(a_high, b_low, dims))


def iota(dims, axis):
    return lax.broadcasted_iota(jnp.int32, dims, axis)


def norm_into(out, x, gain):
    def body(at):
        out[at, :] = rms_norm(x[at, :].astype(F32), gain).astype(BF16)

    strips(x.shape[0], body)


def norm_kernel(place, gains, x, after, out):
    norm_into(out, x, gains[0])


def queries_into(q_out, slots, normed, head):
    rows = normed.shape[0] // len(slots)
    for at, slot in enumerate(slots):
        for part in range(GROUP):
            cols = pl.ds(pl.multiple_of((head * GROUP + part) * HD, HD), HD)
            q_out[slot, pl.ds(part * rows, rows), :] = normed[at * rows : (at + 1) * rows, cols]


def project_kernel(
    place, gains, normed_own, beside, normed_near, w_own, w_other, q_out, kv_out, weights, normed
):
    rows = beside.shape[0]
    head = place[0] % KVH
    key_at = place[1]
    weights[:, pl.ds(pl.multiple_of(key_at * HD, HD), HD)] = w_own[...]
    weights[:, pl.ds(pl.multiple_of((1 - key_at) * HD, HD), HD)] = w_other[...]
    normed[:rows, :] = normed_own[...]
    norm_into(normed.at[pl.ds(rows, rows)], beside, gains[0])
    normed[2 * rows :, :] = normed_near[...]
    both = dot(normed[...], weights[...]).astype(BF16)
    kv_out[0, : 3 * rows, :] = both[:, :HD]
    kv_out[1, : 3 * rows, :] = both[:, HD:]
    queries_into(q_out, (0, 1, 2), normed, head)


def project_last_kernel(place, normed, weights, q_in, kv_in, q_out, kv_out):
    rows = normed.shape[0]
    q_out[:3] = q_in[:3]
    kv_out[:, : 3 * rows, :] = kv_in[:, : 3 * rows, :]
    both = dot(normed[...], weights[...]).astype(BF16)
    kv_out[0, 3 * rows :, :] = both[:, :HD]
    kv_out[1, 3 * rows :, :] = both[:, HD:]
    queries_into(q_out, (3,), normed, place[0] % KVH)


def near_kernel(place, q, kv, largest_out, total_out, summed):
    me = place[0]
    rows = q.shape[1] // GROUP
    count = kv.shape[1]
    lane = iota((rows, count), 1)
    key_shard = me ^ (lane // rows)
    later = lane % rows > iota((rows, count), 0)
    for slot in range(KVH):
        shard = me ^ slot
        hidden = (key_shard > shard) | ((key_shard == shard) & later)
        scores = dot(q[slot], kv[0], ((1,), (1,))) * HD ** (-0.5)
        scores = scores.reshape(GROUP, rows, count)
        scores = jnp.where(hidden[None], -1e30, scores).reshape(GROUP * rows, count)
        largest = jnp.max(scores, -1, keepdims=True)
        weights = jnp.exp(scores - largest)
        total = jnp.sum(weights, -1, keepdims=True)
        summed[slot] = dot(weights.astype(BF16), kv[1])
        largest_out[slot] = jnp.broadcast_to(largest, (GROUP * rows, LANES))
        total_out[slot] = jnp.broadcast_to(total, (GROUP * rows, LANES))


def far_kernel(turn, slots, last, place, q, largest, total, summed, past, *outs):
    rows = q.shape[1] // GROUP
    wide = past.shape[1] // LANES
    mine = place[0] // KVH
    seen = (mine ^ turn) < mine

    def keep(at, top, weight, value):
        if last:
            result = (value / weight).astype(BF16)
            for part in range(GROUP):
                cols = slice(part * HD, (part + 1) * HD)
                outs[at][:, cols] = result[part * rows : (part + 1) * rows]
        else:
            outs[0][slots[at]] = top
            outs[1][slots[at]] = weight
            outs[2][slots[at]] = value

    @pl.when(seen)
    def _():
        for at, slot in enumerate(slots):
            scores = dot(q[slot], past[0], ((1,), (1,))) * HD ** (-0.5)
            top = jnp.broadcast_to(jnp.max(scores, -1, keepdims=True), (GROUP * rows, LANES))
            newest = jnp.maximum(largest[slot], top)
            weights = jnp.exp(scores - jnp.concatenate([newest] * wide, 1))
            fade = jnp.exp(largest[slot] - newest)
            weight = jnp.broadcast_to(jnp.sum(weights, -1, keepdims=True), (GROUP * rows, LANES))
            value = summed[slot] * fade + dot(weights.astype(BF16), past[1])
            keep(at, newest, total[slot] * fade + weight, value)

    @pl.when(jnp.logical_not(seen))
    def _():
        for at, slot in enumerate(slots):
            keep(at, largest[slot], total[slot], summed[slot])


def prepare_kernel(
    place, x, gains, skip, dt_in, dt_out, bias, rate, w_bct, *refs
):
    attended = refs[:KVH]
    base, keep_out, drive_out, chunk_state, chunk_keep, bc_out, coef_out, ends = refs[KVH:-4]
    mixed, pre, tail_high, tail_low = refs[-4:]
    rows, width = x.shape
    state = w_bct.shape[0] // 2
    chunks = rows // EIGHT
    head = place[0] % KVH
    span = GROUP * HD
    for slot in range(KVH):
        cols = pl.ds(pl.multiple_of((head ^ slot) * span, span), span)
        base[:, cols] = x[:, cols].astype(F32) + attended[slot][...].astype(F32)

    def normalize(at):
        first = base[at, :]
        mixed_in = rms_norm(first, gains[1]).astype(BF16)
        mixed[at, :] = mixed_in
        base[at, :] = first + skip[...] * mixed_in.astype(F32)

    strips(rows, normalize)
    low_rank = dot(mixed[...], dt_in[...]).astype(BF16)
    pre[...] = dot(low_rank, dt_out[...])
    bct = dot(w_bct[...], mixed[...], ((1,), (1,)))
    bc = bct.T
    bc_out[...] = bc
    b_rows = bct[:state]
    coupling = dot_split(split(bc[:, state:]), split(b_rows))
    row, lane = iota((rows, rows), 0), iota((rows, rows), 1)
    coef = jnp.zeros((rows, rows), F32)
    for back in range(EIGHT):
        diagonal = jnp.sum(jnp.where(lane == row - back, coupling, 0.0), 1, keepdims=True)
        coef = coef + jnp.where((lane == back) & (row % EIGHT >= back), diagonal, 0.0)
    coef_out[...] = coef

    edge = iota((EIGHT, width), 0)

    def steps(index, carry):
        at = pl.ds(pl.multiple_of(index * STRIP, STRIP), STRIP)
        raw = pre[at, :] + bias[...]
        step_size = jnp.maximum(raw, 0.0) + jnp.log1p(jnp.exp(-jnp.abs(raw)))
        keep = jnp.exp(-step_size * rate[...])
        drive = step_size * mixed[at, :].astype(F32)
        keep_out[at, :] = keep
        drive_out[at, :] = drive
        tails = []
        for part in range(STRIP // EIGHT):
            kept = keep[part * EIGHT : (part + 1) * EIGHT]
            after = jnp.where(edge < EIGHT - 1, pltpu.roll(kept, EIGHT - 1, 0), 1.0)
            for hop in (1, 2, 4):
                after = after * jnp.where(
                    edge < EIGHT - hop, pltpu.roll(after, EIGHT - hop, 0), 1.0
                )
            chunk_keep[pl.ds(index * (STRIP // EIGHT) + part, 1), :] = after[0:1] * kept[0:1]
            tails.append(after * drive[part * EIGHT : (part + 1) * EIGHT])
        high, low = split(jnp.concatenate(tails, 0))
        tail_high[at, :] = high
        tail_low[at, :] = low
        return carry

    lax.fori_loop(0, rows // STRIP, steps, 0, unroll=2)

    spread = jnp.concatenate([b_rows] * chunks, 0)
    own = iota(spread.shape, 0) // state == iota(spread.shape, 1) // EIGHT
    spread = split(jnp.where(own, spread, 0.0))
    chunk_state[...] = dot_split(spread, (tail_high[...], tail_low[...]))
    products = []
    for tile in range(width // LANES):
        cols = pl.ds(tile * LANES, LANES)
        total = jnp.zeros((state, LANES), F32)
        product = jnp.ones((1, LANES), F32)
        for chunk in range(chunks):
            kept = chunk_keep[chunk : chunk + 1, cols]
            total = total * kept + chunk_state[chunk * state : (chunk + 1) * state, cols]
            product = product * kept
        ends[:, cols] = total.astype(BF16)
        products.append(product)
    ends[:, width:] = jnp.concatenate(products, 0).astype(BF16)


def pair_kernel(place, own, other, ends):
    width = own.shape[1] - LANES
    first = lax.rem(place[0], 2) == 0
    mine = own[...].astype(F32)
    its = other[...].astype(F32)
    earlier = jnp.where(first, mine, its)
    later = jnp.where(first, its, mine)
    fade = later[:, width:]
    for tile in range(width // LANES):
        cols = slice(tile * LANES, (tile + 1) * LANES)
        ends[:, cols] = (earlier[:, cols] * fade[tile : tile + 1] + later[:, cols]).astype(BF16)
    ends[:, width:] = (earlier[:, width:] * fade).astype(BF16)


def within_kernel(coef, base, keep, drive, second, faded):
    rows, width = base.shape
    edge = iota((EIGHT, width), 0)

    def chunk(index, carry):
        at = pl.ds(pl.multiple_of(index * EIGHT, EIGHT), EIGHT)
        kept = keep[at, :]
        factors = coef[at, :]
        moved = drive[at, :]
        total = base[at, :] + factors[:, 0:1] * moved
        for back in range(1, EIGHT):
            moved = kept * pltpu.roll(moved, 1, 0)
            total = total + factors[:, back : back + 1] * moved
        second[at, :] = total
        for hop in (1, 2, 4):
            kept = kept * jnp.where(edge >= hop, pltpu.roll(kept, hop, 0), 1.0)
        faded[at, :] = kept
        return carry

    lax.fori_loop(0, rows // EIGHT, chunk, 0, unroll=2)


def route_kernel(
    place, before, faded, chunk_state, chunk_keep, bc, gains, router_t, routes_t, beside, *refs
):
    ends, (second, weighting), packed = refs[:-11], refs[-11:-9], refs[-9:-5]
    state_high, state_low, carried, expert_in, stack = refs[-5:]
    rows, width = before.shape
    chunks = chunk_keep.shape[0]
    state = chunk_state.shape[0] // chunks
    me = place[0]
    own = place[2]
    chip = me // 2
    stack[0] = jnp.zeros_like(beside)
    for slot, end in enumerate(ends, 1):
        stack[slot] = end[...]
    fades = [stack[chip ^ at, :, width:].astype(F32) for at in range(len(ends))]
    last_fade = beside[:, width:].astype(F32)
    second_core = lax.rem(me, 2) == 1
    for tile in range(width // LANES):
        cols = pl.ds(tile * LANES, LANES)
        total = jnp.zeros((state, LANES), F32)
        for at, fade in enumerate(fades):
            joined = total * fade[tile : tile + 1] + stack[chip ^ at, :, cols].astype(F32)
            total = jnp.where(at < chip, joined, total)
        joined = total * last_fade[tile : tile + 1] + beside[:, cols].astype(F32)
        total = jnp.where(second_core, joined, total)
        for chunk in range(chunks):
            at = pl.ds(chunk * state, state)
            high, low = split(total)
            state_high[at, cols] = high
            state_low[at, cols] = low
            total = total * chunk_keep[chunk : chunk + 1, cols] + chunk_state[at, cols]
    wide = chunks * state
    repeat = (iota((state, wide), 1) % state == iota((state, wide), 0)).astype(BF16)
    here = iota((rows, wide), 1) // state == iota((rows, wide), 0) // EIGHT
    spread = [
        jnp.where(here, dot(part, repeat), 0.0).astype(BF16) for part in split(bc[:, state:])
    ]
    carried[...] = dot_split(spread, (state_high[...], state_low[...]))

    def normalize(at):
        values = before[at, :] + carried[at, :] * faded[at, :]
        second[at, :] = values
        expert_in[at, :] = rms_norm(values, gains[2]).astype(BF16)

    strips(rows, normalize)

    expert = iota((EXPERTS, rows), 0)
    uses = (routes_t[0:1, :] == expert) | (routes_t[1:2, :] == expert)
    logits = jnp.where(uses, dot(router_t[...], expert_in[...], ((1,), (1,))), -1e30)
    gates = jnp.where(uses, jnp.exp(logits - jnp.max(logits, 0, keepdims=True)), 0.0)
    gates = gates / jnp.sum(gates, 0, keepdims=True)
    sooner = (iota((rows, rows), 0) < iota((rows, rows), 1)).astype(BF16)
    ranks = dot(jnp.where(uses, 1.0, 0.0).astype(BF16), sooner)
    ranks = jnp.where(uses, ranks, -1.0).astype(jnp.int32)
    capacity = packed[0].shape[0]
    place_row = iota((capacity, rows), 0)
    weights, placings = [], []
    for slot in range(EXPERTS):
        mine = expert == (own ^ slot)
        rank = jnp.sum(jnp.where(mine, ranks, 0), 0, keepdims=True)
        gate = jnp.sum(jnp.where(mine, gates, 0.0), 0, keepdims=True)
        placing = place_row == rank
        weights.append(jnp.where(placing, gate, 0.0))
        placings.append(placing.astype(BF16))
    chosen = dot(jnp.concatenate(placings, 0), expert_in[...]).astype(BF16)
    for slot in range(EXPERTS):
        packed[slot][...] = chosen[slot * capacity : (slot + 1) * capacity]
    weighting[...] = jnp.concatenate(weights, 0).T


def fetch_kernel(pieces, *refs):
    count = len(pieces)
    sources, outs, sems = refs[:count], refs[-count - 1 : -1], refs[-1]
    copies = []
    for source, out, number in zip(sources, outs, pieces):
        rows = source.shape[0] // number
        for piece in range(number):
            at = pl.ds(piece * rows, rows)
            copies.append(
                pltpu.make_async_copy(source.at[at], out.at[at], sems.at[len(copies)])
            )
    for copy in copies:
        copy.start()
    for copy in copies:
        copy.wait()


def fetch(arrays, pieces, after):
    return pl.pallas_call(
        functools.partial(fetch_kernel, pieces),
        out_shape=tuple(shape(array.shape, array.dtype) for array in arrays),
        in_specs=[ANY] * (len(arrays) + 1),
        out_specs=(VMEM,) * len(arrays),
        scratch_shapes=[pltpu.SemaphoreType.DMA((sum(pieces),))],
        compiler_params=params(4),
        cost_estimate=cost(0, sum(array.size * 4 for array in arrays)),
        name="fetch",
    )(*[in_hbm(array) for array in arrays], after)


def gather_kernel(after, *refs):
    blocks, out = refs[:-1], refs[-1]
    capacity = blocks[0].shape[0]
    for at, block in enumerate(blocks):
        out[at * capacity : (at + 1) * capacity, :] = block[...]


def up_kernel(w_up, own, other, hidden):
    tokens = jnp.concatenate([own[...], other[...]], 0)
    tile = 256 if hidden.shape[1] % 256 == 0 else LANES
    for low in range(0, hidden.shape[1], tile):
        cols = slice(low, low + tile)
        raised = dot(tokens, w_up[:, cols])
        hidden[:, cols] = (raised * jax.nn.sigmoid(raised)).astype(BF16)


def down_kernel(start, done, w_down, *refs):
    outs = refs[-PAIR:]
    earlier, hiddens = refs[: PAIR * done], refs[PAIR * done : -PAIR]
    hidden = jnp.concatenate([block[...] for block in hiddens], 0)
    rows = hiddens[0].shape[0] // PAIR
    tile = 256
    for at, block in enumerate(earlier):
        outs[at % PAIR][at // PAIR * rows : (at // PAIR + 1) * rows, :] = block[...]
    for low in range(0, outs[0].shape[1], tile):
        result = dot(hidden, w_down[:, start + low : start + low + tile]).astype(BF16)
        for at in range(PAIR * len(hiddens)):
            batch = done + at // PAIR
            outs[at % PAIR][batch * rows : (batch + 1) * rows, low : low + tile] = result[
                at * rows : (at + 1) * rows
            ]


def join_kernel(*refs):
    parts, outs = refs[:-EXPERTS], refs[-EXPERTS:]
    capacity = outs[0].shape[0]
    for place, slot in enumerate(sum(BATCHES, ())):
        at = slice(place * capacity, (place + 1) * capacity)
        total = parts[0][at, :].astype(F32)
        for part in parts[1:]:
            total = total + part[at, :].astype(F32)
        outs[slot][...] = total.astype(BF16)


def finish_kernel(start, second, weighting, *refs):
    blocks, out = refs[:-1], refs[-1]
    rows = jnp.concatenate([block[...] for block in blocks], 0)
    high, low = split(weighting[...])
    cols = slice(start, start + out.shape[1])
    out[...] = (second[:, cols] + (dot(high, rows) + dot(low, rows))).astype(BF16)


def exchange(value, axis, mask):
    count = lax.axis_size(axis)
    return lax.ppermute(value, axis, [(at, at ^ mask) for at in range(count)])


def shifted(value, axis, steps):
    count = lax.axis_size(axis)
    return lax.ppermute(value, axis, [(at, (at + steps) % count) for at in range(count)])


def head_weights(w_kv, shard_count, shard_index):
    if w_kv.shape[1] == HD and shard_count == 2 * KVH:
        return w_kv, exchange(w_kv, "ctx", KVH), shard_index // KVH
    whole = lax.all_gather(w_kv, "ctx", axis=1, tiled=True)
    head = shard_index % KVH
    return (
        lax.dynamic_slice_in_dim(whole, head * HD, HD, 1),
        lax.dynamic_slice_in_dim(whole, (KVH + head) * HD, HD, 1),
        jnp.zeros_like(shard_index),
    )


def on_device(
    acts,
    norm_gains,
    w_kv,
    dt_in,
    dt_out,
    dt_bias,
    decay_rate,
    w_bc,
    skip_gain,
    w_router,
    routes,
    w_up,
    w_down,
):
    shard_count = lax.axis_size("ctx")
    me = lax.axis_index("ctx")
    tokens = acts[0]
    rows, width = tokens.shape
    gains = norm_gains.transpose(1, 0, 2)
    parts = shard_count // EXPERTS
    group_rows = KVH * rows
    state = w_bc.shape[2] // 2
    chunks = rows // EIGHT
    capacity = rows * routes.shape[2] // EXPERTS

    near_tokens = exchange(tokens, "ctx", 2)
    w_own, w_other, key_at = head_weights(w_kv[0], shard_count, me)
    beside = exchange(tokens, "ctx", 1)
    place = jnp.stack([me, key_at, me // parts]).astype(jnp.int32)

    def norm(block, after):
        return pl.pallas_call(
            norm_kernel,
            out_shape=shape((rows, width), BF16),
            in_specs=[SMEM, VMEM, VMEM, ANY],
            out_specs=VMEM,
            compiler_params=params(4),
            cost_estimate=cost(8 * rows * width, 4 * rows * width),
            name="norm",
        )(place, in_hbm(gains), block, after)

    normed_own = norm(in_hbm(tokens), in_hbm(tokens))
    raising, lowering = fetch([w_up[0], w_down[0]], (16, 16), normed_own)
    normed_near = norm(near_tokens, raising)
    normed_far = exchange(normed_near, "ctx", 1)
    projected = (
        shape((KVH, GROUP * rows, HD), BF16),
        shape((2, group_rows, HD), BF16),
    )
    queries, kv, weights = pl.pallas_call(
        project_kernel,
        out_shape=projected + (shape((width, 2 * HD), BF16),),
        in_specs=[SMEM] + [VMEM] * 6,
        out_specs=(VMEM,) * 3,
        scratch_shapes=[pltpu.VMEM((3 * rows, width), BF16)],
        compiler_params=params(12),
        cost_estimate=cost(12 * rows * width * HD, 24 * rows * width),
        name="project",
    )(
        place,
        in_hbm(gains),
        normed_own,
        beside,
        normed_near,
        in_hbm(w_own),
        w_other,
    )
    queries, kv = pl.pallas_call(
        project_last_kernel,
        out_shape=projected,
        in_specs=[SMEM] + [VMEM] * 4,
        out_specs=(VMEM,) * 2,
        compiler_params=params(12),
        cost_estimate=cost(4 * rows * width * HD, 8 * rows * width),
        name="project_last",
    )(place, normed_far, weights, queries, kv)
    turns = shard_count // KVH
    pasts = [exchange(kv, "ctx", turn * KVH) for turn in range(1, turns)]
    small = [dt_in[0], dt_out[0], w_bc[0].T, tokens, w_router[0].T]
    in_one, in_two, in_bct, in_tokens, in_router = fetch(small, (2, 2, 1, 2, 1), kv)
    scored = GROUP * rows * group_rows * KVH
    tallies = (shape((KVH, GROUP * rows, LANES), F32),) * 2 + (
        shape((KVH, GROUP * rows, HD), F32),
    )
    tally = pl.pallas_call(
        near_kernel,
        out_shape=tallies,
        in_specs=[SMEM, VMEM, VMEM],
        out_specs=(VMEM,) * 3,
        compiler_params=params(16),
        cost_estimate=cost(4 * scored * HD, 4 * group_rows * GROUP * HD * 4, scored),
        name="near",
    )(place, queries, kv)
    attended = [None] * KVH
    for slots in ((2, 3), (0, 1)):
        state_now = tally
        for turn, past in enumerate(pasts, 1):
            last = turn == turns - 1
            state_now = pl.pallas_call(
                functools.partial(far_kernel, turn, slots, last),
                out_shape=(shape((rows, GROUP * HD), BF16),) * len(slots) if last else tallies,
                in_specs=[SMEM] + [VMEM] * 5,
                out_specs=(VMEM,) * (len(slots) if last else 3),
                compiler_params=params(16),
                cost_estimate=cost(2 * scored * HD, 2 * group_rows * GROUP * HD * 4, scored // 2),
                name="far",
            )(place, queries, *state_now, past)
        for slot, block in zip(slots, state_now):
            attended[slot] = exchange(block, "ctx", slot) if slot else block

    base, keep, drive, chunk_state, chunk_keep, bc, coef, ends = pl.pallas_call(
        prepare_kernel,
        out_shape=(
            shape((rows, width), F32),
            shape((rows, width), F32),
            shape((rows, width), F32),
            shape((chunks * state, width), F32),
            shape((chunks, width), F32),
            shape((rows, 2 * state), F32),
            shape((rows, rows), F32),
            shape((state, width + LANES), BF16),
        ),
        in_specs=[SMEM] + [VMEM] * (8 + KVH),
        out_specs=(VMEM,) * 8,
        scratch_shapes=[
            pltpu.VMEM((rows, width), BF16),
            pltpu.VMEM((rows, width), F32),
            pltpu.VMEM((rows, width), BF16),
            pltpu.VMEM((rows, width), BF16),
        ],
        compiler_params=params(20),
        cost_estimate=cost(10 * rows * width * 256, 30 * rows * width, 3 * rows * width),
        name="prepare",
    )(
        place,
        in_tokens,
        in_hbm(gains),
        in_hbm(skip_gain),
        in_one,
        in_two,
        in_hbm(dt_bias),
        in_hbm(decay_rate),
        in_bct,
        *attended,
    )
    beside_ends = exchange(ends, "ctx", 1)
    chip_ends = pl.pallas_call(
        pair_kernel,
        out_shape=shape(ends.shape, BF16),
        in_specs=[SMEM, VMEM, VMEM],
        out_specs=VMEM,
        compiler_params=params(8),
        cost_estimate=cost(4 * ends.size, 8 * ends.size),
        name="pair",
    )(place, ends, beside_ends)
    earlier_ends = [exchange(chip_ends, "ctx", mask) for mask in range(2, shard_count, 2)]
    before, faded = pl.pallas_call(
        within_kernel,
        out_shape=(shape((rows, width), F32), shape((rows, width), F32)),
        in_specs=[VMEM] * 4,
        out_specs=(VMEM, VMEM),
        compiler_params=params(16),
        cost_estimate=cost(40 * rows * width, 20 * rows * width),
        name="within",
    )(coef, base, keep, drive)
    second, weighting, *packed = pl.pallas_call(
        route_kernel,
        out_shape=(shape((rows, width), F32), shape((rows, EXPERTS * capacity), F32))
        + (shape((capacity, width), BF16),) * EXPERTS,
        in_specs=[SMEM] + [VMEM] * (9 + len(earlier_ends)),
        out_specs=(VMEM,) * (2 + EXPERTS),
        scratch_shapes=[
            pltpu.VMEM((chunks * state, width), BF16),
            pltpu.VMEM((chunks * state, width), BF16),
            pltpu.VMEM((rows, width), F32),
            pltpu.VMEM((rows, width), BF16),
            pltpu.VMEM((shard_count // 2, state, width + LANES), BF16),
        ],
        compiler_params=params(16),
        cost_estimate=cost(10 * rows * width * 256, 30 * rows * width),
        name="route",
    )(
        place,
        before,
        faded,
        chunk_state,
        chunk_keep,
        bc,
        in_hbm(gains),
        in_router,
        in_hbm(routes[0].T),
        beside_ends,
        *earlier_ends,
    )

    arrived = [packed[0]] + [
        exchange(packed[slot], "ctx", slot * parts) for slot in range(1, EXPERTS)
    ]
    units = raising.shape[1]
    batch_rows = 2 * capacity
    hiddens = [[] for _ in range(0, parts, PAIR)]
    after = packed[0]
    for batch in BATCHES:
        tokens_here = pl.pallas_call(
            gather_kernel,
            out_shape=shape((batch_rows, width), BF16),
            in_specs=[ANY] + [VMEM] * 2,
            out_specs=VMEM,
            compiler_params=params(4),
            cost_estimate=cost(0, 4 * batch_rows * width),
            name="gather",
        )(after, *[arrived[slot] for slot in batch])
        held = [tokens_here] + [
            exchange(tokens_here, "ctx", turn) for turn in range(1, parts)
        ]
        for turn in range(0, parts, PAIR):
            after = pl.pallas_call(
                up_kernel,
                out_shape=shape((PAIR * batch_rows, units), BF16),
                in_specs=[VMEM] * (1 + PAIR),
                out_specs=VMEM,
                compiler_params=params(12),
                cost_estimate=cost(2 * PAIR * batch_rows * width, 2 * width),
                name="up",
            )(raising, *held[turn : turn + PAIR])
            hiddens[turn // PAIR].append(after)

    def lower(start, span, blocks, earlier=()):
        done = len(earlier) // PAIR
        out_rows = batch_rows * (done + len(blocks))
        return pl.pallas_call(
            functools.partial(down_kernel, start, done),
            out_shape=(shape((out_rows, span), BF16),) * PAIR,
            in_specs=[VMEM] * (1 + len(earlier) + len(blocks)),
            out_specs=(VMEM,) * PAIR,
            compiler_params=params(12),
            cost_estimate=cost(
                2 * PAIR * batch_rows * len(blocks) * span * units, 2 * span * units
            ),
            name="down",
        )(lowering, *earlier, *blocks)

    chunk_width = width // CHUNKS
    results = []
    for chunk in range(CHUNKS):
        start = chunk * chunk_width
        part_out = []
        for first_batch, last_batch in hiddens:
            if chunk == 0:
                earlier = lower(start, chunk_width, [first_batch])
                part_out += lower(start, chunk_width, [last_batch], earlier)
            else:
                part_out += lower(start, chunk_width, [first_batch, last_batch])
        sums = [part_out[0]] + [
            exchange(part_out[turn], "ctx", turn) for turn in range(1, parts)
        ]
        joined = pl.pallas_call(
            join_kernel,
            out_shape=(shape((capacity, chunk_width), BF16),) * EXPERTS,
            in_specs=[VMEM] * parts,
            out_specs=(VMEM,) * EXPERTS,
            compiler_params=params(8),
            cost_estimate=cost(
                4 * EXPERTS * capacity * chunk_width, 8 * EXPERTS * capacity * chunk_width
            ),
            name="join",
        )(*sums)
        returned = [joined[0]] + [
            exchange(joined[slot], "ctx", slot * parts) for slot in range(1, EXPERTS)
        ]
        finished = pl.pallas_call(
            functools.partial(finish_kernel, start),
            out_shape=shape((rows, chunk_width), BF16),
            in_specs=[VMEM] * (2 + EXPERTS),
            out_specs=VMEM,
            compiler_params=params(8),
            cost_estimate=cost(
                4 * rows * EXPERTS * capacity * chunk_width, 10 * rows * chunk_width
            ),
            name="finish",
        )(second, weighting, *returned)
        results.append(shifted(finished, "segment", 1))
    return jnp.concatenate(results, 1)[None]


def solution(mesh):
    in_specs = (
        P("segment", "ctx", None),
        P("segment", None, None),
        P("segment", None, "ctx"),
        P("segment", None, None),
        P("segment", None, None),
        P("segment", None),
        P("segment", None),
        P("segment", None, None),
        P("segment", None),
        P("segment", None, None),
        P("segment", "ctx", None),
        P("segment", None, "ctx"),
        P("segment", "ctx", None),
    )
    out_specs = P("segment", "ctx", None)
    return jax.shard_map(
        on_device, mesh=mesh, in_specs=in_specs, out_specs=out_specs, check_vma=False
    )
```

```python
import functools

import jax
import jax.numpy as jnp
from jax import lax
from jax.experimental import pallas as pl
from jax.experimental.pallas import tpu as pltpu
from jax.sharding import PartitionSpec as P

HEADS = 16
KVH = 4
HD = 128
GROUP = HEADS // KVH
EXPERTS = 4
EIGHT = 8
STRIP = 16
LANES = 128
CHUNKS = 2
F32 = jnp.float32
BF16 = jnp.bfloat16
VMEM = pl.BlockSpec(memory_space=pltpu.VMEM)
ANY = pl.BlockSpec(memory_space=pl.ANY)
SMEM = pl.BlockSpec(memory_space=pltpu.SMEM)


def params(mib):
    return pltpu.CompilerParams(vmem_limit_bytes=mib * 2**20)


def cost(flops, moved, transcendentals=0):
    return pl.CostEstimate(
        flops=int(flops), bytes_accessed=int(moved), transcendentals=int(transcendentals)
    )


def shape(dims, dtype):
    return jax.ShapeDtypeStruct(tuple(dims), dtype)


def in_hbm(array):
    return pltpu.with_memory_space_constraint(array, pltpu.HBM)


def rms_norm(values, gain):
    return values * lax.rsqrt(jnp.mean(values * values, -1, keepdims=True) + 1e-06) * gain


def strips(rows, body):
    def step(index, carry):
        body(pl.ds(pl.multiple_of(index * STRIP, STRIP), STRIP))
        return carry

    lax.fori_loop(0, rows // STRIP, step, 0, unroll=4)


def split(values):
    high = values.astype(BF16)
    return high, (values - high.astype(F32)).astype(BF16)


def dot(a, b, dims=((1,), (0,))):
    return lax.dot_general(a, b, (dims, ((), ())), preferred_element_type=F32)


def dot_split(a, b, dims=((1,), (0,))):
    a_high, a_low = a
    b_high, b_low = b
    count = a_high.shape[0]
    both = dot(jnp.concatenate([a_high, a_low], 0), b_high, dims)
    return both[:count] + (both[count:] + dot(a_high, b_low, dims))


def iota(dims, axis):
    return lax.broadcasted_iota(jnp.int32, dims, axis)


def norm_into(out, x, gain):
    def body(at):
        out[at, :] = rms_norm(x[at, :].astype(F32), gain).astype(BF16)

    strips(x.shape[0], body)


def norm_kernel(place, gains, x, after, out):
    norm_into(out, x, gains[0])


def queries_into(q_out, slots, normed, head):
    rows = normed.shape[0] // len(slots)
    for at, slot in enumerate(slots):
        for part in range(GROUP):
            cols = pl.ds(pl.multiple_of((head * GROUP + part) * HD, HD), HD)
            q_out[slot, pl.ds(part * rows, rows), :] = normed[at * rows : (at + 1) * rows, cols]


def project_kernel(
    place, gains, normed_own, beside, normed_near, w_own, w_other, q_out, kv_out, weights, normed
):
    rows = beside.shape[0]
    head = place[0] % KVH
    key_at = place[1]
    weights[:, pl.ds(pl.multiple_of(key_at * HD, HD), HD)] = w_own[...]
    weights[:, pl.ds(pl.multiple_of((1 - key_at) * HD, HD), HD)] = w_other[...]
    normed[:rows, :] = normed_own[...]
    norm_into(normed.at[pl.ds(rows, rows)], beside, gains[0])
    normed[2 * rows :, :] = normed_near[...]
    both = dot(normed[...], weights[...]).astype(BF16)
    kv_out[0, : 3 * rows, :] = both[:, :HD]
    kv_out[1, : 3 * rows, :] = both[:, HD:]
    queries_into(q_out, (0, 1, 2), normed, head)


def project_last_kernel(place, normed, weights, q_in, kv_in, q_out, kv_out):
    rows = normed.shape[0]
    q_out[:3] = q_in[:3]
    kv_out[:, : 3 * rows, :] = kv_in[:, : 3 * rows, :]
    both = dot(normed[...], weights[...]).astype(BF16)
    kv_out[0, 3 * rows :, :] = both[:, :HD]
    kv_out[1, 3 * rows :, :] = both[:, HD:]
    queries_into(q_out, (3,), normed, place[0] % KVH)


def near_kernel(place, q, kv, largest_out, total_out, summed):
    me = place[0]
    rows = q.shape[1] // GROUP
    count = kv.shape[1]
    lane = iota((rows, count), 1)
    key_shard = me ^ (lane // rows)
    later = lane % rows > iota((rows, count), 0)
    for slot in range(KVH):
        shard = me ^ slot
        hidden = (key_shard > shard) | ((key_shard == shard) & later)
        scores = dot(q[slot], kv[0], ((1,), (1,))) * HD ** (-0.5)
        scores = scores.reshape(GROUP, rows, count)
        scores = jnp.where(hidden[None], -1e30, scores).reshape(GROUP * rows, count)
        largest = jnp.max(scores, -1, keepdims=True)
        weights = jnp.exp(scores - largest)
        total = jnp.sum(weights, -1, keepdims=True)
        summed[slot] = dot(weights.astype(BF16), kv[1])
        largest_out[slot] = jnp.broadcast_to(largest, (GROUP * rows, LANES))
        total_out[slot] = jnp.broadcast_to(total, (GROUP * rows, LANES))


def far_kernel(turn, slots, last, place, q, largest, total, summed, past, *outs):
    rows = q.shape[1] // GROUP
    wide = past.shape[1] // LANES
    mine = place[0] // KVH
    seen = (mine ^ turn) < mine

    def keep(at, top, weight, value):
        if last:
            result = (value / weight).astype(BF16)
            for part in range(GROUP):
                cols = slice(part * HD, (part + 1) * HD)
                outs[at][:, cols] = result[part * rows : (part + 1) * rows]
        else:
            outs[0][slots[at]] = top
            outs[1][slots[at]] = weight
            outs[2][slots[at]] = value

    @pl.when(seen)
    def _():
        for at, slot in enumerate(slots):
            scores = dot(q[slot], past[0], ((1,), (1,))) * HD ** (-0.5)
            top = jnp.broadcast_to(jnp.max(scores, -1, keepdims=True), (GROUP * rows, LANES))
            newest = jnp.maximum(largest[slot], top)
            weights = jnp.exp(scores - jnp.concatenate([newest] * wide, 1))
            fade = jnp.exp(largest[slot] - newest)
            weight = jnp.broadcast_to(jnp.sum(weights, -1, keepdims=True), (GROUP * rows, LANES))
            value = summed[slot] * fade + dot(weights.astype(BF16), past[1])
            keep(at, newest, total[slot] * fade + weight, value)

    @pl.when(jnp.logical_not(seen))
    def _():
        for at, slot in enumerate(slots):
            keep(at, largest[slot], total[slot], summed[slot])


def prepare_kernel(
    place, x, gains, skip, dt_in, dt_out, bias, rate, w_bct, *refs
):
    attended = refs[:KVH]
    base, keep_out, drive_out, chunk_state, chunk_keep, bc_out, bct_out, ends = refs[KVH:-4]
    mixed, pre, tail_high, tail_low = refs[-4:]
    rows, width = x.shape
    state = w_bct.shape[0] // 2
    chunks = rows // EIGHT
    head = place[0] % KVH
    span = GROUP * HD
    for slot in range(KVH):
        cols = pl.ds(pl.multiple_of((head ^ slot) * span, span), span)
        base[:, cols] = x[:, cols].astype(F32) + attended[slot][...].astype(F32)

    def normalize(at):
        first = base[at, :]
        mixed_in = rms_norm(first, gains[1]).astype(BF16)
        mixed[at, :] = mixed_in
        base[at, :] = first + skip[...] * mixed_in.astype(F32)

    strips(rows, normalize)
    low_rank = dot(mixed[...], dt_in[...]).astype(BF16)
    pre[...] = dot(low_rank, dt_out[...])
    bct = dot(w_bct[...], mixed[...], ((1,), (1,)))
    bc = bct.T
    bc_out[...] = bc
    bct_out[...] = bct
    b_rows = bct[:state]
    block = width // 4
    edge = iota((EIGHT, block), 0)

    def steps(index, carry):
        at = pl.ds(pl.multiple_of(index * STRIP, STRIP), STRIP)
        for low in range(0, width, block):
            cols = pl.ds(low, block)
            raw = pre[at, cols] + bias[:, cols]
            step_size = jnp.maximum(raw, 0.0) + jnp.log1p(jnp.exp(-jnp.abs(raw)))
            keep = jnp.exp(-step_size * rate[:, cols])
            drive = step_size * mixed[at, cols].astype(F32)
            keep_out[at, cols] = keep
            drive_out[at, cols] = drive
            tails = []
            for part in range(STRIP // EIGHT):
                kept = keep[part * EIGHT : (part + 1) * EIGHT]
                after = jnp.where(edge < EIGHT - 1, pltpu.roll(kept, EIGHT - 1, 0), 1.0)
                for hop in (1, 2, 4):
                    after = after * jnp.where(
                        edge < EIGHT - hop, pltpu.roll(after, EIGHT - hop, 0), 1.0
                    )
                whole = after[0:1] * kept[0:1]
                chunk_keep[pl.ds(index * (STRIP // EIGHT) + part, 1), cols] = whole
                tails.append(after * drive[part * EIGHT : (part + 1) * EIGHT])
            high, low_part = split(jnp.concatenate(tails, 0))
            tail_high[at, cols] = high
            tail_low[at, cols] = low_part
        return carry

    lax.fori_loop(0, rows // STRIP, steps, 0, unroll=2)

    spread = jnp.concatenate([b_rows] * chunks, 0)
    own = iota(spread.shape, 0) // state == iota(spread.shape, 1) // EIGHT
    spread = split(jnp.where(own, spread, 0.0))
    chunk_state[...] = dot_split(spread, (tail_high[...], tail_low[...]))
    products = []
    for tile in range(width // LANES):
        cols = pl.ds(tile * LANES, LANES)
        total = jnp.zeros((state, LANES), F32)
        product = jnp.ones((1, LANES), F32)
        for chunk in range(chunks):
            kept = chunk_keep[chunk : chunk + 1, cols]
            total = total * kept + chunk_state[chunk * state : (chunk + 1) * state, cols]
            product = product * kept
        ends[:, cols] = total.astype(BF16)
        products.append(product)
    ends[:, width:] = jnp.concatenate(products, 0).astype(BF16)


def pair_kernel(place, own, other, ends):
    width = own.shape[1] - LANES
    first = lax.rem(place[0], 2) == 0
    mine = own[...].astype(F32)
    its = other[...].astype(F32)
    earlier = jnp.where(first, mine, its)
    later = jnp.where(first, its, mine)
    fade = later[:, width:]
    for tile in range(width // LANES):
        cols = slice(tile * LANES, (tile + 1) * LANES)
        ends[:, cols] = (earlier[:, cols] * fade[tile : tile + 1] + later[:, cols]).astype(BF16)
    ends[:, width:] = (earlier[:, width:] * fade).astype(BF16)


def within_kernel(bc, bct, base, keep, drive, second, faded, coef):
    rows, width = base.shape
    state = bct.shape[0] // 2
    coupling = dot_split(split(bc[:, state:]), split(bct[:state]))
    row, lane = iota((rows, rows), 0), iota((rows, rows), 1)
    total = jnp.zeros((rows, rows), F32)
    for back in range(EIGHT):
        diagonal = jnp.sum(jnp.where(lane == row - back, coupling, 0.0), 1, keepdims=True)
        total = total + jnp.where((lane == back) & (row % EIGHT >= back), diagonal, 0.0)
    coef[...] = total
    edge = iota((EIGHT, width), 0)

    def chunk(index, carry):
        at = pl.ds(pl.multiple_of(index * EIGHT, EIGHT), EIGHT)
        kept = keep[at, :]
        factors = coef[at, :]
        moved = drive[at, :]
        total = base[at, :] + factors[:, 0:1] * moved
        for back in range(1, EIGHT):
            moved = kept * pltpu.roll(moved, 1, 0)
            total = total + factors[:, back : back + 1] * moved
        second[at, :] = total
        for hop in (1, 2, 4):
            kept = kept * jnp.where(edge >= hop, pltpu.roll(kept, hop, 0), 1.0)
        faded[at, :] = kept
        return carry

    lax.fori_loop(0, rows // EIGHT, chunk, 0, unroll=2)


def route_kernel(
    place, before, faded, chunk_state, chunk_keep, bc, gains, router_t, routes_t, beside, *refs
):
    ends, (second, weighting), packed = refs[:-11], refs[-11:-9], refs[-9:-5]
    state_high, state_low, carried, expert_in, stack = refs[-5:]
    rows, width = before.shape
    chunks = chunk_keep.shape[0]
    state = chunk_state.shape[0] // chunks
    me = place[0]
    own = place[2]
    chip = me // 2
    stack[0] = jnp.zeros_like(beside)
    for slot, end in enumerate(ends, 1):
        stack[slot] = end[...]
    fades = [stack[chip ^ at, :, width:].astype(F32) for at in range(len(ends))]
    last_fade = beside[:, width:].astype(F32)
    second_core = lax.rem(me, 2) == 1
    for tile in range(width // LANES):
        cols = pl.ds(tile * LANES, LANES)
        total = jnp.zeros((state, LANES), F32)
        for at, fade in enumerate(fades):
            joined = total * fade[tile : tile + 1] + stack[chip ^ at, :, cols].astype(F32)
            total = jnp.where(at < chip, joined, total)
        joined = total * last_fade[tile : tile + 1] + beside[:, cols].astype(F32)
        total = jnp.where(second_core, joined, total)
        for chunk in range(chunks):
            at = pl.ds(chunk * state, state)
            high, low = split(total)
            state_high[at, cols] = high
            state_low[at, cols] = low
            total = total * chunk_keep[chunk : chunk + 1, cols] + chunk_state[at, cols]
    wide = chunks * state
    repeat = (iota((state, wide), 1) % state == iota((state, wide), 0)).astype(BF16)
    here = iota((rows, wide), 1) // state == iota((rows, wide), 0) // EIGHT
    spread = [
        jnp.where(here, dot(part, repeat), 0.0).astype(BF16) for part in split(bc[:, state:])
    ]
    carried[...] = dot_split(spread, (state_high[...], state_low[...]))

    def normalize(at):
        values = before[at, :] + carried[at, :] * faded[at, :]
        second[at, :] = values
        expert_in[at, :] = rms_norm(values, gains[2]).astype(BF16)

    strips(rows, normalize)

    expert = iota((EXPERTS, rows), 0)
    uses = (routes_t[0:1, :] == expert) | (routes_t[1:2, :] == expert)
    logits = jnp.where(uses, dot(router_t[...], expert_in[...], ((1,), (1,))), -1e30)
    gates = jnp.where(uses, jnp.exp(logits - jnp.max(logits, 0, keepdims=True)), 0.0)
    gates = gates / jnp.sum(gates, 0, keepdims=True)
    sooner = (iota((rows, rows), 0) < iota((rows, rows), 1)).astype(BF16)
    ranks = dot(jnp.where(uses, 1.0, 0.0).astype(BF16), sooner)
    ranks = jnp.where(uses, ranks, -1.0).astype(jnp.int32)
    capacity = packed[0].shape[0]
    place_row = iota((capacity, rows), 0)
    weights, placings = [], []
    for slot in range(EXPERTS):
        mine = expert == (own ^ slot)
        rank = jnp.sum(jnp.where(mine, ranks, 0), 0, keepdims=True)
        gate = jnp.sum(jnp.where(mine, gates, 0.0), 0, keepdims=True)
        placing = place_row == rank
        weights.append(jnp.where(placing, gate, 0.0))
        placings.append(placing.astype(BF16))
    chosen = dot(jnp.concatenate(placings, 0), expert_in[...]).astype(BF16)
    for slot in range(EXPERTS):
        packed[slot][...] = chosen[slot * capacity : (slot + 1) * capacity]
    weighting[...] = jnp.concatenate(weights, 0).T


def fetch_kernel(pieces, *refs):
    count = len(pieces)
    sources, outs, sems = refs[:count], refs[-count - 1 : -1], refs[-1]
    copies = []
    for source, out, number in zip(sources, outs, pieces):
        rows = source.shape[0] // number
        for piece in range(number):
            at = pl.ds(piece * rows, rows)
            copies.append(
                pltpu.make_async_copy(source.at[at], out.at[at], sems.at[len(copies)])
            )
    for copy in copies:
        copy.start()
    for copy in copies:
        copy.wait()


def fetch(arrays, pieces, after):
    return pl.pallas_call(
        functools.partial(fetch_kernel, pieces),
        out_shape=tuple(shape(array.shape, array.dtype) for array in arrays),
        in_specs=[ANY] * (len(arrays) + 1),
        out_specs=(VMEM,) * len(arrays),
        scratch_shapes=[pltpu.SemaphoreType.DMA((sum(pieces),))],
        compiler_params=params(4),
        cost_estimate=cost(0, sum(array.size * 4 for array in arrays)),
        name="fetch",
    )(*[in_hbm(array) for array in arrays], after)


def gather_kernel(*refs):
    blocks, out = refs[:-1], refs[-1]
    capacity = blocks[0].shape[0]
    for at, block in enumerate(blocks):
        out[at * capacity : (at + 1) * capacity, :] = block[...]


def up_kernel(w_up, tokens, after, hidden):
    tile = 256 if hidden.shape[1] % 256 == 0 else LANES
    for low in range(0, hidden.shape[1], tile):
        cols = slice(low, low + tile)
        raised = dot(tokens[...], w_up[:, cols])
        hidden[:, cols] = (raised * jax.nn.sigmoid(raised)).astype(BF16)


def down_kernel(start, w_down, hidden, after, out):
    tile = 256
    for low in range(0, out.shape[1], tile):
        part = w_down[:, start + low : start + low + tile]
        out[:, low : low + tile] = dot(hidden[...], part).astype(BF16)


def join_kernel(*refs):
    parts, outs = refs[:-EXPERTS], refs[-EXPERTS:]
    capacity = outs[0].shape[0]
    for slot, out in enumerate(outs):
        at = slice(slot * capacity, (slot + 1) * capacity)
        total = parts[0][at, :].astype(F32)
        for part in parts[1:]:
            total = total + part[at, :].astype(F32)
        out[...] = total.astype(BF16)


def finish_kernel(start, second, weighting, *refs):
    blocks, out = refs[:-1], refs[-1]
    rows = jnp.concatenate([block[...] for block in blocks], 0)
    high, low = split(weighting[...])
    cols = slice(start, start + out.shape[1])
    out[...] = (second[:, cols] + (dot(high, rows) + dot(low, rows))).astype(BF16)


def exchange(value, axis, mask):
    count = lax.axis_size(axis)
    return lax.ppermute(value, axis, [(at, at ^ mask) for at in range(count)])


def shifted(value, axis, steps):
    count = lax.axis_size(axis)
    return lax.ppermute(value, axis, [(at, (at + steps) % count) for at in range(count)])


def head_weights(w_kv, shard_count, shard_index):
    if w_kv.shape[1] == HD and shard_count == 2 * KVH:
        return w_kv, exchange(w_kv, "ctx", KVH), shard_index // KVH
    whole = lax.all_gather(w_kv, "ctx", axis=1, tiled=True)
    head = shard_index % KVH
    return (
        lax.dynamic_slice_in_dim(whole, head * HD, HD, 1),
        lax.dynamic_slice_in_dim(whole, (KVH + head) * HD, HD, 1),
        jnp.zeros_like(shard_index),
    )


def on_device(
    acts,
    norm_gains,
    w_kv,
    dt_in,
    dt_out,
    dt_bias,
    decay_rate,
    w_bc,
    skip_gain,
    w_router,
    routes,
    w_up,
    w_down,
):
    shard_count = lax.axis_size("ctx")
    me = lax.axis_index("ctx")
    tokens = acts[0]
    rows, width = tokens.shape
    gains = norm_gains.transpose(1, 0, 2)
    parts = shard_count // EXPERTS
    group_rows = KVH * rows
    state = w_bc.shape[2] // 2
    chunks = rows // EIGHT
    capacity = rows * routes.shape[2] // EXPERTS

    near_tokens = exchange(tokens, "ctx", 2)
    w_own, w_other, key_at = head_weights(w_kv[0], shard_count, me)
    beside = exchange(tokens, "ctx", 1)
    place = jnp.stack([me, key_at, me // parts]).astype(jnp.int32)

    def norm(block, after):
        return pl.pallas_call(
            norm_kernel,
            out_shape=shape((rows, width), BF16),
            in_specs=[SMEM, VMEM, VMEM, ANY],
            out_specs=VMEM,
            compiler_params=params(4),
            cost_estimate=cost(8 * rows * width, 4 * rows * width),
            name="norm",
        )(place, in_hbm(gains), block, after)

    normed_own = norm(in_hbm(tokens), in_hbm(tokens))
    raising, lowering = fetch([w_up[0], w_down[0]], (16, 16), normed_own)
    normed_near = norm(near_tokens, raising)
    normed_far = exchange(normed_near, "ctx", 1)
    projected = (
        shape((KVH, GROUP * rows, HD), BF16),
        shape((2, group_rows, HD), BF16),
    )
    queries, kv, weights = pl.pallas_call(
        project_kernel,
        out_shape=projected + (shape((width, 2 * HD), BF16),),
        in_specs=[SMEM] + [VMEM] * 6,
        out_specs=(VMEM,) * 3,
        scratch_shapes=[pltpu.VMEM((3 * rows, width), BF16)],
        compiler_params=params(12),
        cost_estimate=cost(12 * rows * width * HD, 24 * rows * width),
        name="project",
    )(
        place,
        in_hbm(gains),
        normed_own,
        beside,
        normed_near,
        in_hbm(w_own),
        w_other,
    )
    queries, kv = pl.pallas_call(
        project_last_kernel,
        out_shape=projected,
        in_specs=[SMEM] + [VMEM] * 4,
        out_specs=(VMEM,) * 2,
        compiler_params=params(12),
        cost_estimate=cost(4 * rows * width * HD, 8 * rows * width),
        name="project_last",
    )(place, normed_far, weights, queries, kv)
    turns = shard_count // KVH
    pasts = [exchange(kv, "ctx", turn * KVH) for turn in range(1, turns)]
    small = [dt_in[0], dt_out[0], w_bc[0].T, tokens, w_router[0].T]
    in_one, in_two, in_bct, in_tokens, in_router = fetch(small, (2, 2, 1, 2, 1), kv)
    scored = GROUP * rows * group_rows * KVH
    tallies = (shape((KVH, GROUP * rows, LANES), F32),) * 2 + (
        shape((KVH, GROUP * rows, HD), F32),
    )
    tally = pl.pallas_call(
        near_kernel,
        out_shape=tallies,
        in_specs=[SMEM, VMEM, VMEM],
        out_specs=(VMEM,) * 3,
        compiler_params=params(16),
        cost_estimate=cost(4 * scored * HD, 4 * group_rows * GROUP * HD * 4, scored),
        name="near",
    )(place, queries, kv)
    attended = [None] * KVH
    for slots in ((2, 3), (0, 1)):
        state_now = tally
        for turn, past in enumerate(pasts, 1):
            last = turn == turns - 1
            state_now = pl.pallas_call(
                functools.partial(far_kernel, turn, slots, last),
                out_shape=(shape((rows, GROUP * HD), BF16),) * len(slots) if last else tallies,
                in_specs=[SMEM] + [VMEM] * 5,
                out_specs=(VMEM,) * (len(slots) if last else 3),
                compiler_params=params(16),
                cost_estimate=cost(2 * scored * HD, 2 * group_rows * GROUP * HD * 4, scored // 2),
                name="far",
            )(place, queries, *state_now, past)
        for slot, block in zip(slots, state_now):
            attended[slot] = exchange(block, "ctx", slot) if slot else block

    base, keep, drive, chunk_state, chunk_keep, bc, bct, ends = pl.pallas_call(
        prepare_kernel,
        out_shape=(
            shape((rows, width), F32),
            shape((rows, width), F32),
            shape((rows, width), F32),
            shape((chunks * state, width), F32),
            shape((chunks, width), F32),
            shape((rows, 2 * state), F32),
            shape((2 * state, rows), F32),
            shape((state, width + LANES), BF16),
        ),
        in_specs=[SMEM] + [VMEM] * (8 + KVH),
        out_specs=(VMEM,) * 8,
        scratch_shapes=[
            pltpu.VMEM((rows, width), BF16),
            pltpu.VMEM((rows, width), F32),
            pltpu.VMEM((rows, width), BF16),
            pltpu.VMEM((rows, width), BF16),
        ],
        compiler_params=params(20),
        cost_estimate=cost(10 * rows * width * 256, 30 * rows * width, 3 * rows * width),
        name="prepare",
    )(
        place,
        in_tokens,
        in_hbm(gains),
        in_hbm(skip_gain),
        in_one,
        in_two,
        in_hbm(dt_bias),
        in_hbm(decay_rate),
        in_bct,
        *attended,
    )
    beside_ends = exchange(ends, "ctx", 1)
    chip_ends = pl.pallas_call(
        pair_kernel,
        out_shape=shape(ends.shape, BF16),
        in_specs=[SMEM, VMEM, VMEM],
        out_specs=VMEM,
        compiler_params=params(8),
        cost_estimate=cost(4 * ends.size, 8 * ends.size),
        name="pair",
    )(place, ends, beside_ends)
    earlier_ends = [exchange(chip_ends, "ctx", mask) for mask in range(2, shard_count, 2)]
    before, faded = pl.pallas_call(
        within_kernel,
        out_shape=(shape((rows, width), F32), shape((rows, width), F32)),
        in_specs=[VMEM] * 5,
        out_specs=(VMEM, VMEM),
        scratch_shapes=[pltpu.VMEM((rows, rows), F32)],
        compiler_params=params(12),
        cost_estimate=cost(40 * rows * width, 20 * rows * width),
        name="within",
    )(bc, bct, base, keep, drive)
    second, weighting, *packed = pl.pallas_call(
        route_kernel,
        out_shape=(shape((rows, width), F32), shape((rows, EXPERTS * capacity), F32))
        + (shape((capacity, width), BF16),) * EXPERTS,
        in_specs=[SMEM] + [VMEM] * (9 + len(earlier_ends)),
        out_specs=(VMEM,) * (2 + EXPERTS),
        scratch_shapes=[
            pltpu.VMEM((chunks * state, width), BF16),
            pltpu.VMEM((chunks * state, width), BF16),
            pltpu.VMEM((rows, width), F32),
            pltpu.VMEM((rows, width), BF16),
            pltpu.VMEM((shard_count // 2, state, width + LANES), BF16),
        ],
        compiler_params=params(16),
        cost_estimate=cost(10 * rows * width * 256, 30 * rows * width),
        name="route",
    )(
        place,
        before,
        faded,
        chunk_state,
        chunk_keep,
        bc,
        in_hbm(gains),
        in_router,
        in_hbm(routes[0].T),
        beside_ends,
        *earlier_ends,
    )

    def between_experts(blocks):
        moved = {slot: exchange(blocks[slot], "ctx", slot * parts) for slot in (3, 1, 2)}
        return [blocks[0]] + [moved[slot] for slot in range(1, EXPERTS)]

    units = raising.shape[1]
    expert_rows = EXPERTS * capacity
    arrived = pl.pallas_call(
        gather_kernel,
        out_shape=shape((expert_rows, width), BF16),
        in_specs=[VMEM] * EXPERTS,
        out_specs=VMEM,
        compiler_params=params(4),
        cost_estimate=cost(0, 4 * expert_rows * width),
        name="gather",
    )(*between_experts(packed))
    hiddens = []
    after = arrived
    for turn in range(parts):
        after = pl.pallas_call(
            up_kernel,
            out_shape=shape((expert_rows, units), BF16),
            in_specs=[VMEM, VMEM, ANY],
            out_specs=VMEM,
            compiler_params=params(12),
            cost_estimate=cost(2 * expert_rows * width * units, 2 * width * units),
            name="up",
        )(raising, exchange(arrived, "ctx", turn) if turn else arrived, after)
        hiddens.append(after)
    chunk_width = width // CHUNKS
    results = []
    for chunk in range(CHUNKS):
        start = chunk * chunk_width
        sums = []
        for turn in reversed(range(parts)):
            part_out = pl.pallas_call(
                functools.partial(down_kernel, start),
                out_shape=shape((expert_rows, chunk_width), BF16),
                in_specs=[VMEM, VMEM, ANY],
                out_specs=VMEM,
                compiler_params=params(12),
                cost_estimate=cost(
                    2 * expert_rows * chunk_width * units, 2 * chunk_width * units
                ),
                name="down",
            )(lowering, hiddens[turn], after)
            sums.append(exchange(part_out, "ctx", turn) if turn else part_out)
            after = part_out
        joined = pl.pallas_call(
            join_kernel,
            out_shape=(shape((capacity, chunk_width), BF16),) * EXPERTS,
            in_specs=[VMEM] * parts,
            out_specs=(VMEM,) * EXPERTS,
            compiler_params=params(8),
            cost_estimate=cost(
                4 * EXPERTS * capacity * chunk_width, 8 * EXPERTS * capacity * chunk_width
            ),
            name="join",
        )(*sums)
        after = joined[0]
        returned = between_experts(joined)
        finished = pl.pallas_call(
            functools.partial(finish_kernel, start),
            out_shape=shape((rows, chunk_width), BF16),
            in_specs=[VMEM] * (2 + EXPERTS),
            out_specs=VMEM,
            compiler_params=params(8),
            cost_estimate=cost(
                4 * rows * EXPERTS * capacity * chunk_width, 10 * rows * chunk_width
            ),
            name="finish",
        )(second, weighting, *returned)
        results.append(shifted(finished, "segment", 1))
    return jnp.concatenate(results, 1)[None]


def solution(mesh):
    in_specs = (
        P("segment", "ctx", None),
        P("segment", None, None),
        P("segment", None, "ctx"),
        P("segment", None, None),
        P("segment", None, None),
        P("segment", None),
        P("segment", None),
        P("segment", None, None),
        P("segment", None),
        P("segment", None, None),
        P("segment", "ctx", None),
        P("segment", None, "ctx"),
        P("segment", "ctx", None),
    )
    out_specs = P("segment", "ctx", None)
    return jax.shard_map(
        on_device, mesh=mesh, in_specs=in_specs, out_specs=out_specs, check_vma=False
    )
```

```python
import functools

import jax
import jax.numpy as jnp
from jax import lax
from jax.experimental import pallas as pl
from jax.experimental.pallas import tpu as pltpu
from jax.sharding import PartitionSpec as P

HEADS = 16
KVH = 4
HD = 128
GROUP = HEADS // KVH
EXPERTS = 4
EIGHT = 8
STRIP = 16
LANES = 128
CHUNKS = 2
F32 = jnp.float32
BF16 = jnp.bfloat16
VMEM = pl.BlockSpec(memory_space=pltpu.VMEM)
ANY = pl.BlockSpec(memory_space=pl.ANY)
SMEM = pl.BlockSpec(memory_space=pltpu.SMEM)


def params(mib):
    return pltpu.CompilerParams(vmem_limit_bytes=mib * 2**20)


def cost(flops, moved, transcendentals=0):
    return pl.CostEstimate(
        flops=int(flops), bytes_accessed=int(moved), transcendentals=int(transcendentals)
    )


def shape(dims, dtype):
    return jax.ShapeDtypeStruct(tuple(dims), dtype)


def in_hbm(array):
    return pltpu.with_memory_space_constraint(array, pltpu.HBM)


def rms_norm(values, gain):
    return values * lax.rsqrt(jnp.mean(values * values, -1, keepdims=True) + 1e-06) * gain


def strips(rows, body):
    def step(index, carry):
        body(pl.ds(pl.multiple_of(index * STRIP, STRIP), STRIP))
        return carry

    lax.fori_loop(0, rows // STRIP, step, 0, unroll=4)


def split(values):
    high = values.astype(BF16)
    return high, (values - high.astype(F32)).astype(BF16)


def dot(a, b, dims=((1,), (0,))):
    return lax.dot_general(a, b, (dims, ((), ())), preferred_element_type=F32)


def dot_split(a, b, dims=((1,), (0,))):
    a_high, a_low = a
    b_high, b_low = b
    count = a_high.shape[0]
    both = dot(jnp.concatenate([a_high, a_low], 0), b_high, dims)
    return both[:count] + (both[count:] + dot(a_high, b_low, dims))


def iota(dims, axis):
    return lax.broadcasted_iota(jnp.int32, dims, axis)


def norm_into(out, x, gain):
    def body(at):
        out[at, :] = rms_norm(x[at, :].astype(F32), gain).astype(BF16)

    strips(x.shape[0], body)


def norm_kernel(place, gains, x, after, out):
    norm_into(out, x, gains[0])


def queries_into(q_out, slots, normed, head):
    rows = normed.shape[0] // len(slots)
    for at, slot in enumerate(slots):
        for part in range(GROUP):
            cols = pl.ds(pl.multiple_of((head * GROUP + part) * HD, HD), HD)
            q_out[slot, pl.ds(part * rows, rows), :] = normed[at * rows : (at + 1) * rows, cols]


def project_kernel(
    place, gains, normed_own, beside, normed_near, w_own, w_other, q_out, kv_out, weights, normed
):
    rows = beside.shape[0]
    head = place[0] % KVH
    key_at = place[1]
    weights[:, pl.ds(pl.multiple_of(key_at * HD, HD), HD)] = w_own[...]
    weights[:, pl.ds(pl.multiple_of((1 - key_at) * HD, HD), HD)] = w_other[...]
    normed[:rows, :] = normed_own[...]
    norm_into(normed.at[pl.ds(rows, rows)], beside, gains[0])
    normed[2 * rows :, :] = normed_near[...]
    both = dot(normed[...], weights[...]).astype(BF16)
    kv_out[0, : 3 * rows, :] = both[:, :HD]
    kv_out[1, : 3 * rows, :] = both[:, HD:]
    queries_into(q_out, (0, 1, 2), normed, head)


def project_last_kernel(place, normed, weights, q_in, kv_in, q_out, kv_out):
    rows = normed.shape[0]
    q_out[:3] = q_in[:3]
    kv_out[:, : 3 * rows, :] = kv_in[:, : 3 * rows, :]
    both = dot(normed[...], weights[...]).astype(BF16)
    kv_out[0, 3 * rows :, :] = both[:, :HD]
    kv_out[1, 3 * rows :, :] = both[:, HD:]
    queries_into(q_out, (3,), normed, place[0] % KVH)


def near_kernel(place, q, kv, largest_out, total_out, summed):
    me = place[0]
    rows = q.shape[1] // GROUP
    count = kv.shape[1]
    lane = iota((rows, count), 1)
    key_shard = me ^ (lane // rows)
    later = lane % rows > iota((rows, count), 0)
    for slot in range(KVH):
        shard = me ^ slot
        hidden = (key_shard > shard) | ((key_shard == shard) & later)
        scores = dot(q[slot], kv[0], ((1,), (1,))) * HD ** (-0.5)
        scores = scores.reshape(GROUP, rows, count)
        scores = jnp.where(hidden[None], -1e30, scores).reshape(GROUP * rows, count)
        largest = jnp.max(scores, -1, keepdims=True)
        weights = jnp.exp(scores - largest)
        total = jnp.sum(weights, -1, keepdims=True)
        summed[slot] = dot(weights.astype(BF16), kv[1])
        largest_out[slot] = jnp.broadcast_to(largest, (GROUP * rows, LANES))
        total_out[slot] = jnp.broadcast_to(total, (GROUP * rows, LANES))


def far_kernel(turn, slots, last, place, q, largest, total, summed, past, *outs):
    rows = q.shape[1] // GROUP
    wide = past.shape[1] // LANES
    mine = place[0] // KVH
    seen = (mine ^ turn) < mine

    def keep(at, top, weight, value):
        if last:
            result = (value / weight).astype(BF16)
            for part in range(GROUP):
                cols = slice(part * HD, (part + 1) * HD)
                outs[at][:, cols] = result[part * rows : (part + 1) * rows]
        else:
            outs[0][slots[at]] = top
            outs[1][slots[at]] = weight
            outs[2][slots[at]] = value

    @pl.when(seen)
    def _():
        for at, slot in enumerate(slots):
            scores = dot(q[slot], past[0], ((1,), (1,))) * HD ** (-0.5)
            top = jnp.broadcast_to(jnp.max(scores, -1, keepdims=True), (GROUP * rows, LANES))
            newest = jnp.maximum(largest[slot], top)
            weights = jnp.exp(scores - jnp.concatenate([newest] * wide, 1))
            fade = jnp.exp(largest[slot] - newest)
            weight = jnp.broadcast_to(jnp.sum(weights, -1, keepdims=True), (GROUP * rows, LANES))
            value = summed[slot] * fade + dot(weights.astype(BF16), past[1])
            keep(at, newest, total[slot] * fade + weight, value)

    @pl.when(jnp.logical_not(seen))
    def _():
        for at, slot in enumerate(slots):
            keep(at, largest[slot], total[slot], summed[slot])


def prepare_kernel(
    place, x, gains, skip, dt_in, dt_out, bias, rate, w_bct, *refs
):
    attended = refs[:KVH]
    base, keep_out, drive_out, chunk_state, chunk_keep, bc_out, bct_out, ends = refs[KVH:-4]
    mixed, pre, tail_high, tail_low = refs[-4:]
    rows, width = x.shape
    state = w_bct.shape[0] // 2
    chunks = rows // EIGHT
    head = place[0] % KVH
    span = GROUP * HD
    for slot in range(KVH):
        cols = pl.ds(pl.multiple_of((head ^ slot) * span, span), span)
        base[:, cols] = x[:, cols].astype(F32) + attended[slot][...].astype(F32)

    def normalize(at):
        first = base[at, :]
        mixed_in = rms_norm(first, gains[1]).astype(BF16)
        mixed[at, :] = mixed_in
        base[at, :] = first + skip[...] * mixed_in.astype(F32)

    strips(rows, normalize)
    low_rank = dot(mixed[...], dt_in[...]).astype(BF16)
    pre[...] = dot(low_rank, dt_out[...])
    bct = dot(w_bct[...], mixed[...], ((1,), (1,)))
    bc = bct.T
    bc_out[...] = bc
    bct_out[...] = bct
    b_rows = bct[:state]
    block = width // 4
    edge = iota((EIGHT, block), 0)

    def steps(index, carry):
        at = pl.ds(pl.multiple_of(index * STRIP, STRIP), STRIP)
        for low in range(0, width, block):
            cols = pl.ds(low, block)
            raw = pre[at, cols] + bias[:, cols]
            step_size = jnp.maximum(raw, 0.0) + jnp.log1p(jnp.exp(-jnp.abs(raw)))
            keep = jnp.exp(-step_size * rate[:, cols])
            drive = step_size * mixed[at, cols].astype(F32)
            keep_out[at, cols] = keep
            drive_out[at, cols] = drive
            tails = []
            for part in range(STRIP // EIGHT):
                kept = keep[part * EIGHT : (part + 1) * EIGHT]
                after = jnp.where(edge < EIGHT - 1, pltpu.roll(kept, EIGHT - 1, 0), 1.0)
                for hop in (1, 2, 4):
                    after = after * jnp.where(
                        edge < EIGHT - hop, pltpu.roll(after, EIGHT - hop, 0), 1.0
                    )
                whole = after[0:1] * kept[0:1]
                chunk_keep[pl.ds(index * (STRIP // EIGHT) + part, 1), cols] = whole
                tails.append(after * drive[part * EIGHT : (part + 1) * EIGHT])
            high, low_part = split(jnp.concatenate(tails, 0))
            tail_high[at, cols] = high
            tail_low[at, cols] = low_part
        return carry

    lax.fori_loop(0, rows // STRIP, steps, 0, unroll=2)

    spread = jnp.concatenate([b_rows] * chunks, 0)
    own = iota(spread.shape, 0) // state == iota(spread.shape, 1) // EIGHT
    spread = split(jnp.where(own, spread, 0.0))
    chunk_state[...] = dot_split(spread, (tail_high[...], tail_low[...]))
    products = []
    for tile in range(width // LANES):
        cols = pl.ds(tile * LANES, LANES)
        total = jnp.zeros((state, LANES), F32)
        product = jnp.ones((1, LANES), F32)
        for chunk in range(chunks):
            kept = chunk_keep[chunk : chunk + 1, cols]
            total = total * kept + chunk_state[chunk * state : (chunk + 1) * state, cols]
            product = product * kept
        ends[:, cols] = total.astype(BF16)
        products.append(product)
    ends[:, width:] = jnp.concatenate(products, 0).astype(BF16)


def pair_kernel(place, own, other, ends):
    width = own.shape[1] - LANES
    first = lax.rem(place[0], 2) == 0
    mine = own[...].astype(F32)
    its = other[...].astype(F32)
    earlier = jnp.where(first, mine, its)
    later = jnp.where(first, its, mine)
    fade = later[:, width:]
    for tile in range(width // LANES):
        cols = slice(tile * LANES, (tile + 1) * LANES)
        ends[:, cols] = (earlier[:, cols] * fade[tile : tile + 1] + later[:, cols]).astype(BF16)
    ends[:, width:] = (earlier[:, width:] * fade).astype(BF16)


def within_kernel(bc, bct, base, keep, drive, second, faded, coef):
    rows, width = base.shape
    state = bct.shape[0] // 2
    coupling = dot_split(split(bc[:, state:]), split(bct[:state]))
    row, lane = iota((rows, rows), 0), iota((rows, rows), 1)
    total = jnp.zeros((rows, rows), F32)
    for back in range(EIGHT):
        diagonal = jnp.sum(jnp.where(lane == row - back, coupling, 0.0), 1, keepdims=True)
        total = total + jnp.where((lane == back) & (row % EIGHT >= back), diagonal, 0.0)
    coef[...] = total
    edge = iota((EIGHT, width), 0)

    def chunk(index, carry):
        at = pl.ds(pl.multiple_of(index * EIGHT, EIGHT), EIGHT)
        kept = keep[at, :]
        factors = coef[at, :]
        moved = drive[at, :]
        total = base[at, :] + factors[:, 0:1] * moved
        for back in range(1, EIGHT):
            moved = kept * pltpu.roll(moved, 1, 0)
            total = total + factors[:, back : back + 1] * moved
        second[at, :] = total
        for hop in (1, 2, 4):
            kept = kept * jnp.where(edge >= hop, pltpu.roll(kept, hop, 0), 1.0)
        faded[at, :] = kept
        return carry

    lax.fori_loop(0, rows // EIGHT, chunk, 0, unroll=2)


def route_kernel(
    place, before, faded, chunk_state, chunk_keep, bc, gains, router_t, routes_t, beside, *refs
):
    ends, (second, weighting), packed = refs[:-11], refs[-11:-9], refs[-9:-5]
    state_high, state_low, carried, expert_in, stack = refs[-5:]
    rows, width = before.shape
    chunks = chunk_keep.shape[0]
    state = chunk_state.shape[0] // chunks
    me = place[0]
    own = place[2]
    chip = me // 2
    stack[0] = jnp.zeros_like(beside)
    for slot, end in enumerate(ends, 1):
        stack[slot] = end[...]
    fades = [stack[chip ^ at, :, width:].astype(F32) for at in range(len(ends))]
    last_fade = beside[:, width:].astype(F32)
    second_core = lax.rem(me, 2) == 1
    for tile in range(width // LANES):
        cols = pl.ds(tile * LANES, LANES)
        total = jnp.zeros((state, LANES), F32)
        for at, fade in enumerate(fades):
            joined = total * fade[tile : tile + 1] + stack[chip ^ at, :, cols].astype(F32)
            total = jnp.where(at < chip, joined, total)
        joined = total * last_fade[tile : tile + 1] + beside[:, cols].astype(F32)
        total = jnp.where(second_core, joined, total)
        for chunk in range(chunks):
            at = pl.ds(chunk * state, state)
            high, low = split(total)
            state_high[at, cols] = high
            state_low[at, cols] = low
            total = total * chunk_keep[chunk : chunk + 1, cols] + chunk_state[at, cols]
    wide = chunks * state
    repeat = (iota((state, wide), 1) % state == iota((state, wide), 0)).astype(BF16)
    here = iota((rows, wide), 1) // state == iota((rows, wide), 0) // EIGHT
    spread = [
        jnp.where(here, dot(part, repeat), 0.0).astype(BF16) for part in split(bc[:, state:])
    ]
    carried[...] = dot_split(spread, (state_high[...], state_low[...]))

    def normalize(at):
        values = before[at, :] + carried[at, :] * faded[at, :]
        second[at, :] = values
        expert_in[at, :] = rms_norm(values, gains[2]).astype(BF16)

    strips(rows, normalize)

    expert = iota((EXPERTS, rows), 0)
    uses = (routes_t[0:1, :] == expert) | (routes_t[1:2, :] == expert)
    logits = jnp.where(uses, dot(router_t[...], expert_in[...], ((1,), (1,))), -1e30)
    gates = jnp.where(uses, jnp.exp(logits - jnp.max(logits, 0, keepdims=True)), 0.0)
    gates = gates / jnp.sum(gates, 0, keepdims=True)
    sooner = (iota((rows, rows), 0) < iota((rows, rows), 1)).astype(BF16)
    ranks = dot(jnp.where(uses, 1.0, 0.0).astype(BF16), sooner)
    ranks = jnp.where(uses, ranks, -1.0).astype(jnp.int32)
    capacity = packed[0].shape[0]
    place_row = iota((capacity, rows), 0)
    weights, placings = [], []
    for slot in range(EXPERTS):
        mine = expert == (own ^ slot)
        rank = jnp.sum(jnp.where(mine, ranks, 0), 0, keepdims=True)
        gate = jnp.sum(jnp.where(mine, gates, 0.0), 0, keepdims=True)
        placing = place_row == rank
        weights.append(jnp.where(placing, gate, 0.0))
        placings.append(placing.astype(BF16))
    chosen = dot(jnp.concatenate(placings, 0), expert_in[...]).astype(BF16)
    for slot in range(EXPERTS):
        packed[slot][...] = chosen[slot * capacity : (slot + 1) * capacity]
    weighting[...] = jnp.concatenate(weights, 0).T


def fetch_kernel(pieces, *refs):
    count = len(pieces)
    sources, outs, sems = refs[:count], refs[-count - 1 : -1], refs[-1]
    copies = []
    for source, out, number in zip(sources, outs, pieces):
        rows = source.shape[0] // number
        for piece in range(number):
            at = pl.ds(piece * rows, rows)
            start, end = (source, out) if number == 1 else (source.at[at], out.at[at])
            copies.append(pltpu.make_async_copy(start, end, sems.at[len(copies)]))
    for copy in copies:
        copy.start()
    for copy in copies:
        copy.wait()


def fetch(arrays, pieces, after):
    return pl.pallas_call(
        functools.partial(fetch_kernel, pieces),
        out_shape=tuple(shape(array.shape, array.dtype) for array in arrays),
        in_specs=[ANY] * (len(arrays) + 1),
        out_specs=(VMEM,) * len(arrays),
        scratch_shapes=[pltpu.SemaphoreType.DMA((sum(pieces),))],
        compiler_params=params(4),
        cost_estimate=cost(0, sum(array.size * 4 for array in arrays)),
        name="fetch",
    )(*[in_hbm(array) for array in arrays], after)


def gather_kernel(after, *refs):
    blocks, out = refs[:-1], refs[-1]
    capacity = blocks[0].shape[0]
    for at, block in enumerate(blocks):
        out[at * capacity : (at + 1) * capacity, :] = block[...]


def up_kernel(w_up, after, *refs):
    blocks, hidden = refs[:-1], refs[-1]
    tokens = jnp.concatenate([block[...] for block in blocks], 0)
    tile = 256 if hidden.shape[1] % 256 == 0 else LANES
    for low in range(0, hidden.shape[1], tile):
        cols = slice(low, low + tile)
        raised = dot(tokens, w_up[:, cols])
        hidden[:, cols] = (raised * jax.nn.sigmoid(raised)).astype(BF16)


def down_kernel(start, w_down, hidden, after, *outs):
    rows, width = outs[0].shape
    tile = 256
    for low in range(0, width, tile):
        part = w_down[:, start + low : start + low + tile]
        result = dot(hidden[...], part).astype(BF16)
        for at, out in enumerate(outs):
            out[:, low : low + tile] = result[at * rows : (at + 1) * rows]


def join_kernel(*refs):
    parts, outs = refs[: 1 - EXPERTS], refs[1 - EXPERTS :]
    capacity = outs[0].shape[0]
    for at, out in enumerate(outs):
        here = slice(at * capacity, (at + 1) * capacity)
        total = parts[0][here, :].astype(F32)
        for part in parts[1:]:
            total = total + part[here, :].astype(F32)
        out[...] = total.astype(BF16)


def finish_kernel(start, second, weighting, *refs):
    blocks, parts, out = refs[: EXPERTS - 1], refs[EXPERTS - 1 : -1], refs[-1]
    cols = slice(start, start + out.shape[1])
    total = parts[0][:, cols].astype(F32)
    for part in parts[1:]:
        total = total + part[:, cols].astype(F32)
    rows = jnp.concatenate([total.astype(BF16)] + [block[...] for block in blocks], 0)
    high, low = split(weighting[...])
    out[...] = (second[:, cols] + (dot(high, rows) + dot(low, rows))).astype(BF16)


def exchange(value, axis, mask):
    count = lax.axis_size(axis)
    return lax.ppermute(value, axis, [(at, at ^ mask) for at in range(count)])


def shifted(value, axis, steps):
    count = lax.axis_size(axis)
    return lax.ppermute(value, axis, [(at, (at + steps) % count) for at in range(count)])


def head_weights(w_kv, shard_count, shard_index):
    if w_kv.shape[1] == HD and shard_count == 2 * KVH:
        return w_kv, exchange(w_kv, "ctx", KVH), shard_index // KVH
    whole = lax.all_gather(w_kv, "ctx", axis=1, tiled=True)
    head = shard_index % KVH
    return (
        lax.dynamic_slice_in_dim(whole, head * HD, HD, 1),
        lax.dynamic_slice_in_dim(whole, (KVH + head) * HD, HD, 1),
        jnp.zeros_like(shard_index),
    )


def on_device(
    acts,
    norm_gains,
    w_kv,
    dt_in,
    dt_out,
    dt_bias,
    decay_rate,
    w_bc,
    skip_gain,
    w_router,
    routes,
    w_up,
    w_down,
):
    shard_count = lax.axis_size("ctx")
    me = lax.axis_index("ctx")
    tokens = acts[0]
    rows, width = tokens.shape
    gains = norm_gains.transpose(1, 0, 2)
    parts = shard_count // EXPERTS
    group_rows = KVH * rows
    state = w_bc.shape[2] // 2
    chunks = rows // EIGHT
    capacity = rows * routes.shape[2] // EXPERTS

    near_tokens = exchange(tokens, "ctx", 2)
    w_own, w_other, key_at = head_weights(w_kv[0], shard_count, me)
    beside = exchange(tokens, "ctx", 1)
    place = jnp.stack([me, key_at, me // parts]).astype(jnp.int32)

    def norm(gains, block, after):
        return pl.pallas_call(
            norm_kernel,
            out_shape=shape((rows, width), BF16),
            in_specs=[SMEM, VMEM, VMEM, ANY],
            out_specs=VMEM,
            compiler_params=params(4),
            cost_estimate=cost(8 * rows * width, 4 * rows * width),
            name="norm",
        )(place, gains, block, after)

    normed_own = norm(in_hbm(gains), in_hbm(tokens), in_hbm(tokens))
    here = [w_up[0], w_down[0], gains, w_own, tokens, dt_in[0], dt_out[0], w_bc[0].T]
    here += [skip_gain, dt_bias, decay_rate, w_router[0].T, routes[0].T]
    here = fetch(here, (16, 16) + (1,) * 11, normed_own)
    raising, lowering, gains, w_own, tokens, dt_first, dt_second, w_bct = here[:8]
    skip_gain, dt_bias, decay_rate, router_t, routes_t = here[8:]
    normed_near = norm(gains, near_tokens, raising)
    normed_far = exchange(normed_near, "ctx", 1)
    projected = (
        shape((KVH, GROUP * rows, HD), BF16),
        shape((2, group_rows, HD), BF16),
    )
    queries, kv, weights = pl.pallas_call(
        project_kernel,
        out_shape=projected + (shape((width, 2 * HD), BF16),),
        in_specs=[SMEM] + [VMEM] * 6,
        out_specs=(VMEM,) * 3,
        scratch_shapes=[pltpu.VMEM((3 * rows, width), BF16)],
        compiler_params=params(12),
        cost_estimate=cost(12 * rows * width * HD, 24 * rows * width),
        name="project",
    )(
        place,
        gains,
        normed_own,
        beside,
        normed_near,
        w_own,
        w_other,
    )
    queries, kv = pl.pallas_call(
        project_last_kernel,
        out_shape=projected,
        in_specs=[SMEM] + [VMEM] * 4,
        out_specs=(VMEM,) * 2,
        compiler_params=params(12),
        cost_estimate=cost(4 * rows * width * HD, 8 * rows * width),
        name="project_last",
    )(place, normed_far, weights, queries, kv)
    turns = shard_count // KVH
    pasts = [exchange(kv, "ctx", turn * KVH) for turn in range(1, turns)]
    scored = GROUP * rows * group_rows * KVH
    tallies = (shape((KVH, GROUP * rows, LANES), F32),) * 2 + (
        shape((KVH, GROUP * rows, HD), F32),
    )
    tally = pl.pallas_call(
        near_kernel,
        out_shape=tallies,
        in_specs=[SMEM, VMEM, VMEM],
        out_specs=(VMEM,) * 3,
        compiler_params=params(16),
        cost_estimate=cost(4 * scored * HD, 4 * group_rows * GROUP * HD * 4, scored),
        name="near",
    )(place, queries, kv)
    attended = [None] * KVH
    for slots in ((2, 3), (0, 1)):
        state_now = tally
        for turn, past in enumerate(pasts, 1):
            last = turn == turns - 1
            state_now = pl.pallas_call(
                functools.partial(far_kernel, turn, slots, last),
                out_shape=(shape((rows, GROUP * HD), BF16),) * len(slots) if last else tallies,
                in_specs=[SMEM] + [VMEM] * 5,
                out_specs=(VMEM,) * (len(slots) if last else 3),
                compiler_params=params(16),
                cost_estimate=cost(2 * scored * HD, 2 * group_rows * GROUP * HD * 4, scored // 2),
                name="far",
            )(place, queries, *state_now, past)
        for slot, block in zip(slots, state_now):
            attended[slot] = exchange(block, "ctx", slot) if slot else block

    base, keep, drive, chunk_state, chunk_keep, bc, bct, ends = pl.pallas_call(
        prepare_kernel,
        out_shape=(
            shape((rows, width), F32),
            shape((rows, width), F32),
            shape((rows, width), F32),
            shape((chunks * state, width), F32),
            shape((chunks, width), F32),
            shape((rows, 2 * state), F32),
            shape((2 * state, rows), F32),
            shape((state, width + LANES), BF16),
        ),
        in_specs=[SMEM] + [VMEM] * (8 + KVH),
        out_specs=(VMEM,) * 8,
        scratch_shapes=[
            pltpu.VMEM((rows, width), BF16),
            pltpu.VMEM((rows, width), F32),
            pltpu.VMEM((rows, width), BF16),
            pltpu.VMEM((rows, width), BF16),
        ],
        compiler_params=params(20),
        cost_estimate=cost(10 * rows * width * 256, 30 * rows * width, 3 * rows * width),
        name="prepare",
    )(
        place,
        tokens,
        gains,
        skip_gain,
        dt_first,
        dt_second,
        dt_bias,
        decay_rate,
        w_bct,
        *attended,
    )
    beside_ends = exchange(ends, "ctx", 1)
    chip_ends = pl.pallas_call(
        pair_kernel,
        out_shape=shape(ends.shape, BF16),
        in_specs=[SMEM, VMEM, VMEM],
        out_specs=VMEM,
        compiler_params=params(8),
        cost_estimate=cost(4 * ends.size, 8 * ends.size),
        name="pair",
    )(place, ends, beside_ends)
    earlier_ends = [exchange(chip_ends, "ctx", mask) for mask in range(2, shard_count, 2)]
    before, faded = pl.pallas_call(
        within_kernel,
        out_shape=(shape((rows, width), F32), shape((rows, width), F32)),
        in_specs=[VMEM] * 5,
        out_specs=(VMEM, VMEM),
        scratch_shapes=[pltpu.VMEM((rows, rows), F32)],
        compiler_params=params(12),
        cost_estimate=cost(40 * rows * width, 20 * rows * width),
        name="within",
    )(bc, bct, base, keep, drive)
    second, weighting, *packed = pl.pallas_call(
        route_kernel,
        out_shape=(shape((rows, width), F32), shape((rows, EXPERTS * capacity), F32))
        + (shape((capacity, width), BF16),) * EXPERTS,
        in_specs=[SMEM] + [VMEM] * (9 + len(earlier_ends)),
        out_specs=(VMEM,) * (2 + EXPERTS),
        scratch_shapes=[
            pltpu.VMEM((chunks * state, width), BF16),
            pltpu.VMEM((chunks * state, width), BF16),
            pltpu.VMEM((rows, width), F32),
            pltpu.VMEM((rows, width), BF16),
            pltpu.VMEM((shard_count // 2, state, width + LANES), BF16),
        ],
        compiler_params=params(16),
        cost_estimate=cost(10 * rows * width * 256, 30 * rows * width),
        name="route",
    )(
        place,
        before,
        faded,
        chunk_state,
        chunk_keep,
        bc,
        gains,
        router_t,
        routes_t,
        beside_ends,
        *earlier_ends,
    )

    units = raising.shape[1]

    def lift(blocks, after):
        count = sum(block.shape[0] for block in blocks)
        return pl.pallas_call(
            up_kernel,
            out_shape=shape((count, units), BF16),
            in_specs=[VMEM, ANY] + [VMEM] * len(blocks),
            out_specs=VMEM,
            compiler_params=params(12),
            cost_estimate=cost(2 * count * width * units, 2 * width * units),
            name="up",
        )(raising, after, *blocks)

    def lower(start, span, hidden, after, outs=1):
        count = hidden.shape[0]
        return pl.pallas_call(
            functools.partial(down_kernel, start),
            out_shape=(shape((count // outs, span), BF16),) * outs,
            in_specs=[VMEM, VMEM, ANY],
            out_specs=(VMEM,) * outs,
            compiler_params=params(12),
            cost_estimate=cost(2 * count * span * units, 2 * span * units),
            name="down",
        )(lowering, hidden, after)

    def between_experts(blocks):
        moved = {slot: exchange(blocks[slot - 1], "ctx", slot * parts) for slot in (3, 1, 2)}
        return [moved[slot] for slot in range(1, EXPERTS)]

    moved = between_experts(packed[1:])
    stay = [exchange(packed[0], "ctx", turn) if turn else packed[0] for turn in range(parts)]
    stay_out = lower(0, width, lift(stay, packed[0]), packed[0], parts)
    stay_sums = [stay_out[0]] + [
        exchange(stay_out[turn], "ctx", turn) for turn in range(1, parts)
    ]

    moved_rows = (EXPERTS - 1) * capacity
    arrived = pl.pallas_call(
        gather_kernel,
        out_shape=shape((moved_rows, width), BF16),
        in_specs=[ANY] + [VMEM] * (EXPERTS - 1),
        out_specs=VMEM,
        compiler_params=params(4),
        cost_estimate=cost(0, 4 * moved_rows * width),
        name="gather",
    )(stay_sums[-1], *moved)
    hiddens = []
    after = arrived
    for turn in range(parts):
        after = lift([exchange(arrived, "ctx", turn) if turn else arrived], after)
        hiddens.append(after)
    chunk_width = width // CHUNKS
    results = []
    for chunk in range(CHUNKS):
        start = chunk * chunk_width
        sums = []
        for turn in reversed(range(parts)):
            (part_out,) = lower(start, chunk_width, hiddens[turn], after)
            sums.append(exchange(part_out, "ctx", turn) if turn else part_out)
            after = part_out
        joined = pl.pallas_call(
            join_kernel,
            out_shape=(shape((capacity, chunk_width), BF16),) * (EXPERTS - 1),
            in_specs=[VMEM] * parts,
            out_specs=(VMEM,) * (EXPERTS - 1),
            compiler_params=params(8),
            cost_estimate=cost(4 * moved_rows * chunk_width, 8 * moved_rows * chunk_width),
            name="join",
        )(*sums)
        after = joined[0]
        returned = between_experts(joined)
        finished = pl.pallas_call(
            functools.partial(finish_kernel, start),
            out_shape=shape((rows, chunk_width), BF16),
            in_specs=[VMEM] * (1 + EXPERTS + parts),
            out_specs=VMEM,
            compiler_params=params(8),
            cost_estimate=cost(
                4 * rows * EXPERTS * capacity * chunk_width, 10 * rows * chunk_width
            ),
            name="finish",
        )(second, weighting, *returned, *stay_sums)
        results.append(shifted(finished, "segment", 1))
    return jnp.concatenate(results, 1)[None]


def solution(mesh):
    in_specs = (
        P("segment", "ctx", None),
        P("segment", None, None),
        P("segment", None, "ctx"),
        P("segment", None, None),
        P("segment", None, None),
        P("segment", None),
        P("segment", None),
        P("segment", None, None),
        P("segment", None),
        P("segment", None, None),
        P("segment", "ctx", None),
        P("segment", None, "ctx"),
        P("segment", "ctx", None),
    )
    out_specs = P("segment", "ctx", None)
    return jax.shard_map(
        on_device, mesh=mesh, in_specs=in_specs, out_specs=out_specs, check_vma=False
    )
```

```python
import functools
import math

import jax
import jax.numpy as jnp
from jax import lax
from jax.experimental import pallas as pl
from jax.experimental.pallas import tpu as pltpu
from jax.sharding import PartitionSpec as P

HEADS = 16
KVH = 4
HD = 128
GROUP = HEADS // KVH
EXPERTS = 4
EIGHT = 8
STRIP = 16
LANES = 128
SCALE = HD ** (-0.5) * math.log2(math.e)
CHUNKS = 2
F32 = jnp.float32
BF16 = jnp.bfloat16
VMEM = pl.BlockSpec(memory_space=pltpu.VMEM)
ANY = pl.BlockSpec(memory_space=pl.ANY)
SMEM = pl.BlockSpec(memory_space=pltpu.SMEM)


def params(mib):
    return pltpu.CompilerParams(vmem_limit_bytes=mib * 2**20)


def cost(flops, moved, transcendentals=0):
    return pl.CostEstimate(
        flops=int(flops), bytes_accessed=int(moved), transcendentals=int(transcendentals)
    )


def shape(dims, dtype):
    return jax.ShapeDtypeStruct(tuple(dims), dtype)


def in_hbm(array):
    return pltpu.with_memory_space_constraint(array, pltpu.HBM)


def rms_norm(values, gain):
    return values * lax.rsqrt(jnp.mean(values * values, -1, keepdims=True) + 1e-06) * gain


def strips(rows, body):
    def step(index, carry):
        body(pl.ds(pl.multiple_of(index * STRIP, STRIP), STRIP))
        return carry

    lax.fori_loop(0, rows // STRIP, step, 0, unroll=4)


def split(values):
    high = values.astype(BF16)
    return high, (values - high.astype(F32)).astype(BF16)


def dot(a, b, dims=((1,), (0,))):
    return lax.dot_general(a, b, (dims, ((), ())), preferred_element_type=F32)


def dot_split(a, b, dims=((1,), (0,))):
    a_high, a_low = a
    b_high, b_low = b
    count = a_high.shape[0]
    both = dot(jnp.concatenate([a_high, a_low], 0), b_high, dims)
    return both[:count] + (both[count:] + dot(a_high, b_low, dims))


def iota(dims, axis):
    return lax.broadcasted_iota(jnp.int32, dims, axis)


def norm_into(out, x, gain):
    def body(at):
        out[at, :] = rms_norm(x[at, :].astype(F32), gain).astype(BF16)

    strips(x.shape[0], body)


def norm_kernel(gains, after, *refs):
    count = len(refs) // 2
    for x, out in zip(refs[:count], refs[count:]):
        norm_into(out, x, gains[0])


def project(head, weights, first, second, q_out, kv_out):
    rows = first.shape[0]
    normed = jnp.concatenate([first[...], second[...]], 0)
    both = dot(normed, weights[...]).astype(BF16)
    kv_out[0] = both[:, :HD]
    kv_out[1] = both[:, HD:]
    for slot, shard in enumerate((first, second)):
        for part in range(GROUP):
            cols = pl.ds(pl.multiple_of((head * GROUP + part) * HD, HD), HD)
            q_out[slot, pl.ds(part * rows, rows), :] = shard[:, cols]


def project_kernel(place, w_own, w_other, first, second, q_out, kv_out, weights):
    key_at = place[1]
    weights[:, pl.ds(pl.multiple_of(key_at * HD, HD), HD)] = w_own[...]
    weights[:, pl.ds(pl.multiple_of((1 - key_at) * HD, HD), HD)] = w_other[...]
    project(place[0] % KVH, weights, first, second, q_out, kv_out)


def project_more_kernel(place, weights, first, second, q_out, kv_out):
    project(place[0] % KVH, weights, first, second, q_out, kv_out)


def joined_keys(halves, which):
    return jnp.concatenate([half[which] for half in halves], 0)


def near_kernel(place, *refs):
    queries, halves, (largest_out, total_out, summed) = refs[:2], refs[2:4], refs[4:]
    me = place[0]
    keys, values = joined_keys(halves, 0), joined_keys(halves, 1)
    count = keys.shape[0]
    rows = count // KVH
    lane = iota((rows, count), 1)
    key_shard = me ^ (lane // rows)
    later = lane % rows > iota((rows, count), 0)
    for slot in range(KVH):
        shard = me ^ slot
        hidden = (key_shard > shard) | ((key_shard == shard) & later)
        scores = dot(queries[slot // 2][slot % 2], keys, ((1,), (1,)))
        scores = scores.reshape(GROUP, rows, count)
        scores = jnp.where(hidden[None], -1e30, scores).reshape(GROUP * rows, count)
        largest = jnp.max(scores, -1, keepdims=True)
        weights = jnp.exp2(scores * SCALE - largest * SCALE)
        total = jnp.sum(weights, -1, keepdims=True)
        summed[slot] = dot(weights.astype(BF16), values)
        largest_out[slot] = jnp.broadcast_to(largest, (GROUP * rows, LANES))
        total_out[slot] = jnp.broadcast_to(total, (GROUP * rows, LANES))


def far_kernel(turn, slots, last, place, after, *refs):
    queries, (largest, total, summed), halves, outs = refs[:2], refs[2:5], refs[5:7], refs[7:]
    rows = queries[0].shape[1] // GROUP
    mine = place[0] // KVH
    seen = (mine ^ turn) < mine

    def keep(at, top, weight, value):
        if last:
            result = (value / weight).astype(BF16)
            for part in range(GROUP):
                cols = slice(part * HD, (part + 1) * HD)
                outs[at][:, cols] = result[part * rows : (part + 1) * rows]
        else:
            outs[0][slots[at]] = top
            outs[1][slots[at]] = weight
            outs[2][slots[at]] = value

    @pl.when(seen)
    def _():
        keys, values = joined_keys(halves, 0), joined_keys(halves, 1)
        wide = keys.shape[0] // LANES
        for at, slot in enumerate(slots):
            scores = dot(queries[slot // 2][slot % 2], keys, ((1,), (1,)))
            top = jnp.broadcast_to(jnp.max(scores, -1, keepdims=True), (GROUP * rows, LANES))
            newest = jnp.maximum(largest[slot], top)
            offset = newest * SCALE
            weights = jnp.exp2(scores * SCALE - jnp.concatenate([offset] * wide, 1))
            fade = jnp.exp2(largest[slot] * SCALE - offset)
            weight = jnp.broadcast_to(jnp.sum(weights, -1, keepdims=True), (GROUP * rows, LANES))
            value = summed[slot] * fade + dot(weights.astype(BF16), values)
            keep(at, newest, total[slot] * fade + weight, value)

    @pl.when(jnp.logical_not(seen))
    def _():
        for at, slot in enumerate(slots):
            keep(at, largest[slot], total[slot], summed[slot])


def prepare_kernel(
    place, x, gains, skip, dt_in, dt_out, bias, rate, w_bct, *refs
):
    attended = refs[:KVH]
    base, keep_out, drive_out, chunk_state, chunk_keep, bc_out, bct_out, ends = refs[KVH:-4]
    mixed, pre, tail_high, tail_low = refs[-4:]
    rows, width = x.shape
    state = w_bct.shape[0] // 2
    chunks = rows // EIGHT
    head = place[0] % KVH
    span = GROUP * HD
    for slot in range(KVH):
        cols = pl.ds(pl.multiple_of((head ^ slot) * span, span), span)
        base[:, cols] = x[:, cols].astype(F32) + attended[slot][...].astype(F32)

    def normalize(at):
        first = base[at, :]
        mixed_in = rms_norm(first, gains[1]).astype(BF16)
        mixed[at, :] = mixed_in
        base[at, :] = first + skip[...] * mixed_in.astype(F32)

    strips(rows, normalize)
    low_rank = dot(mixed[...], dt_in[...]).astype(BF16)
    pre[...] = dot(low_rank, dt_out[...])
    bct = dot(w_bct[...], mixed[...], ((1,), (1,)))
    bc = bct.T
    bc_out[...] = bc
    bct_out[...] = bct
    b_rows = bct[:state]
    block = width // 4
    edge = iota((EIGHT, block), 0)

    def steps(index, carry):
        at = pl.ds(pl.multiple_of(index * STRIP, STRIP), STRIP)
        for low in range(0, width, block):
            cols = pl.ds(low, block)
            raw = pre[at, cols] + bias[:, cols]
            step_size = jnp.maximum(raw, 0.0) + jnp.log1p(jnp.exp(-jnp.abs(raw)))
            keep = jnp.exp(-step_size * rate[:, cols])
            drive = step_size * mixed[at, cols].astype(F32)
            keep_out[at, cols] = keep
            drive_out[at, cols] = drive
            tails = []
            for part in range(STRIP // EIGHT):
                kept = keep[part * EIGHT : (part + 1) * EIGHT]
                after = jnp.where(edge < EIGHT - 1, pltpu.roll(kept, EIGHT - 1, 0), 1.0)
                for hop in (1, 2, 4):
                    after = after * jnp.where(
                        edge < EIGHT - hop, pltpu.roll(after, EIGHT - hop, 0), 1.0
                    )
                whole = after[0:1] * kept[0:1]
                chunk_keep[pl.ds(index * (STRIP // EIGHT) + part, 1), cols] = whole
                tails.append(after * drive[part * EIGHT : (part + 1) * EIGHT])
            high, low_part = split(jnp.concatenate(tails, 0))
            tail_high[at, cols] = high
            tail_low[at, cols] = low_part
        return carry

    lax.fori_loop(0, rows // STRIP, steps, 0, unroll=2)

    spread = jnp.concatenate([b_rows] * chunks, 0)
    own = iota(spread.shape, 0) // state == iota(spread.shape, 1) // EIGHT
    spread = split(jnp.where(own, spread, 0.0))
    chunk_state[...] = dot_split(spread, (tail_high[...], tail_low[...]))
    products = []
    for tile in range(width // LANES):
        cols = pl.ds(tile * LANES, LANES)
        total = jnp.zeros((state, LANES), F32)
        product = jnp.ones((1, LANES), F32)
        for chunk in range(chunks):
            kept = chunk_keep[chunk : chunk + 1, cols]
            total = total * kept + chunk_state[chunk * state : (chunk + 1) * state, cols]
            product = product * kept
        ends[:, cols] = total.astype(BF16)
        products.append(product)
    ends[:, width:] = jnp.concatenate(products, 0).astype(BF16)


def pair_kernel(place, own, other, ends):
    width = own.shape[1] - LANES
    first = lax.rem(place[0], 2) == 0
    mine = own[...].astype(F32)
    its = other[...].astype(F32)
    earlier = jnp.where(first, mine, its)
    later = jnp.where(first, its, mine)
    fade = later[:, width:]
    for tile in range(width // LANES):
        cols = slice(tile * LANES, (tile + 1) * LANES)
        ends[:, cols] = (earlier[:, cols] * fade[tile : tile + 1] + later[:, cols]).astype(BF16)
    ends[:, width:] = (earlier[:, width:] * fade).astype(BF16)


def within_kernel(bc, bct, base, keep, drive, second, faded, coef):
    rows, width = base.shape
    state = bct.shape[0] // 2
    coupling = dot_split(split(bc[:, state:]), split(bct[:state]))
    row, lane = iota((rows, rows), 0), iota((rows, rows), 1)
    total = jnp.zeros((rows, rows), F32)
    for back in range(EIGHT):
        diagonal = jnp.sum(jnp.where(lane == row - back, coupling, 0.0), 1, keepdims=True)
        total = total + jnp.where((lane == back) & (row % EIGHT >= back), diagonal, 0.0)
    coef[...] = total
    edge = iota((EIGHT, width), 0)

    def chunk(index, carry):
        at = pl.ds(pl.multiple_of(index * EIGHT, EIGHT), EIGHT)
        kept = keep[at, :]
        factors = coef[at, :]
        moved = drive[at, :]
        total = base[at, :] + factors[:, 0:1] * moved
        for back in range(1, EIGHT):
            moved = kept * pltpu.roll(moved, 1, 0)
            total = total + factors[:, back : back + 1] * moved
        second[at, :] = total
        for hop in (1, 2, 4):
            kept = kept * jnp.where(edge >= hop, pltpu.roll(kept, hop, 0), 1.0)
        faded[at, :] = kept
        return carry

    lax.fori_loop(0, rows // EIGHT, chunk, 0, unroll=2)


def route_kernel(
    place, before, faded, chunk_state, chunk_keep, bc, gains, router_t, routes_t, beside, *refs
):
    ends, (second, weighting), packed = refs[:-11], refs[-11:-9], refs[-9:-5]
    state_high, state_low, carried, expert_in, stack = refs[-5:]
    rows, width = before.shape
    chunks = chunk_keep.shape[0]
    state = chunk_state.shape[0] // chunks
    me = place[0]
    own = place[2]
    chip = me // 2
    stack[0] = jnp.zeros_like(beside)
    for slot, end in enumerate(ends, 1):
        stack[slot] = end[...]
    fades = [stack[chip ^ at, :, width:].astype(F32) for at in range(len(ends))]
    last_fade = beside[:, width:].astype(F32)
    second_core = lax.rem(me, 2) == 1
    for tile in range(width // LANES):
        cols = pl.ds(tile * LANES, LANES)
        total = jnp.zeros((state, LANES), F32)
        for at, fade in enumerate(fades):
            joined = total * fade[tile : tile + 1] + stack[chip ^ at, :, cols].astype(F32)
            total = jnp.where(at < chip, joined, total)
        joined = total * last_fade[tile : tile + 1] + beside[:, cols].astype(F32)
        total = jnp.where(second_core, joined, total)
        for chunk in range(chunks):
            at = pl.ds(chunk * state, state)
            high, low = split(total)
            state_high[at, cols] = high
            state_low[at, cols] = low
            total = total * chunk_keep[chunk : chunk + 1, cols] + chunk_state[at, cols]
    wide = chunks * state
    repeat = (iota((state, wide), 1) % state == iota((state, wide), 0)).astype(BF16)
    here = iota((rows, wide), 1) // state == iota((rows, wide), 0) // EIGHT
    spread = [
        jnp.where(here, dot(part, repeat), 0.0).astype(BF16) for part in split(bc[:, state:])
    ]
    carried[...] = dot_split(spread, (state_high[...], state_low[...]))

    def normalize(at):
        values = before[at, :] + carried[at, :] * faded[at, :]
        second[at, :] = values
        expert_in[at, :] = rms_norm(values, gains[2]).astype(BF16)

    strips(rows, normalize)

    expert = iota((EXPERTS, rows), 0)
    uses = (routes_t[0:1, :] == expert) | (routes_t[1:2, :] == expert)
    logits = jnp.where(uses, dot(router_t[...], expert_in[...], ((1,), (1,))), -1e30)
    gates = jnp.where(uses, jnp.exp(logits - jnp.max(logits, 0, keepdims=True)), 0.0)
    gates = gates / jnp.sum(gates, 0, keepdims=True)
    sooner = (iota((rows, rows), 0) < iota((rows, rows), 1)).astype(BF16)
    ranks = dot(jnp.where(uses, 1.0, 0.0).astype(BF16), sooner)
    ranks = jnp.where(uses, ranks, -1.0).astype(jnp.int32)
    capacity = packed[0].shape[0]
    place_row = iota((capacity, rows), 0)
    weights, placings = [], []
    for slot in range(EXPERTS):
        mine = expert == (own ^ slot)
        rank = jnp.sum(jnp.where(mine, ranks, 0), 0, keepdims=True)
        gate = jnp.sum(jnp.where(mine, gates, 0.0), 0, keepdims=True)
        placing = place_row == rank
        weights.append(jnp.where(placing, gate, 0.0))
        placings.append(placing.astype(BF16))
    chosen = dot(jnp.concatenate(placings, 0), expert_in[...]).astype(BF16)
    for slot in range(EXPERTS):
        packed[slot][...] = chosen[slot * capacity : (slot + 1) * capacity]
    weighting[...] = jnp.concatenate(weights, 0).T


def fetch_kernel(pieces, starts, *refs):
    count = len(pieces)
    sources, outs, sems = refs[:count], refs[-count - 1 : -1], refs[-1]
    copies = []
    for source, out, number, start in zip(sources, outs, pieces, starts):
        rows = out.shape[0] // number
        for piece in range(number):
            begin, end = source, out
            if number > 1:
                at = pl.ds(piece * rows, rows)
                begin, end = source.at[at, pl.ds(start, out.shape[1])], out.at[at]
            copies.append(pltpu.make_async_copy(begin, end, sems.at[len(copies)]))
    for copy in copies:
        copy.start()
    for copy in copies:
        copy.wait()


def fetch(items, after):
    arrays, pieces, starts, widths = zip(*items)
    return pl.pallas_call(
        functools.partial(fetch_kernel, pieces, starts),
        out_shape=tuple(
            shape(array.shape[:-1] + (width,), array.dtype)
            for array, width in zip(arrays, widths)
        ),
        in_specs=[ANY] * (len(arrays) + 1),
        out_specs=(VMEM,) * len(arrays),
        scratch_shapes=[pltpu.SemaphoreType.DMA((sum(pieces),))],
        compiler_params=params(4),
        cost_estimate=cost(0, sum(array.size * 4 for array in arrays)),
        name="fetch",
    )(*[in_hbm(array) for array in arrays], after)


def gather_kernel(after, *refs):
    blocks, out = refs[:-1], refs[-1]
    capacity = blocks[0].shape[0]
    for at, block in enumerate(blocks):
        out[at * capacity : (at + 1) * capacity, :] = block[...]


def up_kernel(w_up, after, *refs):
    blocks, hidden = refs[:-1], refs[-1]
    tokens = jnp.concatenate([block[...] for block in blocks], 0)
    tile = 256 if hidden.shape[1] % 256 == 0 else LANES
    for low in range(0, hidden.shape[1], tile):
        cols = slice(low, low + tile)
        raised = dot(tokens, w_up[:, cols])
        hidden[:, cols] = (raised * jax.nn.sigmoid(raised)).astype(BF16)


def down_kernel(weights, hidden, after, *refs):
    w_downs, outs = refs[:weights], refs[weights:]
    rows = outs[0].shape[0]
    tile = 256
    begin = 0
    for w_down in w_downs:
        for low in range(0, w_down.shape[1], tile):
            result = dot(hidden[...], w_down[:, low : low + tile]).astype(BF16)
            for at, out in enumerate(outs):
                out[:, begin + low : begin + low + tile] = result[at * rows : (at + 1) * rows]
        begin += w_down.shape[1]


def join_kernel(start, own, *refs):
    parts, outs = refs[: 1 - EXPERTS], refs[1 - EXPERTS :]
    capacity, width = outs[0].shape
    for at, out in enumerate(outs):
        here = slice(at * capacity, (at + 1) * capacity)
        total = own[here, :].astype(F32)
        for part in parts:
            total = total + part[here, start : start + width].astype(F32)
        out[...] = total.astype(BF16)


def finish_kernel(start, second, weighting, *refs):
    blocks, parts, out = refs[: EXPERTS - 1], refs[EXPERTS - 1 : -1], refs[-1]
    cols = slice(start, start + out.shape[1])
    total = parts[0][:, cols].astype(F32)
    for part in parts[1:]:
        total = total + part[:, cols].astype(F32)
    rows = jnp.concatenate([total.astype(BF16)] + [block[...] for block in blocks], 0)
    high, low = split(weighting[...])
    out[...] = (second[:, cols] + (dot(high, rows) + dot(low, rows))).astype(BF16)


def exchange(value, axis, mask):
    count = lax.axis_size(axis)
    return lax.ppermute(value, axis, [(at, at ^ mask) for at in range(count)])


def shifted(value, axis, steps):
    count = lax.axis_size(axis)
    return lax.ppermute(value, axis, [(at, (at + steps) % count) for at in range(count)])


def head_weights(w_kv, shard_count, shard_index):
    if w_kv.shape[1] == HD and shard_count == 2 * KVH:
        return w_kv, exchange(w_kv, "ctx", KVH), shard_index // KVH
    whole = lax.all_gather(w_kv, "ctx", axis=1, tiled=True)
    head = shard_index % KVH
    return (
        lax.dynamic_slice_in_dim(whole, head * HD, HD, 1),
        lax.dynamic_slice_in_dim(whole, (KVH + head) * HD, HD, 1),
        jnp.zeros_like(shard_index),
    )


def on_device(
    acts,
    norm_gains,
    w_kv,
    dt_in,
    dt_out,
    dt_bias,
    decay_rate,
    w_bc,
    skip_gain,
    w_router,
    routes,
    w_up,
    w_down,
):
    shard_count = lax.axis_size("ctx")
    me = lax.axis_index("ctx")
    tokens = acts[0]
    rows, width = tokens.shape
    gains = norm_gains.transpose(1, 0, 2)
    parts = shard_count // EXPERTS
    group_rows = KVH * rows
    state = w_bc.shape[2] // 2
    chunks = rows // EIGHT
    capacity = rows * routes.shape[2] // EXPERTS

    near_tokens = exchange(tokens, "ctx", 2)
    w_own, w_other, key_at = head_weights(w_kv[0], shard_count, me)
    beside = exchange(tokens, "ctx", 1)
    place = jnp.stack([me, key_at, me // parts]).astype(jnp.int32)

    def norm(gains, blocks, after):
        return pl.pallas_call(
            norm_kernel,
            out_shape=(shape((rows, width), BF16),) * len(blocks),
            in_specs=[VMEM, ANY] + [VMEM] * len(blocks),
            out_specs=(VMEM,) * len(blocks),
            compiler_params=params(6),
            cost_estimate=cost(8 * rows * width, 4 * rows * width),
            name="norm",
        )(gains, after, *blocks)

    normed = list(norm(in_hbm(gains), [in_hbm(tokens), beside], place))
    half = width // CHUNKS
    here = [gains, w_own, tokens, dt_in[0], dt_out[0], w_bc[0].T]
    here += [skip_gain, dt_bias, decay_rate, w_router[0].T, routes[0].T]
    here = [(array, 1, 0, array.shape[-1]) for array in here]
    here = [(w_up[0], 16, 0, w_up.shape[2]), (w_down[0], 16, 0, half)] + here
    raising, *here = fetch(here, normed[1])
    lowering, gains, w_own, tokens, dt_first, dt_second, w_bct = here[:7]
    lowering = [lowering]
    skip_gain, dt_bias, decay_rate, router_t, routes_t = here[7:]
    normed += norm(gains, [near_tokens], raising)
    normed.append(exchange(normed[2], "ctx", 1))
    projected = (shape((2, GROUP * rows, HD), BF16), shape((2, 2 * rows, HD), BF16))
    first_q, first_kv, weights = pl.pallas_call(
        project_kernel,
        out_shape=projected + (shape((width, 2 * HD), BF16),),
        in_specs=[SMEM] + [VMEM] * 4,
        out_specs=(VMEM,) * 3,
        compiler_params=params(8),
        cost_estimate=cost(8 * rows * width * HD, 16 * rows * width),
        name="project",
    )(place, w_own, w_other, *normed[:2])
    last_q, last_kv = pl.pallas_call(
        project_more_kernel,
        out_shape=projected,
        in_specs=[SMEM] + [VMEM] * 3,
        out_specs=(VMEM,) * 2,
        compiler_params=params(8),
        cost_estimate=cost(8 * rows * width * HD, 16 * rows * width),
        name="project_more",
    )(place, weights, *normed[2:])
    queries, kv = (first_q, last_q), (first_kv, last_kv)
    turns = shard_count // KVH
    pasts = [
        [exchange(half, "ctx", turn * KVH) for half in kv] for turn in range(1, turns)
    ]
    lowering += fetch([(w_down[0], 16, half, half)], last_kv)
    scored = GROUP * rows * group_rows * KVH
    tallies = (shape((KVH, GROUP * rows, LANES), F32),) * 2 + (
        shape((KVH, GROUP * rows, HD), F32),
    )
    tally = pl.pallas_call(
        near_kernel,
        out_shape=tallies,
        in_specs=[SMEM] + [VMEM] * 4,
        out_specs=(VMEM,) * 3,
        compiler_params=params(16),
        cost_estimate=cost(4 * scored * HD, 4 * group_rows * GROUP * HD * 4, scored),
        name="near",
    )(place, *queries, *kv)
    attended = [None] * KVH
    for slots in ((2, 3), (0, 1)):
        state_now = tally
        for turn, past in enumerate(pasts, 1):
            last = turn == turns - 1
            state_now = pl.pallas_call(
                functools.partial(far_kernel, turn, slots, last),
                out_shape=(shape((rows, GROUP * HD), BF16),) * len(slots) if last else tallies,
                in_specs=[SMEM, ANY] + [VMEM] * 7,
                out_specs=(VMEM,) * (len(slots) if last else 3),
                compiler_params=params(16),
                cost_estimate=cost(2 * scored * HD, 2 * group_rows * GROUP * HD * 4, scored // 2),
                name="far",
            )(place, lowering[1], *queries, *state_now, *past)
        for slot, block in zip(slots, state_now):
            attended[slot] = exchange(block, "ctx", slot) if slot else block

    base, keep, drive, chunk_state, chunk_keep, bc, bct, ends = pl.pallas_call(
        prepare_kernel,
        out_shape=(
            shape((rows, width), F32),
            shape((rows, width), F32),
            shape((rows, width), F32),
            shape((chunks * state, width), F32),
            shape((chunks, width), F32),
            shape((rows, 2 * state), F32),
            shape((2 * state, rows), F32),
            shape((state, width + LANES), BF16),
        ),
        in_specs=[SMEM] + [VMEM] * (8 + KVH),
        out_specs=(VMEM,) * 8,
        scratch_shapes=[
            pltpu.VMEM((rows, width), BF16),
            pltpu.VMEM((rows, width), F32),
            pltpu.VMEM((rows, width), BF16),
            pltpu.VMEM((rows, width), BF16),
        ],
        compiler_params=params(20),
        cost_estimate=cost(10 * rows * width * 256, 30 * rows * width, 3 * rows * width),
        name="prepare",
    )(
        place,
        tokens,
        gains,
        skip_gain,
        dt_first,
        dt_second,
        dt_bias,
        decay_rate,
        w_bct,
        *attended,
    )
    beside_ends = exchange(ends, "ctx", 1)
    chip_ends = pl.pallas_call(
        pair_kernel,
        out_shape=shape(ends.shape, BF16),
        in_specs=[SMEM, VMEM, VMEM],
        out_specs=VMEM,
        compiler_params=params(8),
        cost_estimate=cost(4 * ends.size, 8 * ends.size),
        name="pair",
    )(place, ends, beside_ends)
    earlier_ends = [exchange(chip_ends, "ctx", mask) for mask in range(2, shard_count, 2)]
    before, faded = pl.pallas_call(
        within_kernel,
        out_shape=(shape((rows, width), F32), shape((rows, width), F32)),
        in_specs=[VMEM] * 5,
        out_specs=(VMEM, VMEM),
        scratch_shapes=[pltpu.VMEM((rows, rows), F32)],
        compiler_params=params(12),
        cost_estimate=cost(40 * rows * width, 20 * rows * width),
        name="within",
    )(bc, bct, base, keep, drive)
    second, weighting, *packed = pl.pallas_call(
        route_kernel,
        out_shape=(shape((rows, width), F32), shape((rows, EXPERTS * capacity), F32))
        + (shape((capacity, width), BF16),) * EXPERTS,
        in_specs=[SMEM] + [VMEM] * (9 + len(earlier_ends)),
        out_specs=(VMEM,) * (2 + EXPERTS),
        scratch_shapes=[
            pltpu.VMEM((chunks * state, width), BF16),
            pltpu.VMEM((chunks * state, width), BF16),
            pltpu.VMEM((rows, width), F32),
            pltpu.VMEM((rows, width), BF16),
            pltpu.VMEM((shard_count // 2, state, width + LANES), BF16),
        ],
        compiler_params=params(16),
        cost_estimate=cost(10 * rows * width * 256, 30 * rows * width),
        name="route",
    )(
        place,
        before,
        faded,
        chunk_state,
        chunk_keep,
        bc,
        gains,
        router_t,
        routes_t,
        beside_ends,
        *earlier_ends,
    )

    units = raising.shape[1]

    def lift(blocks, after):
        count = sum(block.shape[0] for block in blocks)
        return pl.pallas_call(
            up_kernel,
            out_shape=shape((count, units), BF16),
            in_specs=[VMEM, ANY] + [VMEM] * len(blocks),
            out_specs=VMEM,
            compiler_params=params(12),
            cost_estimate=cost(2 * count * width * units, 2 * width * units),
            name="up",
        )(raising, after, *blocks)

    def lower(weights, hidden, after, outs=1, hurry=False):
        count, span = hidden.shape[0], half * len(weights)
        work = 1 if hurry else units
        return pl.pallas_call(
            functools.partial(down_kernel, len(weights)),
            out_shape=(shape((count // outs, span), BF16),) * outs,
            in_specs=[VMEM, ANY] + [VMEM] * len(weights),
            out_specs=(VMEM,) * outs,
            compiler_params=params(12),
            cost_estimate=cost(2 * count * span * work, 2 * span * work),
            name="down",
        )(hidden, after, *weights)

    def between_experts(blocks):
        moved = {slot: exchange(blocks[slot - 1], "ctx", slot * parts) for slot in (3, 1, 2)}
        return [moved[slot] for slot in range(1, EXPERTS)]

    moved = between_experts(packed[1:])
    stay = [exchange(packed[0], "ctx", turn) if turn else packed[0] for turn in range(parts)]
    stay_out = lower(lowering, lift(stay, packed[0]), packed[0], parts)
    stay_sums = [stay_out[0]] + [
        exchange(stay_out[turn], "ctx", turn) for turn in range(1, parts)
    ]
    moved_rows = (EXPERTS - 1) * capacity
    arrived = pl.pallas_call(
        gather_kernel,
        out_shape=shape((moved_rows, width), BF16),
        in_specs=[ANY] + [VMEM] * (EXPERTS - 1),
        out_specs=VMEM,
        compiler_params=params(4),
        cost_estimate=cost(0, 4 * moved_rows * width),
        name="gather",
    )(stay_sums[-1], *moved)
    hiddens = []
    after = arrived
    for turn in range(parts):
        after = lift([exchange(arrived, "ctx", turn) if turn else arrived], after)
        hiddens.append(after)
    others = []
    for turn in range(1, parts):
        (after,) = lower(lowering, hiddens[turn], after)
        others.append(exchange(after, "ctx", turn))
    results = []
    for chunk in range(CHUNKS):
        (own,) = lower(lowering[chunk : chunk + 1], hiddens[0], after, hurry=chunk > 0)
        joined = pl.pallas_call(
            functools.partial(join_kernel, chunk * half),
            out_shape=(shape((capacity, half), BF16),) * (EXPERTS - 1),
            in_specs=[VMEM] * parts,
            out_specs=(VMEM,) * (EXPERTS - 1),
            compiler_params=params(8),
            cost_estimate=cost(4 * moved_rows * half, 8 * moved_rows * half),
            name="join",
        )(own, *others)
        after = joined[0]
        returned = between_experts(joined)
        finished = pl.pallas_call(
            functools.partial(finish_kernel, chunk * half),
            out_shape=shape((rows, half), BF16),
            in_specs=[VMEM] * (1 + EXPERTS + parts),
            out_specs=VMEM,
            compiler_params=params(8),
            cost_estimate=cost(
                4 * rows * EXPERTS * capacity * half, 10 * rows * half
            ),
            name="finish",
        )(second, weighting, *returned, *stay_sums)
        results.append(shifted(finished, "segment", 1))
    return jnp.concatenate(results, 1)[None]


def solution(mesh):
    in_specs = (
        P("segment", "ctx", None),
        P("segment", None, None),
        P("segment", None, "ctx"),
        P("segment", None, None),
        P("segment", None, None),
        P("segment", None),
        P("segment", None),
        P("segment", None, None),
        P("segment", None),
        P("segment", None, None),
        P("segment", "ctx", None),
        P("segment", None, "ctx"),
        P("segment", "ctx", None),
    )
    out_specs = P("segment", "ctx", None)
    return jax.shard_map(
        on_device, mesh=mesh, in_specs=in_specs, out_specs=out_specs, check_vma=False
    )
```

```python
import functools
import math

import jax
import jax.numpy as jnp
from jax import lax
from jax.experimental import pallas as pl
from jax.experimental.pallas import tpu as pltpu
from jax.sharding import PartitionSpec as P

HEADS = 16
KVH = 4
HD = 128
GROUP = HEADS // KVH
EXPERTS = 4
EIGHT = 8
STRIP = 16
LANES = 128
SCALE = HD ** (-0.5) * math.log2(math.e)
CHUNKS = 2
F32 = jnp.float32
BF16 = jnp.bfloat16
VMEM = pl.BlockSpec(memory_space=pltpu.VMEM)
ANY = pl.BlockSpec(memory_space=pl.ANY)
SMEM = pl.BlockSpec(memory_space=pltpu.SMEM)


def params(mib):
    return pltpu.CompilerParams(vmem_limit_bytes=mib * 2**20)


def cost(flops, moved, transcendentals=0):
    return pl.CostEstimate(
        flops=int(flops), bytes_accessed=int(moved), transcendentals=int(transcendentals)
    )


def shape(dims, dtype):
    return jax.ShapeDtypeStruct(tuple(dims), dtype)


def in_hbm(array):
    return pltpu.with_memory_space_constraint(array, pltpu.HBM)


def rms_norm(values, gain):
    return values * lax.rsqrt(jnp.mean(values * values, -1, keepdims=True) + 1e-06) * gain


def strips(rows, body):
    def step(index, carry):
        body(pl.ds(pl.multiple_of(index * STRIP, STRIP), STRIP))
        return carry

    lax.fori_loop(0, rows // STRIP, step, 0, unroll=4)


def split(values):
    high = values.astype(BF16)
    return high, (values - high.astype(F32)).astype(BF16)


def dot(a, b, dims=((1,), (0,))):
    return lax.dot_general(a, b, (dims, ((), ())), preferred_element_type=F32)


def dot_high(a, b):
    count = a[0].shape[0]
    both = dot(jnp.concatenate(a, 0), b)
    return both[:count] + both[count:]


def dot_split(a, b, dims=((1,), (0,))):
    a_high, a_low = a
    b_high, b_low = b
    count = a_high.shape[0]
    both = dot(jnp.concatenate([a_high, a_low], 0), b_high, dims)
    return both[:count] + (both[count:] + dot(a_high, b_low, dims))


def iota(dims, axis):
    return lax.broadcasted_iota(jnp.int32, dims, axis)


def norm_into(out, x, gain):
    def body(at):
        out[at, :] = rms_norm(x[at, :].astype(F32), gain).astype(BF16)

    strips(x.shape[0], body)


def norm_kernel(gains, after, *refs):
    count = len(refs) // 2
    for x, out in zip(refs[:count], refs[count:]):
        norm_into(out, x, gains[0])


def project(head, weights, first, second, q_out, kv_out):
    rows = first.shape[0]
    normed = jnp.concatenate([first[...], second[...]], 0)
    both = dot(normed, weights[...]).astype(BF16)
    kv_out[0] = both[:, :HD]
    kv_out[1] = both[:, HD:]
    for slot, shard in enumerate((first, second)):
        for part in range(GROUP):
            cols = pl.ds(pl.multiple_of((head * GROUP + part) * HD, HD), HD)
            q_out[slot, pl.ds(part * rows, rows), :] = shard[:, cols]


def project_kernel(place, w_own, w_other, first, second, q_out, kv_out, weights):
    key_at = place[1]
    weights[:, pl.ds(pl.multiple_of(key_at * HD, HD), HD)] = w_own[...]
    weights[:, pl.ds(pl.multiple_of((1 - key_at) * HD, HD), HD)] = w_other[...]
    project(place[0] % KVH, weights, first, second, q_out, kv_out)


def project_more_kernel(place, weights, first, second, q_out, kv_out):
    project(place[0] % KVH, weights, first, second, q_out, kv_out)


def joined_keys(halves, which):
    return jnp.concatenate([half[which] for half in halves], 0)


def near_kernel(place, *refs):
    queries, halves, (largest_out, total_out, summed) = refs[:2], refs[2:4], refs[4:]
    me = place[0]
    keys, values = joined_keys(halves, 0), joined_keys(halves, 1)
    count = keys.shape[0]
    rows = count // KVH
    lane = iota((rows, count), 1)
    key_shard = me ^ (lane // rows)
    later = lane % rows > iota((rows, count), 0)
    for slot in range(KVH):
        shard = me ^ slot
        hidden = (key_shard > shard) | ((key_shard == shard) & later)
        scores = dot(queries[slot // 2][slot % 2], keys, ((1,), (1,)))
        scores = scores.reshape(GROUP, rows, count)
        scores = jnp.where(hidden[None], -1e30, scores).reshape(GROUP * rows, count)
        largest = jnp.max(scores, -1, keepdims=True)
        weights = jnp.exp2(scores * SCALE - largest * SCALE)
        total = jnp.sum(weights, -1, keepdims=True)
        summed[slot] = dot(weights.astype(BF16), values)
        largest_out[slot] = jnp.broadcast_to(largest, (GROUP * rows, LANES))
        total_out[slot] = jnp.broadcast_to(total, (GROUP * rows, LANES))


def far_kernel(turn, slots, last, place, *refs):
    queries, (largest, total, summed), halves, outs = refs[:2], refs[2:5], refs[5:7], refs[7:]
    rows = queries[0].shape[1] // GROUP
    mine = place[0] // KVH
    seen = (mine ^ turn) < mine

    def keep(at, top, weight, value):
        if last:
            result = (value / weight).astype(BF16)
            for part in range(GROUP):
                cols = slice(part * HD, (part + 1) * HD)
                outs[at][:, cols] = result[part * rows : (part + 1) * rows]
        else:
            outs[0][slots[at]] = top
            outs[1][slots[at]] = weight
            outs[2][slots[at]] = value

    @pl.when(seen)
    def _():
        keys, values = joined_keys(halves, 0), joined_keys(halves, 1)
        wide = keys.shape[0] // LANES
        for at, slot in enumerate(slots):
            scores = dot(queries[slot // 2][slot % 2], keys, ((1,), (1,)))
            top = jnp.broadcast_to(jnp.max(scores, -1, keepdims=True), (GROUP * rows, LANES))
            newest = jnp.maximum(largest[slot], top)
            offset = newest * SCALE
            weights = jnp.exp2(scores * SCALE - jnp.concatenate([offset] * wide, 1))
            fade = jnp.exp2(largest[slot] * SCALE - offset)
            weight = jnp.broadcast_to(jnp.sum(weights, -1, keepdims=True), (GROUP * rows, LANES))
            value = summed[slot] * fade + dot(weights.astype(BF16), values)
            keep(at, newest, total[slot] * fade + weight, value)

    @pl.when(jnp.logical_not(seen))
    def _():
        for at, slot in enumerate(slots):
            keep(at, largest[slot], total[slot], summed[slot])


def prepare_kernel(
    place, x, gains, skip, dt_in, dt_out, bias, rate, w_bct, *refs
):
    attended = refs[:KVH]
    base, keep_out, drive_out, chunk_state, chunk_keep, bc_out, bct_out, ends = refs[KVH:-3]
    mixed, pre, tail = refs[-3:]
    rows, width = x.shape
    state = w_bct.shape[0] // 2
    chunks = rows // EIGHT
    head = place[0] % KVH
    span = GROUP * HD
    for slot in range(KVH):
        cols = pl.ds(pl.multiple_of((head ^ slot) * span, span), span)
        base[:, cols] = x[:, cols].astype(F32) + attended[slot][...].astype(F32)

    def normalize(at):
        first = base[at, :]
        mixed_in = rms_norm(first, gains[1]).astype(BF16)
        mixed[at, :] = mixed_in
        base[at, :] = first + skip[...] * mixed_in.astype(F32)

    strips(rows, normalize)
    low_rank = dot(mixed[...], dt_in[...]).astype(BF16)
    pre[...] = dot(low_rank, dt_out[...])
    bct = dot(w_bct[...], mixed[...], ((1,), (1,)))
    bc = bct.T
    bc_out[...] = bc
    bct_out[...] = bct
    b_rows = bct[:state]
    block = width // 4
    edge = iota((EIGHT, block), 0)

    def steps(index, carry):
        at = pl.ds(pl.multiple_of(index * STRIP, STRIP), STRIP)
        for low in range(0, width, block):
            cols = pl.ds(low, block)
            raw = pre[at, cols] + bias[:, cols]
            step_size = jnp.maximum(raw, 0.0) + jnp.log(1.0 + jnp.exp(-jnp.abs(raw)))
            keep = jnp.exp(-step_size * rate[:, cols])
            drive = step_size * mixed[at, cols].astype(F32)
            keep_out[at, cols] = keep
            drive_out[at, cols] = drive
            tails = []
            for part in range(STRIP // EIGHT):
                kept = keep[part * EIGHT : (part + 1) * EIGHT]
                after = jnp.where(edge < EIGHT - 1, pltpu.roll(kept, EIGHT - 1, 0), 1.0)
                for hop in (1, 2, 4):
                    after = after * jnp.where(
                        edge < EIGHT - hop, pltpu.roll(after, EIGHT - hop, 0), 1.0
                    )
                whole = after[0:1] * kept[0:1]
                chunk_keep[pl.ds(index * (STRIP // EIGHT) + part, 1), cols] = whole
                tails.append(after * drive[part * EIGHT : (part + 1) * EIGHT])
            tail[at, cols] = jnp.concatenate(tails, 0).astype(BF16)
        return carry

    lax.fori_loop(0, rows // STRIP, steps, 0, unroll=2)

    spread = jnp.concatenate([b_rows] * chunks, 0)
    own = iota(spread.shape, 0) // state == iota(spread.shape, 1) // EIGHT
    chunk_state[...] = dot_high(split(jnp.where(own, spread, 0.0)), tail[...])
    products = []
    for tile in range(width // LANES):
        cols = pl.ds(tile * LANES, LANES)
        total = jnp.zeros((state, LANES), F32)
        product = jnp.ones((1, LANES), F32)
        for chunk in range(chunks):
            kept = chunk_keep[chunk : chunk + 1, cols]
            total = total * kept + chunk_state[chunk * state : (chunk + 1) * state, cols]
            product = product * kept
        ends[:, cols] = total.astype(BF16)
        products.append(product)
    ends[:, width:] = jnp.concatenate(products, 0).astype(BF16)


def pair_kernel(place, after, own, other, ends):
    width = own.shape[1] - LANES
    first = lax.rem(place[0], 2) == 0
    mine = own[...].astype(F32)
    its = other[...].astype(F32)
    earlier = jnp.where(first, mine, its)
    later = jnp.where(first, its, mine)
    fade = later[:, width:]
    for tile in range(width // LANES):
        cols = slice(tile * LANES, (tile + 1) * LANES)
        ends[:, cols] = (earlier[:, cols] * fade[tile : tile + 1] + later[:, cols]).astype(BF16)
    ends[:, width:] = (earlier[:, width:] * fade).astype(BF16)


def couple_kernel(bc, bct, coef):
    rows = bc.shape[0]
    state = bct.shape[0] // 2
    coupling = dot_split(split(bc[:, state:]), split(bct[:state]))
    row, lane = iota((rows, rows), 0), iota((rows, rows), 1)
    total = jnp.zeros((rows, rows), F32)
    for back in range(EIGHT):
        diagonal = jnp.sum(jnp.where(lane == row - back, coupling, 0.0), 1, keepdims=True)
        total = total + jnp.where((lane == back) & (row % EIGHT >= back), diagonal, 0.0)
    coef[...] = total


def within_kernel(coef, base, keep, drive, second, faded):
    rows, width = base.shape
    edge = iota((EIGHT, width), 0)

    def chunk(index, carry):
        at = pl.ds(pl.multiple_of(index * EIGHT, EIGHT), EIGHT)
        kept = keep[at, :]
        factors = coef[at, :]
        moved = drive[at, :]
        total = base[at, :] + factors[:, 0:1] * moved
        for back in range(1, EIGHT):
            moved = kept * pltpu.roll(moved, 1, 0)
            total = total + factors[:, back : back + 1] * moved
        second[at, :] = total
        for hop in (1, 2, 4):
            kept = kept * jnp.where(edge >= hop, pltpu.roll(kept, hop, 0), 1.0)
        faded[at, :] = kept
        return carry

    lax.fori_loop(0, rows // EIGHT, chunk, 0, unroll=2)


def route_kernel(
    place, before, faded, chunk_state, chunk_keep, bc, gains, router_t, routes_t, beside, *refs
):
    ends, (second, weighting), packed = refs[:-10], refs[-10:-8], refs[-8:-4]
    states, carried, expert_in, stack = refs[-4:]
    rows, width = before.shape
    chunks = chunk_keep.shape[0]
    state = chunk_state.shape[0] // chunks
    me = place[0]
    own = place[2]
    chip = me // 2
    stack[0] = jnp.zeros_like(beside)
    for slot, end in enumerate(ends, 1):
        stack[slot] = end[...]
    fades = [stack[chip ^ at, :, width:].astype(F32) for at in range(len(ends))]
    last_fade = beside[:, width:].astype(F32)
    second_core = lax.rem(me, 2) == 1
    for tile in range(width // LANES):
        cols = pl.ds(tile * LANES, LANES)
        total = jnp.zeros((state, LANES), F32)
        for at, fade in enumerate(fades):
            joined = total * fade[tile : tile + 1] + stack[chip ^ at, :, cols].astype(F32)
            total = jnp.where(at < chip, joined, total)
        joined = total * last_fade[tile : tile + 1] + beside[:, cols].astype(F32)
        total = jnp.where(second_core, joined, total)
        for chunk in range(chunks):
            at = pl.ds(chunk * state, state)
            states[at, cols] = total.astype(BF16)
            total = total * chunk_keep[chunk : chunk + 1, cols] + chunk_state[at, cols]
    wide = chunks * state
    repeat = (iota((state, wide), 1) % state == iota((state, wide), 0)).astype(BF16)
    here = iota((rows, wide), 1) // state == iota((rows, wide), 0) // EIGHT
    spread = [
        jnp.where(here, dot(part, repeat), 0.0).astype(BF16) for part in split(bc[:, state:])
    ]
    carried[...] = dot_high(spread, states[...])

    def normalize(at):
        values = before[at, :] + carried[at, :] * faded[at, :]
        second[at, :] = values
        expert_in[at, :] = rms_norm(values, gains[2]).astype(BF16)

    strips(rows, normalize)

    expert = iota((EXPERTS, rows), 0)
    uses = (routes_t[0:1, :] == expert) | (routes_t[1:2, :] == expert)
    logits = jnp.where(uses, dot(router_t[...], expert_in[...], ((1,), (1,))), -1e30)
    gates = jnp.where(uses, jnp.exp(logits - jnp.max(logits, 0, keepdims=True)), 0.0)
    gates = gates / jnp.sum(gates, 0, keepdims=True)
    sooner = (iota((rows, rows), 0) < iota((rows, rows), 1)).astype(BF16)
    ranks = dot(jnp.where(uses, 1.0, 0.0).astype(BF16), sooner)
    ranks = jnp.where(uses, ranks, -1.0).astype(jnp.int32)
    capacity = packed[0].shape[0]
    place_row = iota((capacity, rows), 0)
    weights, placings = [], []
    for slot in range(EXPERTS):
        mine = expert == (own ^ slot)
        rank = jnp.sum(jnp.where(mine, ranks, 0), 0, keepdims=True)
        gate = jnp.sum(jnp.where(mine, gates, 0.0), 0, keepdims=True)
        placing = place_row == rank
        weights.append(jnp.where(placing, gate, 0.0))
        placings.append(placing.astype(BF16))
    chosen = dot(jnp.concatenate(placings, 0), expert_in[...]).astype(BF16)
    for slot in range(EXPERTS):
        packed[slot][...] = chosen[slot * capacity : (slot + 1) * capacity]
    weighting[...] = jnp.concatenate(weights, 0).T


def fetch_kernel(pieces, starts, *refs):
    count = len(pieces)
    sources, outs, sems = refs[:count], refs[-count - 1 : -1], refs[-1]
    copies = []
    for source, out, number, start in zip(sources, outs, pieces, starts):
        rows = out.shape[0] // number
        for piece in range(number):
            begin, end = source, out
            if number > 1:
                at = pl.ds(piece * rows, rows)
                begin, end = source.at[at, pl.ds(start, out.shape[1])], out.at[at]
            copies.append(pltpu.make_async_copy(begin, end, sems.at[len(copies)]))
    for copy in copies:
        copy.start()
    for copy in copies:
        copy.wait()


def fetch(items, after, hurry=False):
    arrays, pieces, starts, widths = zip(*items)
    return pl.pallas_call(
        functools.partial(fetch_kernel, pieces, starts),
        out_shape=tuple(
            shape(array.shape[:-1] + (width,), array.dtype)
            for array, width in zip(arrays, widths)
        ),
        in_specs=[ANY] * (len(arrays) + 1),
        out_specs=(VMEM,) * len(arrays),
        scratch_shapes=[pltpu.SemaphoreType.DMA((sum(pieces),))],
        compiler_params=params(4),
        cost_estimate=cost(0, 0 if hurry else sum(array.size * 4 for array in arrays)),
        name="fetch",
    )(*[in_hbm(array) for array in arrays], after)


def gather_kernel(after, *refs):
    blocks, out = refs[:-1], refs[-1]
    capacity = blocks[0].shape[0]
    for at, block in enumerate(blocks):
        out[at * capacity : (at + 1) * capacity, :] = block[...]


def up_kernel(w_up, after, *refs):
    blocks, hidden = refs[:-1], refs[-1]
    tokens = jnp.concatenate([block[...] for block in blocks], 0)
    tile = 256 if hidden.shape[1] % 256 == 0 else LANES
    for low in range(0, hidden.shape[1], tile):
        cols = slice(low, low + tile)
        raised = dot(tokens, w_up[:, cols])
        hidden[:, cols] = (raised * jax.nn.sigmoid(raised)).astype(BF16)


def down_kernel(weights, hidden, after, *refs):
    w_downs, outs = refs[:weights], refs[weights:]
    rows = outs[0].shape[0]
    tile = 256
    begin = 0
    for w_down in w_downs:
        for low in range(0, w_down.shape[1], tile):
            result = dot(hidden[...], w_down[:, low : low + tile]).astype(BF16)
            for at, out in enumerate(outs):
                out[:, begin + low : begin + low + tile] = result[at * rows : (at + 1) * rows]
        begin += w_down.shape[1]


def join_kernel(start, own, *refs):
    parts, outs = refs[: 1 - EXPERTS], refs[1 - EXPERTS :]
    capacity, width = outs[0].shape
    for at, out in enumerate(outs):
        here = slice(at * capacity, (at + 1) * capacity)
        total = own[here, :].astype(F32)
        for part in parts:
            total = total + part[here, start : start + width].astype(F32)
        out[...] = total.astype(BF16)


def finish_kernel(start, second, weighting, *refs):
    blocks, parts, out = refs[: EXPERTS - 1], refs[EXPERTS - 1 : -1], refs[-1]
    cols = slice(start, start + out.shape[1])
    total = parts[0][:, cols].astype(F32)
    for part in parts[1:]:
        total = total + part[:, cols].astype(F32)
    rows = jnp.concatenate([total.astype(BF16)] + [block[...] for block in blocks], 0)
    high, low = split(weighting[...])
    out[...] = (second[:, cols] + (dot(high, rows) + dot(low, rows))).astype(BF16)


def exchange(value, axis, mask):
    count = lax.axis_size(axis)
    return lax.ppermute(value, axis, [(at, at ^ mask) for at in range(count)])


def shifted(value, axis, steps):
    count = lax.axis_size(axis)
    return lax.ppermute(value, axis, [(at, (at + steps) % count) for at in range(count)])


def head_weights(w_kv, shard_count, shard_index):
    if w_kv.shape[1] == HD and shard_count == 2 * KVH:
        return w_kv, exchange(w_kv, "ctx", KVH), shard_index // KVH
    whole = lax.all_gather(w_kv, "ctx", axis=1, tiled=True)
    head = shard_index % KVH
    return (
        lax.dynamic_slice_in_dim(whole, head * HD, HD, 1),
        lax.dynamic_slice_in_dim(whole, (KVH + head) * HD, HD, 1),
        jnp.zeros_like(shard_index),
    )


def on_device(
    acts,
    norm_gains,
    w_kv,
    dt_in,
    dt_out,
    dt_bias,
    decay_rate,
    w_bc,
    skip_gain,
    w_router,
    routes,
    w_up,
    w_down,
):
    shard_count = lax.axis_size("ctx")
    me = lax.axis_index("ctx")
    tokens = acts[0]
    rows, width = tokens.shape
    gains = norm_gains.transpose(1, 0, 2)
    parts = shard_count // EXPERTS
    group_rows = KVH * rows
    state = w_bc.shape[2] // 2
    chunks = rows // EIGHT
    capacity = rows * routes.shape[2] // EXPERTS

    near_tokens = exchange(tokens, "ctx", 2)
    w_own, w_other, key_at = head_weights(w_kv[0], shard_count, me)
    beside = exchange(tokens, "ctx", 1)
    place = jnp.stack([me, key_at, me // parts]).astype(jnp.int32)

    def norm(gains, blocks, after):
        return pl.pallas_call(
            norm_kernel,
            out_shape=(shape((rows, width), BF16),) * len(blocks),
            in_specs=[VMEM, ANY] + [VMEM] * len(blocks),
            out_specs=(VMEM,) * len(blocks),
            compiler_params=params(6),
            cost_estimate=cost(8 * rows * width, 4 * rows * width),
            name="norm",
        )(gains, after, *blocks)

    normed = list(norm(in_hbm(gains), [in_hbm(tokens), beside], place))
    half = width // CHUNKS
    here = [gains, w_own, tokens, dt_in[0], dt_out[0], w_bc[0].T]
    here += [skip_gain, dt_bias, decay_rate, w_router[0].T, routes[0].T]
    here = [(array, 1, 0, array.shape[-1]) for array in here]
    here = [(w_up[0], 16, 0, w_up.shape[2]), (w_down[0], 16, 0, half)] + here
    raising, *here = fetch(here, normed[1])
    lowering, gains, w_own, tokens, dt_first, dt_second, w_bct = here[:7]
    lowering = [lowering]
    skip_gain, dt_bias, decay_rate, router_t, routes_t = here[7:]
    normed += norm(gains, [near_tokens], raising)
    normed.append(exchange(normed[2], "ctx", 1))
    projected = (shape((2, GROUP * rows, HD), BF16), shape((2, 2 * rows, HD), BF16))
    first_q, first_kv, weights = pl.pallas_call(
        project_kernel,
        out_shape=projected + (shape((width, 2 * HD), BF16),),
        in_specs=[SMEM] + [VMEM] * 4,
        out_specs=(VMEM,) * 3,
        compiler_params=params(8),
        cost_estimate=cost(8 * rows * width * HD, 16 * rows * width),
        name="project",
    )(place, w_own, w_other, *normed[:2])
    last_q, last_kv = pl.pallas_call(
        project_more_kernel,
        out_shape=projected,
        in_specs=[SMEM] + [VMEM] * 3,
        out_specs=(VMEM,) * 2,
        compiler_params=params(8),
        cost_estimate=cost(8 * rows * width * HD, 16 * rows * width),
        name="project_more",
    )(place, weights, *normed[2:])
    queries, kv = (first_q, last_q), (first_kv, last_kv)
    turns = shard_count // KVH
    pasts = [
        [exchange(half, "ctx", turn * KVH) for half in kv] for turn in range(1, turns)
    ]
    scored = GROUP * rows * group_rows * KVH
    tallies = (shape((KVH, GROUP * rows, LANES), F32),) * 2 + (
        shape((KVH, GROUP * rows, HD), F32),
    )
    tally = pl.pallas_call(
        near_kernel,
        out_shape=tallies,
        in_specs=[SMEM] + [VMEM] * 4,
        out_specs=(VMEM,) * 3,
        compiler_params=params(16),
        cost_estimate=cost(4 * scored * HD, 4 * group_rows * GROUP * HD * 4, scored),
        name="near",
    )(place, *queries, *kv)
    attended = [None] * KVH
    for slots in ((2, 3), (0, 1)):
        state_now = tally
        for turn, past in enumerate(pasts, 1):
            last = turn == turns - 1
            state_now = pl.pallas_call(
                functools.partial(far_kernel, turn, slots, last),
                out_shape=(shape((rows, GROUP * HD), BF16),) * len(slots) if last else tallies,
                in_specs=[SMEM] + [VMEM] * 7,
                out_specs=(VMEM,) * (len(slots) if last else 3),
                compiler_params=params(16),
                cost_estimate=cost(2 * scored * HD, 2 * group_rows * GROUP * HD * 4, scored // 2),
                name="far",
            )(place, *queries, *state_now, *past)
        for slot, block in zip(slots, state_now):
            attended[slot] = exchange(block, "ctx", slot) if slot else block

    base, keep, drive, chunk_state, chunk_keep, bc, bct, ends = pl.pallas_call(
        prepare_kernel,
        out_shape=(
            shape((rows, width), F32),
            shape((rows, width), F32),
            shape((rows, width), F32),
            shape((chunks * state, width), F32),
            shape((chunks, width), F32),
            shape((rows, 2 * state), F32),
            shape((2 * state, rows), F32),
            shape((state, width + LANES), BF16),
        ),
        in_specs=[SMEM] + [VMEM] * (8 + KVH),
        out_specs=(VMEM,) * 8,
        scratch_shapes=[
            pltpu.VMEM((rows, width), BF16),
            pltpu.VMEM((rows, width), F32),
            pltpu.VMEM((rows, width), BF16),
        ],
        compiler_params=params(20),
        cost_estimate=cost(10 * rows * width * 256, 30 * rows * width, 3 * rows * width),
        name="prepare",
    )(
        place,
        tokens,
        gains,
        skip_gain,
        dt_first,
        dt_second,
        dt_bias,
        decay_rate,
        w_bct,
        *attended,
    )
    beside_ends = exchange(ends, "ctx", 1)
    coef = pl.pallas_call(
        couple_kernel,
        out_shape=shape((rows, rows), F32),
        in_specs=[VMEM, VMEM],
        out_specs=VMEM,
        compiler_params=params(4),
        cost_estimate=cost(20 * rows * rows, 20 * rows * rows),
        name="couple",
    )(bc, bct)
    chip_ends = pl.pallas_call(
        pair_kernel,
        out_shape=shape(ends.shape, BF16),
        in_specs=[SMEM, ANY, VMEM, VMEM],
        out_specs=VMEM,
        compiler_params=params(8),
        cost_estimate=cost(4 * ends.size, 8 * ends.size),
        name="pair",
    )(place, coef, ends, beside_ends)
    earlier_ends = [exchange(chip_ends, "ctx", mask) for mask in range(2, shard_count, 2)]
    before, faded = pl.pallas_call(
        within_kernel,
        out_shape=(shape((rows, width), F32), shape((rows, width), F32)),
        in_specs=[VMEM] * 4,
        out_specs=(VMEM, VMEM),
        compiler_params=params(12),
        cost_estimate=cost(40 * rows * width, 20 * rows * width),
        name="within",
    )(coef, base, keep, drive)
    second, weighting, *packed = pl.pallas_call(
        route_kernel,
        out_shape=(shape((rows, width), F32), shape((rows, EXPERTS * capacity), F32))
        + (shape((capacity, width), BF16),) * EXPERTS,
        in_specs=[SMEM] + [VMEM] * (9 + len(earlier_ends)),
        out_specs=(VMEM,) * (2 + EXPERTS),
        scratch_shapes=[
            pltpu.VMEM((chunks * state, width), BF16),
            pltpu.VMEM((rows, width), F32),
            pltpu.VMEM((rows, width), BF16),
            pltpu.VMEM((shard_count // 2, state, width + LANES), BF16),
        ],
        compiler_params=params(16),
        cost_estimate=cost(10 * rows * width * 256, 30 * rows * width),
        name="route",
    )(
        place,
        before,
        faded,
        chunk_state,
        chunk_keep,
        bc,
        gains,
        router_t,
        routes_t,
        beside_ends,
        *earlier_ends,
    )

    units = raising.shape[1]

    def lift(blocks, after):
        count = sum(block.shape[0] for block in blocks)
        return pl.pallas_call(
            up_kernel,
            out_shape=shape((count, units), BF16),
            in_specs=[VMEM, ANY] + [VMEM] * len(blocks),
            out_specs=VMEM,
            compiler_params=params(12),
            cost_estimate=cost(2 * count * width * units, 2 * width * units),
            name="up",
        )(raising, after, *blocks)

    def lower(weights, hidden, after, outs=1, hurry=False):
        count, span = hidden.shape[0], half * len(weights)
        work = 1 if hurry else units
        return pl.pallas_call(
            functools.partial(down_kernel, len(weights)),
            out_shape=(shape((count // outs, span), BF16),) * outs,
            in_specs=[VMEM, ANY] + [VMEM] * len(weights),
            out_specs=(VMEM,) * outs,
            compiler_params=params(12),
            cost_estimate=cost(2 * count * span * work, 2 * span * work),
            name="down",
        )(hidden, after, *weights)

    def between_experts(blocks):
        moved = {slot: exchange(blocks[slot - 1], "ctx", slot * parts) for slot in (3, 1, 2)}
        return [moved[slot] for slot in range(1, EXPERTS)]

    moved = between_experts(packed[1:])
    stay = [exchange(packed[0], "ctx", turn) if turn else packed[0] for turn in range(parts)]
    stay_hidden = lift(stay, packed[0])
    lowering += fetch([(w_down[0], 16, half, half)], stay_hidden, hurry=True)
    stay_out = lower(lowering, stay_hidden, packed[0], parts)
    stay_sums = [stay_out[0]] + [
        exchange(stay_out[turn], "ctx", turn) for turn in range(1, parts)
    ]
    moved_rows = (EXPERTS - 1) * capacity
    arrived = pl.pallas_call(
        gather_kernel,
        out_shape=shape((moved_rows, width), BF16),
        in_specs=[ANY] + [VMEM] * (EXPERTS - 1),
        out_specs=VMEM,
        compiler_params=params(4),
        cost_estimate=cost(0, 4 * moved_rows * width),
        name="gather",
    )(stay_sums[-1], *moved)
    hiddens = []
    after = arrived
    for turn in range(parts):
        after = lift([exchange(arrived, "ctx", turn) if turn else arrived], after)
        hiddens.append(after)
    others = []
    for turn in range(1, parts):
        (after,) = lower(lowering, hiddens[turn], after)
        others.append(exchange(after, "ctx", turn))
    results = []
    for chunk in range(CHUNKS):
        (own,) = lower(lowering[chunk : chunk + 1], hiddens[0], after, hurry=chunk > 0)
        joined = pl.pallas_call(
            functools.partial(join_kernel, chunk * half),
            out_shape=(shape((capacity, half), BF16),) * (EXPERTS - 1),
            in_specs=[VMEM] * parts,
            out_specs=(VMEM,) * (EXPERTS - 1),
            compiler_params=params(8),
            cost_estimate=cost(4 * moved_rows * half, 8 * moved_rows * half),
            name="join",
        )(own, *others)
        after = joined[0]
        returned = between_experts(joined)
        finished = pl.pallas_call(
            functools.partial(finish_kernel, chunk * half),
            out_shape=shape((rows, half), BF16),
            in_specs=[VMEM] * (1 + EXPERTS + parts),
            out_specs=VMEM,
            compiler_params=params(8),
            cost_estimate=cost(
                4 * rows * EXPERTS * capacity * half, 10 * rows * half
            ),
            name="finish",
        )(second, weighting, *returned, *stay_sums)
        results.append(shifted(finished, "segment", 1))
    return jnp.concatenate(results, 1)[None]


def solution(mesh):
    in_specs = (
        P("segment", "ctx", None),
        P("segment", None, None),
        P("segment", None, "ctx"),
        P("segment", None, None),
        P("segment", None, None),
        P("segment", None),
        P("segment", None),
        P("segment", None, None),
        P("segment", None),
        P("segment", None, None),
        P("segment", "ctx", None),
        P("segment", None, "ctx"),
        P("segment", "ctx", None),
    )
    out_specs = P("segment", "ctx", None)
    return jax.shard_map(
        on_device, mesh=mesh, in_specs=in_specs, out_specs=out_specs, check_vma=False
    )
```

```python
import functools
import math

import jax
import jax.numpy as jnp
from jax import lax
from jax.experimental import pallas as pl
from jax.experimental.pallas import tpu as pltpu
from jax.sharding import PartitionSpec as P

HEADS = 16
KVH = 4
HD = 128
GROUP = HEADS // KVH
EXPERTS = 4
EIGHT = 8
STRIP = 16
LANES = 128
SCALE = HD ** (-0.5) * math.log2(math.e)
CUTS = (0, 9, 16)
F32 = jnp.float32
BF16 = jnp.bfloat16
VMEM = pl.BlockSpec(memory_space=pltpu.VMEM)
ANY = pl.BlockSpec(memory_space=pl.ANY)
SMEM = pl.BlockSpec(memory_space=pltpu.SMEM)


def params(mib):
    return pltpu.CompilerParams(vmem_limit_bytes=mib * 2**20)


def cost(flops, moved, transcendentals=0):
    return pl.CostEstimate(
        flops=int(flops), bytes_accessed=int(moved), transcendentals=int(transcendentals)
    )


def shape(dims, dtype):
    return jax.ShapeDtypeStruct(tuple(dims), dtype)


def in_hbm(array):
    return pltpu.with_memory_space_constraint(array, pltpu.HBM)


def rms_norm(values, gain):
    return values * lax.rsqrt(jnp.mean(values * values, -1, keepdims=True) + 1e-06) * gain


def strips(rows, body):
    def step(index, carry):
        body(pl.ds(pl.multiple_of(index * STRIP, STRIP), STRIP))
        return carry

    lax.fori_loop(0, rows // STRIP, step, 0, unroll=4)


def split(values):
    high = values.astype(BF16)
    return high, (values - high.astype(F32)).astype(BF16)


def dot(a, b, dims=((1,), (0,))):
    return lax.dot_general(a, b, (dims, ((), ())), preferred_element_type=F32)


def dot_high(a, b):
    count = a[0].shape[0]
    both = dot(jnp.concatenate(a, 0), b)
    return both[:count] + both[count:]


def dot_split(a, b, dims=((1,), (0,))):
    a_high, a_low = a
    b_high, b_low = b
    count = a_high.shape[0]
    both = dot(jnp.concatenate([a_high, a_low], 0), b_high, dims)
    return both[:count] + (both[count:] + dot(a_high, b_low, dims))


def iota(dims, axis):
    return lax.broadcasted_iota(jnp.int32, dims, axis)


def norm_into(out, x, gain):
    def body(at):
        out[at, :] = rms_norm(x[at, :].astype(F32), gain).astype(BF16)

    strips(x.shape[0], body)


def norm_kernel(gains, after, *refs):
    count = len(refs) // 2
    for x, out in zip(refs[:count], refs[count:]):
        norm_into(out, x, gains[0])


def project(head, weights, first, second, q_out, kv_out):
    rows = first.shape[0]
    normed = jnp.concatenate([first[...], second[...]], 0)
    both = dot(normed, weights[...]).astype(BF16)
    kv_out[0] = both[:, :HD]
    kv_out[1] = both[:, HD:]
    for slot, shard in enumerate((first, second)):
        for part in range(GROUP):
            cols = pl.ds(pl.multiple_of((head * GROUP + part) * HD, HD), HD)
            q_out[slot, pl.ds(part * rows, rows), :] = shard[:, cols]


def project_kernel(place, w_own, w_other, first, second, q_out, kv_out, weights):
    key_at = place[1]
    weights[:, pl.ds(pl.multiple_of(key_at * HD, HD), HD)] = w_own[...]
    weights[:, pl.ds(pl.multiple_of((1 - key_at) * HD, HD), HD)] = w_other[...]
    project(place[0] % KVH, weights, first, second, q_out, kv_out)


def project_more_kernel(place, weights, first, second, q_out, kv_out):
    project(place[0] % KVH, weights, first, second, q_out, kv_out)


def joined_keys(halves, which):
    return jnp.concatenate([half[which] for half in halves], 0)


def near_kernel(place, *refs):
    queries, halves, (largest_out, total_out, summed) = refs[:2], refs[2:4], refs[4:]
    me = place[0]
    keys, values = joined_keys(halves, 0), joined_keys(halves, 1)
    count = keys.shape[0]
    rows = count // KVH
    lane = iota((rows, count), 1)
    key_shard = me ^ (lane // rows)
    later = lane % rows > iota((rows, count), 0)
    for slot in range(KVH):
        shard = me ^ slot
        hidden = (key_shard > shard) | ((key_shard == shard) & later)
        scores = dot(queries[slot // 2][slot % 2], keys, ((1,), (1,)))
        scores = scores.reshape(GROUP, rows, count)
        scores = jnp.where(hidden[None], -1e30, scores).reshape(GROUP * rows, count)
        largest = jnp.max(scores, -1, keepdims=True)
        weights = jnp.exp2(scores * SCALE - largest * SCALE)
        total = jnp.sum(weights, -1, keepdims=True)
        summed[slot] = dot(weights.astype(BF16), values)
        largest_out[slot] = jnp.broadcast_to(largest, (GROUP * rows, LANES))
        total_out[slot] = jnp.broadcast_to(total, (GROUP * rows, LANES))


def far_kernel(turn, slots, last, parts, place, *refs):
    queries, (largest, total, summed), refs = refs[:2], refs[2:5], refs[5:]
    halves, outs = refs[:parts], refs[parts:]
    rows = queries[0].shape[1] // GROUP
    mine = place[0] // KVH
    seen = (mine ^ turn) < mine

    def keep(at, top, weight, value):
        if last:
            result = (value / weight).astype(BF16)
            for part in range(GROUP):
                cols = slice(part * HD, (part + 1) * HD)
                outs[at][:, cols] = result[part * rows : (part + 1) * rows]
        else:
            outs[0][slots[at]] = top
            outs[1][slots[at]] = weight
            outs[2][slots[at]] = value

    @pl.when(seen)
    def _():
        keys, values = joined_keys(halves, 0), joined_keys(halves, 1)
        wide = keys.shape[0] // LANES
        for at, slot in enumerate(slots):
            scores = dot(queries[slot // 2][slot % 2], keys, ((1,), (1,)))
            top = jnp.broadcast_to(jnp.max(scores, -1, keepdims=True), (GROUP * rows, LANES))
            newest = jnp.maximum(largest[slot], top)
            offset = newest * SCALE
            weights = jnp.exp2(scores * SCALE - jnp.concatenate([offset] * wide, 1))
            fade = jnp.exp2(largest[slot] * SCALE - offset)
            weight = jnp.broadcast_to(jnp.sum(weights, -1, keepdims=True), (GROUP * rows, LANES))
            value = summed[slot] * fade + dot(weights.astype(BF16), values)
            keep(at, newest, total[slot] * fade + weight, value)

    @pl.when(jnp.logical_not(seen))
    def _():
        for at, slot in enumerate(slots):
            keep(at, largest[slot], total[slot], summed[slot])


def prepare_kernel(
    place, x, gains, skip, dt_in, dt_out, bias, rate, w_bct, *refs
):
    attended = refs[:KVH]
    base, keep_out, drive_out, chunk_state, chunk_keep, bc_out, bct_out, ends = refs[KVH:-3]
    mixed, pre, tail = refs[-3:]
    rows, width = x.shape
    state = w_bct.shape[0] // 2
    chunks = rows // EIGHT
    head = place[0] % KVH
    span = GROUP * HD
    for slot in range(KVH):
        cols = pl.ds(pl.multiple_of((head ^ slot) * span, span), span)
        base[:, cols] = x[:, cols].astype(F32) + attended[slot][...].astype(F32)

    def normalize(at):
        first = base[at, :]
        mixed_in = rms_norm(first, gains[1]).astype(BF16)
        mixed[at, :] = mixed_in
        base[at, :] = first + skip[...] * mixed_in.astype(F32)

    strips(rows, normalize)
    low_rank = dot(mixed[...], dt_in[...]).astype(BF16)
    pre[...] = dot(low_rank, dt_out[...])
    bct = dot(w_bct[...], mixed[...], ((1,), (1,)))
    bc = bct.T
    bc_out[...] = bc
    bct_out[...] = bct
    b_rows = bct[:state]
    block = width // 4
    edge = iota((EIGHT, block), 0)

    def steps(index, carry):
        at = pl.ds(pl.multiple_of(index * STRIP, STRIP), STRIP)
        for low in range(0, width, block):
            cols = pl.ds(low, block)
            raw = pre[at, cols] + bias[:, cols]
            step_size = jnp.maximum(raw, 0.0) + jnp.log(1.0 + jnp.exp(-jnp.abs(raw)))
            keep = jnp.exp(-step_size * rate[:, cols])
            drive = step_size * mixed[at, cols].astype(F32)
            keep_out[at, cols] = keep
            drive_out[at, cols] = drive
            tails = []
            for part in range(STRIP // EIGHT):
                kept = keep[part * EIGHT : (part + 1) * EIGHT]
                after = jnp.where(edge < EIGHT - 1, pltpu.roll(kept, EIGHT - 1, 0), 1.0)
                for hop in (1, 2, 4):
                    after = after * jnp.where(
                        edge < EIGHT - hop, pltpu.roll(after, EIGHT - hop, 0), 1.0
                    )
                whole = after[0:1] * kept[0:1]
                chunk_keep[pl.ds(index * (STRIP // EIGHT) + part, 1), cols] = whole
                tails.append(after * drive[part * EIGHT : (part + 1) * EIGHT])
            tail[at, cols] = jnp.concatenate(tails, 0).astype(BF16)
        return carry

    lax.fori_loop(0, rows // STRIP, steps, 0, unroll=2)

    spread = jnp.concatenate([b_rows] * chunks, 0)
    own = iota(spread.shape, 0) // state == iota(spread.shape, 1) // EIGHT
    chunk_state[...] = dot_high(split(jnp.where(own, spread, 0.0)), tail[...])
    products = []
    for tile in range(width // LANES):
        cols = pl.ds(tile * LANES, LANES)
        total = jnp.zeros((state, LANES), F32)
        product = jnp.ones((1, LANES), F32)
        for chunk in range(chunks):
            kept = chunk_keep[chunk : chunk + 1, cols]
            total = total * kept + chunk_state[chunk * state : (chunk + 1) * state, cols]
            product = product * kept
        ends[:, cols] = total.astype(BF16)
        products.append(product)
    ends[:, width:] = jnp.concatenate(products, 0).astype(BF16)


def pair_kernel(place, after, own, other, ends):
    width = own.shape[1] - LANES
    first = lax.rem(place[0], 2) == 0
    mine = own[...].astype(F32)
    its = other[...].astype(F32)
    earlier = jnp.where(first, mine, its)
    later = jnp.where(first, its, mine)
    fade = later[:, width:]
    for tile in range(width // LANES):
        cols = slice(tile * LANES, (tile + 1) * LANES)
        ends[:, cols] = (earlier[:, cols] * fade[tile : tile + 1] + later[:, cols]).astype(BF16)
    ends[:, width:] = (earlier[:, width:] * fade).astype(BF16)


def couple_kernel(bc, bct, coef):
    rows = bc.shape[0]
    state = bct.shape[0] // 2
    coupling = dot_split(split(bc[:, state:]), split(bct[:state]))
    row, lane = iota((rows, rows), 0), iota((rows, rows), 1)
    total = jnp.zeros((rows, rows), F32)
    for back in range(EIGHT):
        diagonal = jnp.sum(jnp.where(lane == row - back, coupling, 0.0), 1, keepdims=True)
        total = total + jnp.where((lane == back) & (row % EIGHT >= back), diagonal, 0.0)
    coef[...] = total


def within_kernel(coef, base, keep, drive, second, faded):
    rows, width = base.shape
    edge = iota((EIGHT, width), 0)

    def chunk(index, carry):
        at = pl.ds(pl.multiple_of(index * EIGHT, EIGHT), EIGHT)
        kept = keep[at, :]
        factors = coef[at, :]
        moved = drive[at, :]
        total = base[at, :] + factors[:, 0:1] * moved
        for back in range(1, EIGHT):
            moved = kept * pltpu.roll(moved, 1, 0)
            total = total + factors[:, back : back + 1] * moved
        second[at, :] = total
        for hop in (1, 2, 4):
            kept = kept * jnp.where(edge >= hop, pltpu.roll(kept, hop, 0), 1.0)
        faded[at, :] = kept
        return carry

    lax.fori_loop(0, rows // EIGHT, chunk, 0, unroll=2)


def route_kernel(
    place, before, faded, chunk_state, chunk_keep, bc, gains, router_t, routes_t, beside, *refs
):
    ends, (second, weighting), packed = refs[:-10], refs[-10:-8], refs[-8:-4]
    states, carried, expert_in, stack = refs[-4:]
    rows, width = before.shape
    chunks = chunk_keep.shape[0]
    state = chunk_state.shape[0] // chunks
    me = place[0]
    own = place[2]
    chip = me // 2
    stack[0] = jnp.zeros_like(beside)
    for slot, end in enumerate(ends, 1):
        stack[slot] = end[...]
    fades = [stack[chip ^ at, :, width:].astype(F32) for at in range(len(ends))]
    last_fade = beside[:, width:].astype(F32)
    second_core = lax.rem(me, 2) == 1
    for tile in range(width // LANES):
        cols = pl.ds(tile * LANES, LANES)
        total = jnp.zeros((state, LANES), F32)
        for at, fade in enumerate(fades):
            joined = total * fade[tile : tile + 1] + stack[chip ^ at, :, cols].astype(F32)
            total = jnp.where(at < chip, joined, total)
        joined = total * last_fade[tile : tile + 1] + beside[:, cols].astype(F32)
        total = jnp.where(second_core, joined, total)
        for chunk in range(chunks):
            at = pl.ds(chunk * state, state)
            states[at, cols] = total.astype(BF16)
            total = total * chunk_keep[chunk : chunk + 1, cols] + chunk_state[at, cols]
    wide = chunks * state
    repeat = (iota((state, wide), 1) % state == iota((state, wide), 0)).astype(BF16)
    here = iota((rows, wide), 1) // state == iota((rows, wide), 0) // EIGHT
    spread = [
        jnp.where(here, dot(part, repeat), 0.0).astype(BF16) for part in split(bc[:, state:])
    ]
    carried[...] = dot_high(spread, states[...])

    def normalize(at):
        values = before[at, :] + carried[at, :] * faded[at, :]
        second[at, :] = values
        expert_in[at, :] = rms_norm(values, gains[2]).astype(BF16)

    strips(rows, normalize)

    expert = iota((EXPERTS, rows), 0)
    uses = (routes_t[0:1, :] == expert) | (routes_t[1:2, :] == expert)
    logits = jnp.where(uses, dot(router_t[...], expert_in[...], ((1,), (1,))), -1e30)
    gates = jnp.where(uses, jnp.exp(logits - jnp.max(logits, 0, keepdims=True)), 0.0)
    gates = gates / jnp.sum(gates, 0, keepdims=True)
    sooner = (iota((rows, rows), 0) < iota((rows, rows), 1)).astype(BF16)
    ranks = dot(jnp.where(uses, 1.0, 0.0).astype(BF16), sooner)
    ranks = jnp.where(uses, ranks, -1.0).astype(jnp.int32)
    capacity = packed[0].shape[0]
    place_row = iota((capacity, rows), 0)
    weights, placings = [], []
    for slot in range(EXPERTS):
        mine = expert == (own ^ slot)
        rank = jnp.sum(jnp.where(mine, ranks, 0), 0, keepdims=True)
        gate = jnp.sum(jnp.where(mine, gates, 0.0), 0, keepdims=True)
        placing = place_row == rank
        weights.append(jnp.where(placing, gate, 0.0))
        placings.append(placing.astype(BF16))
    chosen = dot(jnp.concatenate(placings, 0), expert_in[...]).astype(BF16)
    for slot in range(EXPERTS):
        packed[slot][...] = chosen[slot * capacity : (slot + 1) * capacity]
    weighting[...] = jnp.concatenate(weights, 0).T


def fetch_kernel(pieces, starts, *refs):
    count = len(pieces)
    sources, outs, sems = refs[:count], refs[-count - 1 : -1], refs[-1]
    copies = []
    for source, out, number, start in zip(sources, outs, pieces, starts):
        rows = out.shape[0] // number
        for piece in range(number):
            begin, end = source, out
            if number > 1:
                at = pl.ds(piece * rows, rows)
                begin, end = source.at[at, pl.ds(start, out.shape[1])], out.at[at]
            copies.append(pltpu.make_async_copy(begin, end, sems.at[len(copies)]))
    for copy in copies:
        copy.start()
    for copy in copies:
        copy.wait()


def fetch(items, after, hurry=False):
    arrays, pieces, starts, widths = zip(*items)
    return pl.pallas_call(
        functools.partial(fetch_kernel, pieces, starts),
        out_shape=tuple(
            shape(array.shape[:-1] + (width,), array.dtype)
            for array, width in zip(arrays, widths)
        ),
        in_specs=[ANY] * (len(arrays) + 1),
        out_specs=(VMEM,) * len(arrays),
        scratch_shapes=[pltpu.SemaphoreType.DMA((sum(pieces),))],
        compiler_params=params(4),
        cost_estimate=cost(0, 0 if hurry else sum(array.size * 4 for array in arrays)),
        name="fetch",
    )(*[in_hbm(array) for array in arrays], after)


def gather_kernel(after, *refs):
    blocks, out = refs[:-1], refs[-1]
    capacity = blocks[0].shape[0]
    for at, block in enumerate(blocks):
        out[at * capacity : (at + 1) * capacity, :] = block[...]


def up_kernel(w_up, after, *refs):
    blocks, hidden = refs[:-1], refs[-1]
    tokens = jnp.concatenate([block[...] for block in blocks], 0)
    tile = 256 if hidden.shape[1] % 256 == 0 else LANES
    for low in range(0, hidden.shape[1], tile):
        cols = slice(low, low + tile)
        raised = dot(tokens, w_up[:, cols])
        hidden[:, cols] = (raised * jax.nn.sigmoid(raised)).astype(BF16)


def down_kernel(weights, hidden, after, *refs):
    w_downs, outs = refs[:weights], refs[weights:]
    rows = outs[0].shape[0]
    tile = 256
    begin = 0
    for w_down in w_downs:
        for low in range(0, w_down.shape[1], tile):
            high = min(low + tile, w_down.shape[1])
            result = dot(hidden[...], w_down[:, low:high]).astype(BF16)
            for at, out in enumerate(outs):
                out[:, begin + low : begin + high] = result[at * rows : (at + 1) * rows]
        begin += w_down.shape[1]


def join_kernel(start, outs_count, after, own, *refs):
    parts, outs = refs[:-outs_count], refs[-outs_count:]
    capacity, width = outs[0].shape
    for at, out in enumerate(outs):
        here = slice(at * capacity, (at + 1) * capacity)
        total = own[here, :].astype(F32)
        for part in parts:
            total = total + part[here, start : start + width].astype(F32)
        out[...] = total.astype(BF16)


def finish_kernel(start, second, weighting, *refs):
    blocks, last, parts, out = refs[: EXPERTS - 2], refs[EXPERTS - 2], refs[EXPERTS - 1 : -1], refs[-1]
    cols = slice(start, start + out.shape[1])
    total = parts[0][:, cols].astype(F32)
    for part in parts[1:]:
        total = total + part[:, cols].astype(F32)
    rows = [total.astype(BF16)] + [block[...] for block in blocks] + [last[:, cols]]
    rows = jnp.concatenate(rows, 0)
    high, low = split(weighting[...])
    out[...] = (second[:, cols] + (dot(high, rows) + dot(low, rows))).astype(BF16)


def exchange(value, axis, mask):
    count = lax.axis_size(axis)
    return lax.ppermute(value, axis, [(at, at ^ mask) for at in range(count)])


def shifted(value, axis, steps):
    count = lax.axis_size(axis)
    return lax.ppermute(value, axis, [(at, (at + steps) % count) for at in range(count)])


def head_weights(w_kv, shard_count, shard_index):
    if w_kv.shape[1] == HD and shard_count == 2 * KVH:
        return w_kv, exchange(w_kv, "ctx", KVH), shard_index // KVH
    whole = lax.all_gather(w_kv, "ctx", axis=1, tiled=True)
    head = shard_index % KVH
    return (
        lax.dynamic_slice_in_dim(whole, head * HD, HD, 1),
        lax.dynamic_slice_in_dim(whole, (KVH + head) * HD, HD, 1),
        jnp.zeros_like(shard_index),
    )


def on_device(
    acts,
    norm_gains,
    w_kv,
    dt_in,
    dt_out,
    dt_bias,
    decay_rate,
    w_bc,
    skip_gain,
    w_router,
    routes,
    w_up,
    w_down,
):
    shard_count = lax.axis_size("ctx")
    me = lax.axis_index("ctx")
    tokens = acts[0]
    rows, width = tokens.shape
    gains = norm_gains.transpose(1, 0, 2)
    parts = shard_count // EXPERTS
    group_rows = KVH * rows
    state = w_bc.shape[2] // 2
    chunks = rows // EIGHT
    capacity = rows * routes.shape[2] // EXPERTS

    near_tokens = exchange(tokens, "ctx", 2)
    w_own, w_other, key_at = head_weights(w_kv[0], shard_count, me)
    beside = exchange(tokens, "ctx", 1)
    place = jnp.stack([me, key_at, me // parts]).astype(jnp.int32)

    def norm(gains, blocks, after):
        return pl.pallas_call(
            norm_kernel,
            out_shape=(shape((rows, width), BF16),) * len(blocks),
            in_specs=[VMEM, ANY] + [VMEM] * len(blocks),
            out_specs=(VMEM,) * len(blocks),
            compiler_params=params(6),
            cost_estimate=cost(8 * rows * width, 4 * rows * width),
            name="norm",
        )(gains, after, *blocks)

    normed = list(norm(in_hbm(gains), [in_hbm(tokens), beside], place))
    cuts = [width * cut // 16 for cut in CUTS]
    spans = [high - low for low, high in zip(cuts, cuts[1:])]
    here = [gains, w_own, tokens, dt_in[0], dt_out[0], w_bc[0].T]
    here += [skip_gain, dt_bias, decay_rate, w_router[0].T, routes[0].T]
    here = [(array, 1, 0, array.shape[-1]) for array in here]
    here = [(w_up[0], 16, 0, w_up.shape[2]), (w_down[0], 16, 0, spans[0])] + here
    raising, *here = fetch(here, normed[1])
    lowering, gains, w_own, tokens, dt_first, dt_second, w_bct = here[:7]
    lowering = [lowering]
    skip_gain, dt_bias, decay_rate, router_t, routes_t = here[7:]
    normed += norm(gains, [near_tokens], raising)
    normed.append(exchange(normed[2], "ctx", 1))
    projected = (shape((2, GROUP * rows, HD), BF16), shape((2, 2 * rows, HD), BF16))
    first_q, first_kv, weights = pl.pallas_call(
        project_kernel,
        out_shape=projected + (shape((width, 2 * HD), BF16),),
        in_specs=[SMEM] + [VMEM] * 4,
        out_specs=(VMEM,) * 3,
        compiler_params=params(8),
        cost_estimate=cost(8 * rows * width * HD, 16 * rows * width),
        name="project",
    )(place, w_own, w_other, *normed[:2])
    last_q, last_kv = pl.pallas_call(
        project_more_kernel,
        out_shape=projected,
        in_specs=[SMEM] + [VMEM] * 3,
        out_specs=(VMEM,) * 2,
        compiler_params=params(8),
        cost_estimate=cost(8 * rows * width * HD, 16 * rows * width),
        name="project_more",
    )(place, weights, *normed[2:])
    queries, kv = (first_q, last_q), (first_kv, last_kv)
    turns = shard_count // KVH
    pasts = [
        [exchange(half, "ctx", turn * KVH) for half in kv] for turn in range(1, turns)
    ]
    scored = GROUP * rows * group_rows * KVH
    tallies = (shape((KVH, GROUP * rows, LANES), F32),) * 2 + (
        shape((KVH, GROUP * rows, HD), F32),
    )
    tally = pl.pallas_call(
        near_kernel,
        out_shape=tallies,
        in_specs=[SMEM] + [VMEM] * 4,
        out_specs=(VMEM,) * 3,
        compiler_params=params(16),
        cost_estimate=cost(4 * scored * HD, 4 * group_rows * GROUP * HD * 4, scored),
        name="near",
    )(place, *queries, *kv)
    attended = [None] * KVH
    for slots in ((2, 3), (0, 1)):
        state_now = tally
        steps = []
        for turn, past in enumerate(pasts, 1):
            steps += [(turn, [half]) for half in past]
        for step, (turn, past) in enumerate(steps, 1):
            last = step == len(steps)
            state_now = pl.pallas_call(
                functools.partial(far_kernel, turn, slots, last, len(past)),
                out_shape=(shape((rows, GROUP * HD), BF16),) * len(slots) if last else tallies,
                in_specs=[SMEM] + [VMEM] * (5 + len(past)),
                out_specs=(VMEM,) * (len(slots) if last else 3),
                compiler_params=params(16),
                cost_estimate=cost(
                    scored * HD * len(past), group_rows * GROUP * HD * 8, scored // 4 * len(past)
                ),
                name="far",
            )(place, *queries, *state_now, *past)
        for slot, block in zip(slots, state_now):
            attended[slot] = exchange(block, "ctx", slot) if slot else block

    base, keep, drive, chunk_state, chunk_keep, bc, bct, ends = pl.pallas_call(
        prepare_kernel,
        out_shape=(
            shape((rows, width), F32),
            shape((rows, width), F32),
            shape((rows, width), F32),
            shape((chunks * state, width), F32),
            shape((chunks, width), F32),
            shape((rows, 2 * state), F32),
            shape((2 * state, rows), F32),
            shape((state, width + LANES), BF16),
        ),
        in_specs=[SMEM] + [VMEM] * (8 + KVH),
        out_specs=(VMEM,) * 8,
        scratch_shapes=[
            pltpu.VMEM((rows, width), BF16),
            pltpu.VMEM((rows, width), F32),
            pltpu.VMEM((rows, width), BF16),
        ],
        compiler_params=params(20),
        cost_estimate=cost(10 * rows * width * 256, 30 * rows * width, 3 * rows * width),
        name="prepare",
    )(
        place,
        tokens,
        gains,
        skip_gain,
        dt_first,
        dt_second,
        dt_bias,
        decay_rate,
        w_bct,
        *attended,
    )
    beside_ends = exchange(ends, "ctx", 1)
    coef = pl.pallas_call(
        couple_kernel,
        out_shape=shape((rows, rows), F32),
        in_specs=[VMEM, VMEM],
        out_specs=VMEM,
        compiler_params=params(4),
        cost_estimate=cost(20 * rows * rows, 20 * rows * rows),
        name="couple",
    )(bc, bct)
    chip_ends = pl.pallas_call(
        pair_kernel,
        out_shape=shape(ends.shape, BF16),
        in_specs=[SMEM, ANY, VMEM, VMEM],
        out_specs=VMEM,
        compiler_params=params(8),
        cost_estimate=cost(4 * ends.size, 8 * ends.size),
        name="pair",
    )(place, coef, ends, beside_ends)
    earlier_ends = [exchange(chip_ends, "ctx", mask) for mask in range(2, shard_count, 2)]
    before, faded = pl.pallas_call(
        within_kernel,
        out_shape=(shape((rows, width), F32), shape((rows, width), F32)),
        in_specs=[VMEM] * 4,
        out_specs=(VMEM, VMEM),
        compiler_params=params(12),
        cost_estimate=cost(40 * rows * width, 20 * rows * width),
        name="within",
    )(coef, base, keep, drive)
    second, weighting, *packed = pl.pallas_call(
        route_kernel,
        out_shape=(shape((rows, width), F32), shape((rows, EXPERTS * capacity), F32))
        + (shape((capacity, width), BF16),) * EXPERTS,
        in_specs=[SMEM] + [VMEM] * (9 + len(earlier_ends)),
        out_specs=(VMEM,) * (2 + EXPERTS),
        scratch_shapes=[
            pltpu.VMEM((chunks * state, width), BF16),
            pltpu.VMEM((rows, width), F32),
            pltpu.VMEM((rows, width), BF16),
            pltpu.VMEM((shard_count // 2, state, width + LANES), BF16),
        ],
        compiler_params=params(16),
        cost_estimate=cost(10 * rows * width * 256, 30 * rows * width),
        name="route",
    )(
        place,
        before,
        faded,
        chunk_state,
        chunk_keep,
        bc,
        gains,
        router_t,
        routes_t,
        beside_ends,
        *earlier_ends,
    )

    units = raising.shape[1]

    def lift(blocks, after, hurry=False):
        count = sum(block.shape[0] for block in blocks)
        work = 1 if hurry else units
        return pl.pallas_call(
            up_kernel,
            out_shape=shape((count, units), BF16),
            in_specs=[VMEM, ANY] + [VMEM] * len(blocks),
            out_specs=VMEM,
            compiler_params=params(12),
            cost_estimate=cost(2 * count * width * work, 2 * width * work),
            name="up",
        )(raising, after, *blocks)

    def lower(weights, hidden, after, outs=1, hurry=False):
        count, span = hidden.shape[0], sum(weight.shape[1] for weight in weights)
        work = 1 if hurry else units
        return pl.pallas_call(
            functools.partial(down_kernel, len(weights)),
            out_shape=(shape((count // outs, span), BF16),) * outs,
            in_specs=[VMEM, ANY] + [VMEM] * len(weights),
            out_specs=(VMEM,) * outs,
            compiler_params=params(12),
            cost_estimate=cost(2 * count * span * work, 2 * span * work),
            name="down",
        )(hidden, after, *weights)

    def shared(blocks):
        return [blocks[0]] + [
            exchange(blocks[turn], "ctx", turn) for turn in range(1, parts)
        ]

    def join(start, span, sums, outs, after):
        return pl.pallas_call(
            functools.partial(join_kernel, start, outs),
            out_shape=(shape((capacity, span), BF16),) * outs,
            in_specs=[ANY] + [VMEM] * parts,
            out_specs=(VMEM,) * outs,
            compiler_params=params(8),
            cost_estimate=cost(4 * outs * capacity * span, 8 * outs * capacity * span),
            name="join",
        )(after, *sums)

    across = exchange(packed[3], "ctx", 3 * parts)
    stay_hidden = lift(shared([packed[0]] * parts), packed[0])
    lowering += fetch([(w_down[0], 16, cuts[1], spans[1])], stay_hidden, hurry=True)
    stay_out = lower(lowering, stay_hidden, packed[0], parts)
    stay_sums = shared(stay_out)

    across_hidden = lift(shared([across] * parts), stay_sums[-1], True)
    across_out = lower(lowering, across_hidden, packed[0], parts, True)
    (across,) = join(0, width, shared(across_out), 1, across_hidden)
    across_back = exchange(across, "ctx", 3 * parts)

    near_slots = (1, 2)
    near_rows = len(near_slots) * capacity
    arrived = pl.pallas_call(
        gather_kernel,
        out_shape=shape((near_rows, width), BF16),
        in_specs=[ANY] + [VMEM] * len(near_slots),
        out_specs=VMEM,
        compiler_params=params(4),
        cost_estimate=cost(0, 4 * near_rows * width),
        name="gather",
    )(across_out[0], *[exchange(packed[slot], "ctx", slot * parts) for slot in near_slots])
    hiddens = []
    after = across
    for block in shared([arrived] * parts):
        after = lift([block], after, True)
        hiddens.append(after)
    others = []
    after = across_back
    for turn in range(1, parts):
        (after,) = lower(lowering, hiddens[turn], after, hurry=True)
        others.append(exchange(after, "ctx", turn))
    results = []
    ready = hiddens[0]
    for chunk, span in enumerate(spans):
        (own,) = lower(lowering[chunk : chunk + 1], hiddens[0], after, hurry=True)
        joined = join(cuts[chunk], span, [own] + others, len(near_slots), ready)
        after = joined[0]
        returned = [
            exchange(block, "ctx", slot * parts) for slot, block in zip(near_slots, joined)
        ]
        finished = pl.pallas_call(
            functools.partial(finish_kernel, cuts[chunk]),
            out_shape=shape((rows, span), BF16),
            in_specs=[VMEM] * (1 + EXPERTS + parts),
            out_specs=VMEM,
            compiler_params=params(8),
            cost_estimate=cost(
                4 * rows * EXPERTS * capacity * span, 10 * rows * span
            ),
            name="finish",
        )(second, weighting, *returned, across_back, *stay_sums)
        results.append(shifted(finished, "segment", 1))
    return jnp.concatenate(results, 1)[None]


def solution(mesh):
    in_specs = (
        P("segment", "ctx", None),
        P("segment", None, None),
        P("segment", None, "ctx"),
        P("segment", None, None),
        P("segment", None, None),
        P("segment", None),
        P("segment", None),
        P("segment", None, None),
        P("segment", None),
        P("segment", None, None),
        P("segment", "ctx", None),
        P("segment", None, "ctx"),
        P("segment", "ctx", None),
    )
    out_specs = P("segment", "ctx", None)
    return jax.shard_map(
        on_device, mesh=mesh, in_specs=in_specs, out_specs=out_specs, check_vma=False
    )
```

```python
import functools
import math

import jax
import jax.numpy as jnp
from jax import lax
from jax.experimental import pallas as pl
from jax.experimental.pallas import tpu as pltpu
from jax.sharding import PartitionSpec as P

HEADS = 16
KVH = 4
HD = 128
GROUP = HEADS // KVH
EXPERTS = 4
EIGHT = 8
STRIP = 16
LANES = 128
SCALE = HD ** (-0.5) * math.log2(math.e)
SENT = (3, 1, 2)
BACK = ((1, 3, 2), (3, 1, 2))
CHUNKS = 2
F32 = jnp.float32
BF16 = jnp.bfloat16
VMEM = pl.BlockSpec(memory_space=pltpu.VMEM)
ANY = pl.BlockSpec(memory_space=pl.ANY)
SMEM = pl.BlockSpec(memory_space=pltpu.SMEM)


def params(mib):
    return pltpu.CompilerParams(vmem_limit_bytes=mib * 2**20)


def cost(flops, moved, transcendentals=0):
    return pl.CostEstimate(
        flops=int(flops), bytes_accessed=int(moved), transcendentals=int(transcendentals)
    )


def shape(dims, dtype):
    return jax.ShapeDtypeStruct(tuple(dims), dtype)


def in_hbm(array):
    return pltpu.with_memory_space_constraint(array, pltpu.HBM)


def rms_norm(values, gain):
    return values * lax.rsqrt(jnp.mean(values * values, -1, keepdims=True) + 1e-06) * gain


def strips(rows, body):
    def step(index, carry):
        body(pl.ds(pl.multiple_of(index * STRIP, STRIP), STRIP))
        return carry

    lax.fori_loop(0, rows // STRIP, step, 0, unroll=4)


def split(values):
    high = values.astype(BF16)
    return high, (values - high.astype(F32)).astype(BF16)


def dot(a, b, dims=((1,), (0,))):
    return lax.dot_general(a, b, (dims, ((), ())), preferred_element_type=F32)


def dot_high(a, b):
    count = a[0].shape[0]
    both = dot(jnp.concatenate(a, 0), b)
    return both[:count] + both[count:]


def dot_split(a, b, dims=((1,), (0,))):
    a_high, a_low = a
    b_high, b_low = b
    count = a_high.shape[0]
    both = dot(jnp.concatenate([a_high, a_low], 0), b_high, dims)
    return both[:count] + (both[count:] + dot(a_high, b_low, dims))


def iota(dims, axis):
    return lax.broadcasted_iota(jnp.int32, dims, axis)


def norm_into(out, x, gain):
    def body(at):
        out[at, :] = rms_norm(x[at, :].astype(F32), gain).astype(BF16)

    strips(x.shape[0], body)


def norm_kernel(gains, after, *refs):
    count = len(refs) // 2
    for x, out in zip(refs[:count], refs[count:]):
        norm_into(out, x, gains[0])


def project(head, weights, first, second, q_out, kv_out):
    rows = first.shape[0]
    normed = jnp.concatenate([first[...], second[...]], 0)
    both = dot(normed, weights[...]).astype(BF16)
    kv_out[0] = both[:, :HD]
    kv_out[1] = both[:, HD:]
    for slot, shard in enumerate((first, second)):
        for part in range(GROUP):
            cols = pl.ds(pl.multiple_of((head * GROUP + part) * HD, HD), HD)
            q_out[slot, pl.ds(part * rows, rows), :] = shard[:, cols]


def project_kernel(place, w_own, w_other, first, second, q_out, kv_out, weights):
    key_at = place[1]
    weights[:, pl.ds(pl.multiple_of(key_at * HD, HD), HD)] = w_own[...]
    weights[:, pl.ds(pl.multiple_of((1 - key_at) * HD, HD), HD)] = w_other[...]
    project(place[0] % KVH, weights, first, second, q_out, kv_out)


def project_more_kernel(place, weights, first, second, q_out, kv_out):
    project(place[0] % KVH, weights, first, second, q_out, kv_out)


def joined_keys(halves, which):
    return jnp.concatenate([half[which] for half in halves], 0)


def near_kernel(place, *refs):
    queries, halves, (largest_out, total_out, summed) = refs[:2], refs[2:4], refs[4:]
    me = place[0]
    keys, values = joined_keys(halves, 0), joined_keys(halves, 1)
    count = keys.shape[0]
    rows = count // KVH
    lane = iota((rows, count), 1)
    key_shard = me ^ (lane // rows)
    later = lane % rows > iota((rows, count), 0)
    for slot in range(KVH):
        shard = me ^ slot
        hidden = (key_shard > shard) | ((key_shard == shard) & later)
        scores = dot(queries[slot // 2][slot % 2], keys, ((1,), (1,)))
        scores = scores.reshape(GROUP, rows, count)
        scores = jnp.where(hidden[None], -1e30, scores).reshape(GROUP * rows, count)
        largest = jnp.max(scores, -1, keepdims=True)
        weights = jnp.exp2(scores * SCALE - largest * SCALE)
        total = jnp.sum(weights, -1, keepdims=True)
        summed[slot] = dot(weights.astype(BF16), values)
        largest_out[slot] = jnp.broadcast_to(largest, (GROUP * rows, LANES))
        total_out[slot] = jnp.broadcast_to(total, (GROUP * rows, LANES))


def far_kernel(turn, slots, last, place, *refs):
    queries, (largest, total, summed), halves, outs = refs[:2], refs[2:5], refs[5:7], refs[7:]
    rows = queries[0].shape[1] // GROUP
    mine = place[0] // KVH
    seen = (mine ^ turn) < mine

    def keep(at, top, weight, value):
        if last:
            result = (value / weight).astype(BF16)
            for part in range(GROUP):
                cols = slice(part * HD, (part + 1) * HD)
                outs[at][:, cols] = result[part * rows : (part + 1) * rows]
        else:
            outs[0][slots[at]] = top
            outs[1][slots[at]] = weight
            outs[2][slots[at]] = value

    @pl.when(seen)
    def _():
        keys, values = joined_keys(halves, 0), joined_keys(halves, 1)
        wide = keys.shape[0] // LANES
        for at, slot in enumerate(slots):
            scores = dot(queries[slot // 2][slot % 2], keys, ((1,), (1,)))
            top = jnp.broadcast_to(jnp.max(scores, -1, keepdims=True), (GROUP * rows, LANES))
            newest = jnp.maximum(largest[slot], top)
            offset = newest * SCALE
            weights = jnp.exp2(scores * SCALE - jnp.concatenate([offset] * wide, 1))
            fade = jnp.exp2(largest[slot] * SCALE - offset)
            weight = jnp.broadcast_to(jnp.sum(weights, -1, keepdims=True), (GROUP * rows, LANES))
            value = summed[slot] * fade + dot(weights.astype(BF16), values)
            keep(at, newest, total[slot] * fade + weight, value)

    @pl.when(jnp.logical_not(seen))
    def _():
        for at, slot in enumerate(slots):
            keep(at, largest[slot], total[slot], summed[slot])


def prepare_kernel(
    place, x, gains, skip, dt_in, dt_out, bias, rate, w_bct, *refs
):
    attended = refs[:KVH]
    base, keep_out, drive_out, chunk_state, chunk_keep, bc_out, bct_out, ends = refs[KVH:-3]
    mixed, pre, tail = refs[-3:]
    rows, width = x.shape
    state = w_bct.shape[0] // 2
    chunks = rows // EIGHT
    head = place[0] % KVH
    span = GROUP * HD
    for slot in range(KVH):
        cols = pl.ds(pl.multiple_of((head ^ slot) * span, span), span)
        base[:, cols] = x[:, cols].astype(F32) + attended[slot][...].astype(F32)

    def normalize(at):
        first = base[at, :]
        mixed_in = rms_norm(first, gains[1]).astype(BF16)
        mixed[at, :] = mixed_in
        base[at, :] = first + skip[...] * mixed_in.astype(F32)

    strips(rows, normalize)
    low_rank = dot(mixed[...], dt_in[...]).astype(BF16)
    pre[...] = dot(low_rank, dt_out[...])
    bct = dot(w_bct[...], mixed[...], ((1,), (1,)))
    bc = bct.T
    bc_out[...] = bc
    bct_out[...] = bct
    b_rows = bct[:state]
    block = width // 4
    edge = iota((EIGHT, block), 0)

    def steps(index, carry):
        at = pl.ds(pl.multiple_of(index * STRIP, STRIP), STRIP)
        for low in range(0, width, block):
            cols = pl.ds(low, block)
            raw = pre[at, cols] + bias[:, cols]
            step_size = jnp.maximum(raw, 0.0) + jnp.log(1.0 + jnp.exp(-jnp.abs(raw)))
            keep = jnp.exp(-step_size * rate[:, cols])
            drive = step_size * mixed[at, cols].astype(F32)
            keep_out[at, cols] = keep
            drive_out[at, cols] = drive
            tails = []
            for part in range(STRIP // EIGHT):
                kept = keep[part * EIGHT : (part + 1) * EIGHT]
                after = jnp.where(edge < EIGHT - 1, pltpu.roll(kept, EIGHT - 1, 0), 1.0)
                for hop in (1, 2, 4):
                    after = after * jnp.where(
                        edge < EIGHT - hop, pltpu.roll(after, EIGHT - hop, 0), 1.0
                    )
                whole = after[0:1] * kept[0:1]
                chunk_keep[pl.ds(index * (STRIP // EIGHT) + part, 1), cols] = whole
                tails.append(after * drive[part * EIGHT : (part + 1) * EIGHT])
            tail[at, cols] = jnp.concatenate(tails, 0).astype(BF16)
        return carry

    lax.fori_loop(0, rows // STRIP, steps, 0, unroll=2)

    spread = jnp.concatenate([b_rows] * chunks, 0)
    own = iota(spread.shape, 0) // state == iota(spread.shape, 1) // EIGHT
    chunk_state[...] = dot_high(split(jnp.where(own, spread, 0.0)), tail[...])
    products = []
    for tile in range(width // LANES):
        cols = pl.ds(tile * LANES, LANES)
        total = jnp.zeros((state, LANES), F32)
        product = jnp.ones((1, LANES), F32)
        for chunk in range(chunks):
            kept = chunk_keep[chunk : chunk + 1, cols]
            total = total * kept + chunk_state[chunk * state : (chunk + 1) * state, cols]
            product = product * kept
        ends[:, cols] = total.astype(BF16)
        products.append(product)
    ends[:, width:] = jnp.concatenate(products, 0).astype(BF16)


def pair_kernel(place, after, own, other, ends):
    width = own.shape[1] - LANES
    first = lax.rem(place[0], 2) == 0
    mine = own[...].astype(F32)
    its = other[...].astype(F32)
    earlier = jnp.where(first, mine, its)
    later = jnp.where(first, its, mine)
    fade = later[:, width:]
    for tile in range(width // LANES):
        cols = slice(tile * LANES, (tile + 1) * LANES)
        ends[:, cols] = (earlier[:, cols] * fade[tile : tile + 1] + later[:, cols]).astype(BF16)
    ends[:, width:] = (earlier[:, width:] * fade).astype(BF16)


def couple_kernel(bc, bct, coef):
    rows = bc.shape[0]
    state = bct.shape[0] // 2
    coupling = dot_split(split(bc[:, state:]), split(bct[:state]))
    row, lane = iota((rows, rows), 0), iota((rows, rows), 1)
    total = jnp.zeros((rows, rows), F32)
    for back in range(EIGHT):
        diagonal = jnp.sum(jnp.where(lane == row - back, coupling, 0.0), 1, keepdims=True)
        total = total + jnp.where((lane == back) & (row % EIGHT >= back), diagonal, 0.0)
    coef[...] = total


def within_kernel(coef, base, keep, drive, second, faded):
    rows, width = base.shape
    edge = iota((EIGHT, width), 0)

    def chunk(index, carry):
        at = pl.ds(pl.multiple_of(index * EIGHT, EIGHT), EIGHT)
        kept = keep[at, :]
        factors = coef[at, :]
        moved = drive[at, :]
        total = base[at, :] + factors[:, 0:1] * moved
        for back in range(1, EIGHT):
            moved = kept * pltpu.roll(moved, 1, 0)
            total = total + factors[:, back : back + 1] * moved
        second[at, :] = total
        for hop in (1, 2, 4):
            kept = kept * jnp.where(edge >= hop, pltpu.roll(kept, hop, 0), 1.0)
        faded[at, :] = kept
        return carry

    lax.fori_loop(0, rows // EIGHT, chunk, 0, unroll=2)


def route_kernel(
    place, before, faded, chunk_state, chunk_keep, bc, gains, router_t, routes_t, beside, *refs
):
    ends, (second, weighting), packed = refs[:-10], refs[-10:-8], refs[-8:-4]
    states, carried, expert_in, stack = refs[-4:]
    rows, width = before.shape
    chunks = chunk_keep.shape[0]
    state = chunk_state.shape[0] // chunks
    me = place[0]
    own = place[2]
    chip = me // 2
    stack[0] = jnp.zeros_like(beside)
    for slot, end in enumerate(ends, 1):
        stack[slot] = end[...]
    fades = [stack[chip ^ at, :, width:].astype(F32) for at in range(len(ends))]
    last_fade = beside[:, width:].astype(F32)
    second_core = lax.rem(me, 2) == 1
    for tile in range(width // LANES):
        cols = pl.ds(tile * LANES, LANES)
        total = jnp.zeros((state, LANES), F32)
        for at, fade in enumerate(fades):
            joined = total * fade[tile : tile + 1] + stack[chip ^ at, :, cols].astype(F32)
            total = jnp.where(at < chip, joined, total)
        joined = total * last_fade[tile : tile + 1] + beside[:, cols].astype(F32)
        total = jnp.where(second_core, joined, total)
        for chunk in range(chunks):
            at = pl.ds(chunk * state, state)
            states[at, cols] = total.astype(BF16)
            total = total * chunk_keep[chunk : chunk + 1, cols] + chunk_state[at, cols]
    wide = chunks * state
    repeat = (iota((state, wide), 1) % state == iota((state, wide), 0)).astype(BF16)
    here = iota((rows, wide), 1) // state == iota((rows, wide), 0) // EIGHT
    spread = [
        jnp.where(here, dot(part, repeat), 0.0).astype(BF16) for part in split(bc[:, state:])
    ]
    carried[...] = dot_high(spread, states[...])

    def normalize(at):
        values = before[at, :] + carried[at, :] * faded[at, :]
        second[at, :] = values
        expert_in[at, :] = rms_norm(values, gains[2]).astype(BF16)

    strips(rows, normalize)

    expert = iota((EXPERTS, rows), 0)
    uses = (routes_t[0:1, :] == expert) | (routes_t[1:2, :] == expert)
    logits = jnp.where(uses, dot(router_t[...], expert_in[...], ((1,), (1,))), -1e30)
    gates = jnp.where(uses, jnp.exp(logits - jnp.max(logits, 0, keepdims=True)), 0.0)
    gates = gates / jnp.sum(gates, 0, keepdims=True)
    sooner = (iota((rows, rows), 0) < iota((rows, rows), 1)).astype(BF16)
    ranks = dot(jnp.where(uses, 1.0, 0.0).astype(BF16), sooner)
    ranks = jnp.where(uses, ranks, -1.0).astype(jnp.int32)
    capacity = packed[0].shape[0]
    place_row = iota((capacity, rows), 0)
    weights, placings = [], []
    for slot in range(EXPERTS):
        mine = expert == (own ^ slot)
        rank = jnp.sum(jnp.where(mine, ranks, 0), 0, keepdims=True)
        gate = jnp.sum(jnp.where(mine, gates, 0.0), 0, keepdims=True)
        placing = place_row == rank
        weights.append(jnp.where(placing, gate, 0.0))
        placings.append(placing.astype(BF16))
    chosen = dot(jnp.concatenate(placings, 0), expert_in[...]).astype(BF16)
    for slot in range(EXPERTS):
        packed[slot][...] = chosen[slot * capacity : (slot + 1) * capacity]
    weighting[...] = jnp.concatenate(weights, 0).T


def fetch_kernel(pieces, starts, *refs):
    count = len(pieces)
    sources, outs, sems = refs[:count], refs[-count - 1 : -1], refs[-1]
    copies = []
    for source, out, number, start in zip(sources, outs, pieces, starts):
        rows = out.shape[0] // number
        for piece in range(number):
            begin, end = source, out
            if number > 1:
                at = pl.ds(piece * rows, rows)
                begin, end = source.at[at, pl.ds(start, out.shape[1])], out.at[at]
            copies.append(pltpu.make_async_copy(begin, end, sems.at[len(copies)]))
    for copy in copies:
        copy.start()
    for copy in copies:
        copy.wait()


def fetch(items, after, hurry=False):
    arrays, pieces, starts, widths = zip(*items)
    return pl.pallas_call(
        functools.partial(fetch_kernel, pieces, starts),
        out_shape=tuple(
            shape(array.shape[:-1] + (width,), array.dtype)
            for array, width in zip(arrays, widths)
        ),
        in_specs=[ANY] * (len(arrays) + 1),
        out_specs=(VMEM,) * len(arrays),
        scratch_shapes=[pltpu.SemaphoreType.DMA((sum(pieces),))],
        compiler_params=params(4),
        cost_estimate=cost(0, 0 if hurry else sum(array.size * 4 for array in arrays)),
        name="fetch",
    )(*[in_hbm(array) for array in arrays], after)


def gather_kernel(order, after, *refs):
    blocks, out = refs[:-1], refs[-1]
    capacity = blocks[0].shape[0]
    for slot, block in zip(order, blocks):
        out[(slot - 1) * capacity : slot * capacity, :] = block[...]


def up_kernel(w_up, after, *refs):
    blocks, hidden = refs[:-1], refs[-1]
    tokens = jnp.concatenate([block[...] for block in blocks], 0)
    tile = 256 if hidden.shape[1] % 256 == 0 else LANES
    for low in range(0, hidden.shape[1], tile):
        cols = slice(low, low + tile)
        raised = dot(tokens, w_up[:, cols])
        hidden[:, cols] = (raised * jax.nn.sigmoid(raised)).astype(BF16)


def down_kernel(weights, hidden, after, *refs):
    w_downs, outs = refs[:weights], refs[weights:]
    rows = outs[0].shape[0]
    tile = 256
    begin = 0
    for w_down in w_downs:
        for low in range(0, w_down.shape[1], tile):
            result = dot(hidden[...], w_down[:, low : low + tile]).astype(BF16)
            for at, out in enumerate(outs):
                out[:, begin + low : begin + low + tile] = result[at * rows : (at + 1) * rows]
        begin += w_down.shape[1]


def join_kernel(start, own, *refs):
    parts, outs = refs[: 1 - EXPERTS], refs[1 - EXPERTS :]
    capacity, width = outs[0].shape
    for at, out in enumerate(outs):
        here = slice(at * capacity, (at + 1) * capacity)
        total = own[here, :].astype(F32)
        for part in parts:
            total = total + part[here, start : start + width].astype(F32)
        out[...] = total.astype(BF16)


def finish_kernel(start, order, second, weighting, *refs):
    blocks, parts, out = refs[: EXPERTS - 1], refs[EXPERTS - 1 : -1], refs[-1]
    cols = slice(start, start + out.shape[1])
    total = parts[0][:, cols].astype(F32)
    for part in parts[1:]:
        total = total + part[:, cols].astype(F32)
    blocks = [blocks[order.index(slot)][...] for slot in sorted(order)]
    rows = jnp.concatenate([total.astype(BF16)] + blocks, 0)
    high, low = split(weighting[...])
    out[...] = (second[:, cols] + (dot(high, rows) + dot(low, rows))).astype(BF16)


def exchange(value, axis, mask):
    count = lax.axis_size(axis)
    return lax.ppermute(value, axis, [(at, at ^ mask) for at in range(count)])


def shifted(value, axis, steps):
    count = lax.axis_size(axis)
    return lax.ppermute(value, axis, [(at, (at + steps) % count) for at in range(count)])


def head_weights(w_kv, shard_count, shard_index):
    if w_kv.shape[1] == HD and shard_count == 2 * KVH:
        return w_kv, exchange(w_kv, "ctx", KVH), shard_index // KVH
    whole = lax.all_gather(w_kv, "ctx", axis=1, tiled=True)
    head = shard_index % KVH
    return (
        lax.dynamic_slice_in_dim(whole, head * HD, HD, 1),
        lax.dynamic_slice_in_dim(whole, (KVH + head) * HD, HD, 1),
        jnp.zeros_like(shard_index),
    )


def on_device(
    acts,
    norm_gains,
    w_kv,
    dt_in,
    dt_out,
    dt_bias,
    decay_rate,
    w_bc,
    skip_gain,
    w_router,
    routes,
    w_up,
    w_down,
):
    shard_count = lax.axis_size("ctx")
    me = lax.axis_index("ctx")
    tokens = acts[0]
    rows, width = tokens.shape
    gains = norm_gains.transpose(1, 0, 2)
    parts = shard_count // EXPERTS
    group_rows = KVH * rows
    state = w_bc.shape[2] // 2
    chunks = rows // EIGHT
    capacity = rows * routes.shape[2] // EXPERTS

    near_tokens = exchange(tokens, "ctx", 2)
    w_own, w_other, key_at = head_weights(w_kv[0], shard_count, me)
    beside = exchange(tokens, "ctx", 1)
    place = jnp.stack([me, key_at, me // parts]).astype(jnp.int32)

    def norm(gains, blocks, after):
        return pl.pallas_call(
            norm_kernel,
            out_shape=(shape((rows, width), BF16),) * len(blocks),
            in_specs=[VMEM, ANY] + [VMEM] * len(blocks),
            out_specs=(VMEM,) * len(blocks),
            compiler_params=params(6),
            cost_estimate=cost(8 * rows * width, 4 * rows * width),
            name="norm",
        )(gains, after, *blocks)

    normed = list(norm(in_hbm(gains), [in_hbm(tokens), beside], place))
    half = width // CHUNKS
    here = [gains, w_own, tokens, dt_in[0], dt_out[0], w_bc[0].T]
    here += [skip_gain, dt_bias, decay_rate, w_router[0].T, routes[0].T]
    here = [(array, 1, 0, array.shape[-1]) for array in here]
    here = [(w_up[0], 16, 0, w_up.shape[2]), (w_down[0], 16, 0, half)] + here
    raising, *here = fetch(here, normed[1])
    lowering, gains, w_own, tokens, dt_first, dt_second, w_bct = here[:7]
    lowering = [lowering]
    skip_gain, dt_bias, decay_rate, router_t, routes_t = here[7:]
    normed += norm(gains, [near_tokens], raising)
    normed.append(exchange(normed[2], "ctx", 1))
    projected = (shape((2, GROUP * rows, HD), BF16), shape((2, 2 * rows, HD), BF16))
    first_q, first_kv, weights = pl.pallas_call(
        project_kernel,
        out_shape=projected + (shape((width, 2 * HD), BF16),),
        in_specs=[SMEM] + [VMEM] * 4,
        out_specs=(VMEM,) * 3,
        compiler_params=params(8),
        cost_estimate=cost(8 * rows * width * HD, 16 * rows * width),
        name="project",
    )(place, w_own, w_other, *normed[:2])
    last_q, last_kv = pl.pallas_call(
        project_more_kernel,
        out_shape=projected,
        in_specs=[SMEM] + [VMEM] * 3,
        out_specs=(VMEM,) * 2,
        compiler_params=params(8),
        cost_estimate=cost(8 * rows * width * HD, 16 * rows * width),
        name="project_more",
    )(place, weights, *normed[2:])
    queries, kv = (first_q, last_q), (first_kv, last_kv)
    turns = shard_count // KVH
    pasts = [
        [exchange(half, "ctx", turn * KVH) for half in kv] for turn in range(1, turns)
    ]
    scored = GROUP * rows * group_rows * KVH
    tallies = (shape((KVH, GROUP * rows, LANES), F32),) * 2 + (
        shape((KVH, GROUP * rows, HD), F32),
    )
    tally = pl.pallas_call(
        near_kernel,
        out_shape=tallies,
        in_specs=[SMEM] + [VMEM] * 4,
        out_specs=(VMEM,) * 3,
        compiler_params=params(16),
        cost_estimate=cost(4 * scored * HD, 4 * group_rows * GROUP * HD * 4, scored),
        name="near",
    )(place, *queries, *kv)
    attended = [None] * KVH
    for slots in ((2, 3), (0, 1)):
        state_now = tally
        for turn, past in enumerate(pasts, 1):
            last = turn == turns - 1
            state_now = pl.pallas_call(
                functools.partial(far_kernel, turn, slots, last),
                out_shape=(shape((rows, GROUP * HD), BF16),) * len(slots) if last else tallies,
                in_specs=[SMEM] + [VMEM] * 7,
                out_specs=(VMEM,) * (len(slots) if last else 3),
                compiler_params=params(16),
                cost_estimate=cost(2 * scored * HD, 2 * group_rows * GROUP * HD * 4, scored // 2),
                name="far",
            )(place, *queries, *state_now, *past)
        for slot, block in zip(slots, state_now):
            attended[slot] = exchange(block, "ctx", slot) if slot else block

    base, keep, drive, chunk_state, chunk_keep, bc, bct, ends = pl.pallas_call(
        prepare_kernel,
        out_shape=(
            shape((rows, width), F32),
            shape((rows, width), F32),
            shape((rows, width), F32),
            shape((chunks * state, width), F32),
            shape((chunks, width), F32),
            shape((rows, 2 * state), F32),
            shape((2 * state, rows), F32),
            shape((state, width + LANES), BF16),
        ),
        in_specs=[SMEM] + [VMEM] * (8 + KVH),
        out_specs=(VMEM,) * 8,
        scratch_shapes=[
            pltpu.VMEM((rows, width), BF16),
            pltpu.VMEM((rows, width), F32),
            pltpu.VMEM((rows, width), BF16),
        ],
        compiler_params=params(20),
        cost_estimate=cost(10 * rows * width * 256, 30 * rows * width, 3 * rows * width),
        name="prepare",
    )(
        place,
        tokens,
        gains,
        skip_gain,
        dt_first,
        dt_second,
        dt_bias,
        decay_rate,
        w_bct,
        *attended,
    )
    beside_ends = exchange(ends, "ctx", 1)
    coef = pl.pallas_call(
        couple_kernel,
        out_shape=shape((rows, rows), F32),
        in_specs=[VMEM, VMEM],
        out_specs=VMEM,
        compiler_params=params(4),
        cost_estimate=cost(20 * rows * rows, 20 * rows * rows),
        name="couple",
    )(bc, bct)
    chip_ends = pl.pallas_call(
        pair_kernel,
        out_shape=shape(ends.shape, BF16),
        in_specs=[SMEM, ANY, VMEM, VMEM],
        out_specs=VMEM,
        compiler_params=params(8),
        cost_estimate=cost(4 * ends.size, 8 * ends.size),
        name="pair",
    )(place, coef, ends, beside_ends)
    earlier_ends = [exchange(chip_ends, "ctx", mask) for mask in range(2, shard_count, 2)]
    before, faded = pl.pallas_call(
        within_kernel,
        out_shape=(shape((rows, width), F32), shape((rows, width), F32)),
        in_specs=[VMEM] * 4,
        out_specs=(VMEM, VMEM),
        compiler_params=params(12),
        cost_estimate=cost(40 * rows * width, 20 * rows * width),
        name="within",
    )(coef, base, keep, drive)
    second, weighting, *packed = pl.pallas_call(
        route_kernel,
        out_shape=(shape((rows, width), F32), shape((rows, EXPERTS * capacity), F32))
        + (shape((capacity, width), BF16),) * EXPERTS,
        in_specs=[SMEM] + [VMEM] * (9 + len(earlier_ends)),
        out_specs=(VMEM,) * (2 + EXPERTS),
        scratch_shapes=[
            pltpu.VMEM((chunks * state, width), BF16),
            pltpu.VMEM((rows, width), F32),
            pltpu.VMEM((rows, width), BF16),
            pltpu.VMEM((shard_count // 2, state, width + LANES), BF16),
        ],
        compiler_params=params(16),
        cost_estimate=cost(10 * rows * width * 256, 30 * rows * width),
        name="route",
    )(
        place,
        before,
        faded,
        chunk_state,
        chunk_keep,
        bc,
        gains,
        router_t,
        routes_t,
        beside_ends,
        *earlier_ends,
    )

    units = raising.shape[1]

    def lift(blocks, after):
        count = sum(block.shape[0] for block in blocks)
        return pl.pallas_call(
            up_kernel,
            out_shape=shape((count, units), BF16),
            in_specs=[VMEM, ANY] + [VMEM] * len(blocks),
            out_specs=VMEM,
            compiler_params=params(12),
            cost_estimate=cost(2 * count * width * units, 2 * width * units),
            name="up",
        )(raising, after, *blocks)

    def lower(weights, hidden, after, outs=1, hurry=False):
        count, span = hidden.shape[0], half * len(weights)
        work = 1 if hurry else units
        return pl.pallas_call(
            functools.partial(down_kernel, len(weights)),
            out_shape=(shape((count // outs, span), BF16),) * outs,
            in_specs=[VMEM, ANY] + [VMEM] * len(weights),
            out_specs=(VMEM,) * outs,
            compiler_params=params(12),
            cost_estimate=cost(2 * count * span * work, 2 * span * work),
            name="down",
        )(hidden, after, *weights)

    def between_experts(blocks):
        moved = {slot: exchange(blocks[slot - 1], "ctx", slot * parts) for slot in (3, 1, 2)}
        return [moved[slot] for slot in range(1, EXPERTS)]

    moved = between_experts(packed[1:])
    stay = [exchange(packed[0], "ctx", turn) if turn else packed[0] for turn in range(parts)]
    stay_hidden = lift(stay, packed[0])
    lowering += fetch([(w_down[0], 16, half, half)], stay_hidden, hurry=True)
    stay_out = lower(lowering, stay_hidden, packed[0], parts)
    stay_sums = [stay_out[0]] + [
        exchange(stay_out[turn], "ctx", turn) for turn in range(1, parts)
    ]
    moved_rows = (EXPERTS - 1) * capacity
    arrived = pl.pallas_call(
        functools.partial(gather_kernel, SENT),
        out_shape=shape((moved_rows, width), BF16),
        in_specs=[ANY] + [VMEM] * (EXPERTS - 1),
        out_specs=VMEM,
        compiler_params=params(4),
        cost_estimate=cost(0, 4 * moved_rows * width),
        name="gather",
    )(stay_sums[-1], *[moved[slot - 1] for slot in SENT])
    hiddens = []
    after = arrived
    for turn in range(parts):
        after = lift([exchange(arrived, "ctx", turn) if turn else arrived], after)
        hiddens.append(after)
    others = []
    for turn in range(1, parts):
        (after,) = lower(lowering, hiddens[turn], after)
        others.append(exchange(after, "ctx", turn))
    results = []
    for chunk in range(CHUNKS):
        (own,) = lower(lowering[chunk : chunk + 1], hiddens[0], after, hurry=chunk > 0)
        joined = pl.pallas_call(
            functools.partial(join_kernel, chunk * half),
            out_shape=(shape((capacity, half), BF16),) * (EXPERTS - 1),
            in_specs=[VMEM] * parts,
            out_specs=(VMEM,) * (EXPERTS - 1),
            compiler_params=params(8),
            cost_estimate=cost(4 * moved_rows * half, 8 * moved_rows * half),
            name="join",
        )(own, *others)
        after = joined[0]
        returned = between_experts(joined)
        finished = pl.pallas_call(
            functools.partial(finish_kernel, chunk * half, BACK[chunk]),
            out_shape=shape((rows, half), BF16),
            in_specs=[VMEM] * (1 + EXPERTS + parts),
            out_specs=VMEM,
            compiler_params=params(8),
            cost_estimate=cost(
                4 * rows * EXPERTS * capacity * half, 10 * rows * half
            ),
            name="finish",
        )(second, weighting, *[returned[slot - 1] for slot in BACK[chunk]], *stay_sums)
        results.append(shifted(finished, "segment", 1))
    return jnp.concatenate(results, 1)[None]


def solution(mesh):
    in_specs = (
        P("segment", "ctx", None),
        P("segment", None, None),
        P("segment", None, "ctx"),
        P("segment", None, None),
        P("segment", None, None),
        P("segment", None),
        P("segment", None),
        P("segment", None, None),
        P("segment", None),
        P("segment", None, None),
        P("segment", "ctx", None),
        P("segment", None, "ctx"),
        P("segment", "ctx", None),
    )
    out_specs = P("segment", "ctx", None)
    return jax.shard_map(
        on_device, mesh=mesh, in_specs=in_specs, out_specs=out_specs, check_vma=False
    )
```
